32 devices in a mesh: dp: 8 (over z, core), fsdp: 4 (over y, x).
Axes of the slice: x: 2, y: 2, z: 4, core: 2. Of those that a mesh axis runs over, the one named last changes fastest.
Arguments:
- node_feat: bfloat16 [32768, 256], P(('dp', 'fsdp')), may hold values from -3 to 3
- out_cot: bfloat16 [32768, 256], P(('dp', 'fsdp')), may hold values from -3 to 3
- node_type: int32 [32768], P(('dp', 'fsdp')), may hold values from 0 to 3
- node_count: int32 [32], P(('dp', 'fsdp')), may hold values from 256 to 1024, as said below
- edge_src: int32 [256, 1024], P(('dp', 'fsdp')), may hold values from 0 to 1023, as said below
- edge_dst: int32 [256, 1024], P(('dp', 'fsdp')), may hold values from 0 to 1023, as said below
- edge_time: int32 [256, 1024], P(('dp', 'fsdp')), may hold values from 0 to 239
- edge_count: int32 [256], P(('dp', 'fsdp')), may hold values from 128 to 1024, as said below
- type_weight: float32 [1024, 1024], P('fsdp'), may hold values from -0.26516504 to 0.26516504
- type_first: float32 [1024, 1024], P('fsdp'), may hold values from -32 to 32
- type_second: float32 [1024, 1024], P('fsdp'), may hold values from 4.096 to 16.384
- type_avg: float32 [1024, 1024], P('fsdp'), may hold values from -0.26516504 to 0.26516504
- edge_weight: float32 [256, 768], P('fsdp'), may hold values from -0.26516504 to 0.26516504
- edge_first: float32 [256, 768], P('fsdp'), may hold values from -128 to 128
- edge_second: float32 [256, 768], P('fsdp'), may hold values from 45.8752 to 183.5008
- edge_avg: float32 [256, 768], P('fsdp'), may hold values from -0.26516504 to 0.26516504
- norm_params: float32 [8, 256], P(None, 'fsdp')
- norm_first: float32 [8, 256], P(None, 'fsdp'), may hold values from -48 to 48
- norm_second: float32 [8, 256], P(None, 'fsdp'), may hold values from 7.3728 to 29.4912
- norm_avg: float32 [8, 256], P(None, 'fsdp')
- mix_params: float32 [68], replicated, may hold values from 0.25 to 1.5
- mix_first: float32 [68], replicated, may hold values from -384 to 384
- mix_second: float32 [68], replicated, may hold values from 461.37344 to 1887.4368
- mix_avg: float32 [68], replicated, may hold values from 0.25 to 1.5
Outputs:
- layer_out: bfloat16 [32768, 256], P(('dp', 'fsdp'))
- input_grad: bfloat16 [32768, 256], P(('dp', 'fsdp'))
- new_type_weight: float32 [1024, 1024], P('fsdp')
- new_type_first: float32 [1024, 1024], P('fsdp')
- new_type_second: float32 [1024, 1024], P('fsdp')
- new_type_avg: float32 [1024, 1024], P('fsdp')
- new_edge_weight: float32 [256, 768], P('fsdp')
- new_edge_first: float32 [256, 768], P('fsdp')
- new_edge_second: float32 [256, 768], P('fsdp')
- new_edge_avg: float32 [256, 768], P('fsdp')
- new_norm_params: float32 [8, 256], P(None, 'fsdp')
- new_norm_first: float32 [8, 256], P(None, 'fsdp')
- new_norm_second: float32 [8, 256], P(None, 'fsdp')
- new_norm_avg: float32 [8, 256], P(None, 'fsdp')
- new_mix_params: float32 [68], replicated
- new_mix_first: float32 [68], replicated
- new_mix_second: float32 [68], replicated
- new_mix_avg: float32 [68], replicated
The draws below stay inside these ranges and needn't reach their ends.
Inputs may be any that keep to these rules, and one draw needn't show every extreme that they name: `node_count`: each subgraph holds at least 256 live nodes in its first slots, and in every draw one subgraph fills all 1024 slots. `edge_count`: the first that many slots of a relation's row are counted; every live node is the target and the source of some counted edge; in every draw one row is full. `edge_src`: every entry is a live node of its own subgraph. `edge_dst`: every entry is a live node of its own subgraph.
All inputs are finite; a program needn't handle non-finite values.
Results may differ from the reference program's by a relative error of at most 0.012.
The reference program's roundings to bfloat16 on the way count: a program that leaves them out, or rounds other values in their place, can miss the bound.
Values may be sent and summed in bfloat16 or wider, within the bound.
No kernel may reach another device: no remote copies, remote signals or barrier semaphores. Data moves between devices by JAX's collectives and lax.ppermute only.
A program may use at most 256 MiB of HBM per device.

```python
import math
import jax
import jax.numpy as jnp
import numpy as np
from jax import lax

D = 256
H = 8
DK = 32
TYPES = 4
REL = 8
TB = 240
NODE_DEV = 1024
EDGE_REL = 1024
STEP = 10
BLOCKS = 32
NODES = 32768


def graph_layout(key):
    key_list = jax.random.split(key, 5)
    block_ids = jnp.arange(BLOCKS, dtype=jnp.int32)
    relation_ids = jnp.arange(REL, dtype=jnp.int32)
    slot_ids = jnp.arange(EDGE_REL, dtype=jnp.int32)
    node_ids = jnp.arange(NODE_DEV, dtype=jnp.int32)
    live_nodes = jax.random.randint(key_list[0], (BLOCKS,), NODE_DEV // 4, NODE_DEV + 1)
    full_block = jax.random.randint(key_list[1], (), 0, BLOCKS)
    live_nodes = jnp.where(block_ids == full_block, NODE_DEV, live_nodes)
    low_edges = jnp.maximum(EDGE_REL * live_nodes // (2 * NODE_DEV), live_nodes // REL + 1)
    high_edges = EDGE_REL * live_nodes // NODE_DEV + 1
    raw_counts = jax.random.randint(key_list[2], (BLOCKS, REL), 0, 1 << 20)
    counts = low_edges[:, None] + raw_counts % (high_edges - low_edges)[:, None]
    counts = jnp.where((block_ids[:, None] == full_block) & (relation_ids[None, :] == 0), EDGE_REL, counts)
    spread_limit = (1 << 30) // NODE_DEV
    noise = jax.random.randint(key_list[3], (BLOCKS, NODE_DEV), 0, spread_limit)
    order_key = noise * NODE_DEV + node_ids[None, :]
    order_key = jnp.where(node_ids[None, :] < live_nodes[:, None], order_key, (1 << 30) + node_ids[None, :])
    order = jnp.argsort(order_key, axis=1).astype(jnp.int32)
    per_relation = (live_nodes + REL - 1) // REL
    cover = slot_ids[None, None, :] < per_relation[:, None, None]
    global_slot = relation_ids[None, :, None] * per_relation[:, None, None] + slot_ids[None, None, :]
    dst_pos = (global_slot % live_nodes[:, None, None]).reshape(BLOCKS, REL * EDGE_REL)
    src_pos = ((global_slot + 1) % live_nodes[:, None, None]).reshape(BLOCKS, REL * EDGE_REL)
    dst_cover = jnp.take_along_axis(order, dst_pos, axis=1).reshape(BLOCKS, REL, EDGE_REL)
    src_cover = jnp.take_along_axis(order, src_pos, axis=1).reshape(BLOCKS, REL, EDGE_REL)
    pair_keys = jax.random.split(key_list[4], 2)
    dst_rand = jax.random.randint(pair_keys[0], (BLOCKS, REL, EDGE_REL), 0, live_nodes[:, None, None])
    src_rand = jax.random.randint(pair_keys[1], (BLOCKS, REL, EDGE_REL), 0, live_nodes[:, None, None])
    targets = jnp.where(cover, dst_cover, dst_rand).reshape(BLOCKS * REL, EDGE_REL)
    sources = jnp.where(cover, src_cover, src_rand).reshape(BLOCKS * REL, EDGE_REL)
    return (live_nodes.astype(jnp.int32), counts.reshape(BLOCKS * REL).astype(jnp.int32), sources.astype(jnp.int32), targets.astype(jnp.int32))


def draw_node_count(key, part):
    return graph_layout(key)[0]


def draw_edge_count(key, part):
    return graph_layout(key)[1]


def draw_edge_src(key, part):
    return graph_layout(key)[2]


def draw_edge_dst(key, part):
    return graph_layout(key)[3]


def norm_table(key):
    key_gain, key_bias = jax.random.split(key)
    gains = jax.random.uniform(key_gain, (TYPES, D), jnp.float32, 0.6, 1.6)
    biases = 0.3 * jax.random.normal(key_bias, (TYPES, D), jnp.float32)
    return jnp.concatenate([gains, biases], axis=0)


def draw_norm_params(key, part):
    key = jax.random.fold_in(key, 11)
    return norm_table(key)


def draw_norm_avg(key, part):
    key = jax.random.fold_in(key, 12)
    return norm_table(key)


def clipped_normal(key, shape, deviation):
    return deviation * jnp.clip(jax.random.normal(key, shape, jnp.float32), -3.0, 3.0)


def draw_node_feat(key, part):
    key = jax.random.fold_in(key, 21)
    return clipped_normal(key, (NODES, D), 1.0).astype(jnp.bfloat16)


def draw_out_cot(key, part):
    key = jax.random.fold_in(key, 22)
    return clipped_normal(key, (NODES, D), 1.0).astype(jnp.bfloat16)


def draw_type_weight(key, part):
    key = jax.random.fold_in(key, 23)
    return clipped_normal(key, (TYPES * D, 4 * D), (2.0 / D) ** 0.5)


def draw_type_avg(key, part):
    key = jax.random.fold_in(key, 24)
    return clipped_normal(key, (TYPES * D, 4 * D), (2.0 / D) ** 0.5)


def draw_edge_weight(key, part):
    key = jax.random.fold_in(key, 25)
    return clipped_normal(key, (D, 2 * REL * DK + D), (2.0 / D) ** 0.5)


def draw_edge_avg(key, part):
    key = jax.random.fold_in(key, 26)
    return clipped_normal(key, (D, 2 * REL * DK + D), (2.0 / D) ** 0.5)


def touch_ends(array, rng, low, largest):
    longest = array.shape.index(max(array.shape))
    spots = []
    for shift in (0, 1):
        where = [jax.random.randint(jax.random.fold_in(rng, axis), (), 0, length) for axis, length in enumerate(array.shape)]
        where[longest] = (where[longest] + shift) % array.shape[longest]
        spots.append(tuple(where))
    return array.at[spots[0]].set(low).at[spots[1]].set(largest)


def steps_of(key, shape, cuts, low, largest):
    level, own = 1.0, jax.random.fold_in(key, 6)
    for dim, shards_of in cuts:
        draws = jnp.exp(jax.random.uniform(jax.random.fold_in(own, dim), (shards_of,), jnp.float32, low / len(cuts), largest / len(cuts)))
        level = level * jnp.repeat(draws, shape[dim] // shards_of).reshape([-1 if axis == dim else 1 for axis in range(len(shape))])
    return level


def rank_table(amount, skew):
    loads = [(1 << 20) // math.isqrt(standing ** skew) + 1 for standing in range(1, amount + 1)]
    scale = 1 + sum(loads) // (1 << 30)
    return np.cumsum(np.array([max(1, weight // scale) for weight in loads]))


def ranked(key, dims, count, slope):
    table = rank_table(count, slope)
    pick = jax.random.randint(jax.random.fold_in(key, 1), dims, 0, int(table[count - 1]))
    grade = jnp.searchsorted(jnp.asarray(table, jnp.int32), pick, side="right")
    return jax.random.permutation(jax.random.fold_in(key, 2), count)[grade].astype(jnp.int32)


def gaussian(own_key, shape, scale, most, cuts=(), kind=jnp.bfloat16):
    drawn = jax.random.normal(own_key, shape, jnp.float32) * scale
    if len(cuts) > 0:
        drawn = steps_of(own_key, shape, cuts, -0.22, 0.18) * drawn
    return jnp.clip(drawn, min=-most, max=most).astype(kind)


def setup_inputs(seed: int = 0) -> dict:
    splits = jax.random.split(jax.random.key(seed), 25)
    return {
        "node_feat": draw_node_feat(jax.random.fold_in(splits[24], 71), 0),
        "out_cot": draw_out_cot(jax.random.fold_in(splits[24], 71), 0),
        "node_type": touch_ends(ranked(splits[2], (NODES,), TYPES, 2), jax.random.fold_in(splits[2], 3), 0, TYPES - 1).astype(jnp.int32),
        "node_count": draw_node_count(jax.random.fold_in(splits[24], 71), 0),
        "edge_src": draw_edge_src(jax.random.fold_in(splits[24], 71), 0),
        "edge_dst": draw_edge_dst(jax.random.fold_in(splits[24], 71), 0),
        "edge_time": touch_ends(jax.random.randint(splits[6], (BLOCKS * REL, EDGE_REL), 0, TB), jax.random.fold_in(splits[6], 1), 0, TB - 1).astype(jnp.int32),
        "edge_count": draw_edge_count(jax.random.fold_in(splits[24], 71), 0),
        "type_weight": draw_type_weight(jax.random.fold_in(splits[24], 71), 0),
        "type_first": gaussian(splits[9], (TYPES * D, 4 * D), (0.067 * (NODES // TYPES) ** 0.5), 32.0, ((0, 4),), jnp.float32),
        "type_second": jnp.clip(jnp.exp(math.log(16.384) - 1.3862944 * jax.random.uniform(splits[10], (TYPES * D, 4 * D), jnp.float32) ** steps_of(splits[10], (TYPES * D, 4 * D), ((0, 4),), -0.2, 0.2)), 4.096, 16.384),
        "type_avg": draw_type_avg(jax.random.fold_in(splits[24], 71), 0),
        "edge_weight": draw_edge_weight(jax.random.fold_in(splits[24], 71), 0),
        "edge_first": gaussian(splits[13], (D, 2 * REL * DK + D), (0.11 * (EDGE_REL * BLOCKS) ** 0.5), 128.0, ((0, 4),), jnp.float32),
        "edge_second": jnp.clip(jnp.exp(math.log(183.5008) - 1.3862944 * jax.random.uniform(splits[14], (D, 2 * REL * DK + D), jnp.float32) ** steps_of(splits[14], (D, 2 * REL * DK + D), ((0, 4),), -0.2, 0.2)), 45.8752, 183.5008),
        "edge_avg": draw_edge_avg(jax.random.fold_in(splits[24], 71), 0),
        "norm_params": draw_norm_params(jax.random.fold_in(splits[24], 71), 0),
        "norm_first": gaussian(splits[17], (2 * TYPES, D), (0.089 * (NODES // TYPES) ** 0.5), 48.0, ((1, 4),), jnp.float32),
        "norm_second": jnp.clip(jnp.exp(math.log(29.4912) - 1.3862944 * jax.random.uniform(splits[18], (2 * TYPES, D), jnp.float32) ** steps_of(splits[18], (2 * TYPES, D), ((1, 4),), -0.2, 0.2)), 7.3728, 29.4912),
        "norm_avg": draw_norm_avg(jax.random.fold_in(splits[24], 71), 0),
        "mix_params": jnp.clip(jax.random.uniform(splits[20], (REL * H + TYPES,), jnp.float32, 0.25, 1.5), 0.25, 1.5),
        "mix_first": gaussian(splits[21], (REL * H + TYPES,), (0.044 * (D * NODES // TYPES) ** 0.5), 384.0, (), jnp.float32),
        "mix_second": jnp.clip(jnp.exp(jax.random.uniform(splits[22], (REL * H + TYPES,), jnp.float32, math.log(461.37344), math.log(1887.4368))), 461.37344, 1887.4368),
        "mix_avg": jnp.clip(jax.random.uniform(splits[23], (REL * H + TYPES,), jnp.float32, 0.25, 1.5), 0.25, 1.5),
    }


@jax.custom_vjp
def low(v):
    return lax.optimization_barrier(v.astype(jnp.bfloat16)).astype(jnp.float32)

@jax.custom_vjp
def low_back(v):
    return v

def low_keep(v):
    return (low(v), None)

def low_pass(kept, grad):
    return (grad,)

def back_keep(v):
    return (v, None)

def back_low(kept, grad):
    return (low(grad),)
low.defvjp(low_keep, low_pass)
low_back.defvjp(back_keep, back_low)
beta_one = 0.9
beta_two = 0.999
adam_eps = 1e-08
decay_rate = 0.01
ema_keep = 0.7
norm_eps = 1e-05
rate_type = 0.2
rate_edge = 0.2
rate_norm = 0.6
rate_mix = 0.6

def time_table():
    steps = lax.broadcasted_iota(jnp.int32, (TB, D), 0).astype(jnp.float32)
    column = lax.broadcasted_iota(jnp.int32, (TB, D), 1)
    freq = jnp.exp(-jnp.log(10000.0) * (2 * (column // 2)).astype(jnp.float32) / D)
    angle = steps * freq
    return jnp.where(column % 2 == 0, jnp.sin(angle), jnp.cos(angle))

def matmul(left, right):
    return jnp.dot(left, right, precision=lax.Precision.HIGHEST, preferred_element_type=jnp.float32)

def exact_gelu(values):
    return jax.nn.gelu(values, approximate=False)

def device_block(weights, emb_low, feat, kinds, live_count, src_rows, dst_rows, time_rows, count_rows):
    type_w, edge_w, norm_w, mix_w = weights
    node_total = feat.shape[0]
    edge_slots = src_rows.shape[1]
    score_scale = DK ** (-0.5)
    onehot = (kinds[:, None] == jnp.arange(TYPES, dtype=jnp.int32)[None, :]).astype(jnp.float32)
    live_mask = (jnp.arange(node_total, dtype=jnp.int32) < live_count[0]).astype(jnp.float32)
    typed_feat = (onehot[:, :, None] * feat[:, None, :]).reshape(node_total, TYPES * D)
    qkv_node = low_back(matmul(typed_feat, type_w[:, :3 * D]))
    query_node = qkv_node[:, :D]
    keyval = qkv_node[:, D:]
    rte_low = low(low_back(matmul(emb_low, edge_w[:, REL * 2 * DK:])))
    kv_types = type_w[:, D:3 * D].reshape(TYPES, D, 2 * D)
    time_kv = low_back(jnp.einsum('td,sde->ste', rte_low, kv_types, precision=lax.Precision.HIGHEST)).reshape(TYPES * TB, 2 * D)
    rel_blocks = edge_w[:, :REL * 2 * DK].reshape(H, DK, REL, 2, DK)
    rel_prior = mix_w[:REL * H].reshape(REL, H)
    skip_logit = mix_w[REL * H:]
    denom_sum = jnp.zeros((node_total, H), jnp.float32)
    numer_sum = jnp.zeros((node_total, D), jnp.float32)
    for relation in range(REL):
        source = src_rows[relation]
        target = dst_rows[relation]
        bucket = kinds[source] * TB + time_rows[relation]
        valid_edge = (jnp.arange(edge_slots, dtype=jnp.int32) < count_rows[relation]).astype(jnp.float32)
        kv_edge = low(keyval[source] + time_kv[bucket])
        key_edge = kv_edge[:, :D].reshape(edge_slots, H, DK)
        val_edge = kv_edge[:, D:].reshape(edge_slots, H, DK)
        key_att = low_back(jnp.einsum('ehi,hij->ehj', key_edge, rel_blocks[:, :, relation, 0, :], precision=lax.Precision.HIGHEST))
        message = low_back(jnp.einsum('ehi,hij->ehj', val_edge, rel_blocks[:, :, relation, 1, :], precision=lax.Precision.HIGHEST))
        q_target = query_node[target].reshape(edge_slots, H, DK)
        raw_score = lax.optimization_barrier(jnp.sum(key_att * q_target, axis=2))
        weight = valid_edge[:, None] * jnp.exp(raw_score * rel_prior[relation][None, :] * score_scale)
        denom_sum = denom_sum + jax.ops.segment_sum(weight, target, num_segments=node_total)
        numer_sum = numer_sum + jax.ops.segment_sum((weight[:, :, None] * message).reshape(edge_slots, D), target, num_segments=node_total)
    den_safe = denom_sum + 1.0 - live_mask[:, None]
    agg_node = numer_sum / jnp.repeat(den_safe, DK, axis=1)
    act_low = low(exact_gelu(agg_node))
    typed_act = (onehot[:, :, None] * act_low[:, None, :]).reshape(node_total, TYPES * D)
    trans_node = low_back(matmul(typed_act, type_w[:, 3 * D:]))
    alpha_node = jax.nn.sigmoid(lax.optimization_barrier(jnp.sum(onehot * skip_logit[None, :], axis=1)))[:, None]
    resid = alpha_node * trans_node + (1.0 - alpha_node) * feat
    mean_node = lax.optimization_barrier(jnp.mean(resid, axis=1, keepdims=True))
    centered = resid - mean_node
    var_node = lax.optimization_barrier(jnp.mean(centered * centered, axis=1, keepdims=True))
    normed = centered * lax.rsqrt(var_node + norm_eps)
    gain_node = matmul(onehot, norm_w[:TYPES])
    bias_node = matmul(onehot, norm_w[TYPES:])
    return live_mask[:, None] * (normed * gain_node + bias_node)

def adam_step(param, first, second, avg, grad, rate):
    first_new = beta_one * first + (1.0 - beta_one) * grad
    second_new = beta_two * second + (1.0 - beta_two) * grad * grad
    first_hat = first_new / (1.0 - beta_one ** STEP)
    second_hat = second_new / (1.0 - beta_two ** STEP)
    param_new = param - rate * (first_hat / (jnp.sqrt(second_hat) + adam_eps) + decay_rate * param)
    avg_new = ema_keep * avg + (1.0 - ema_keep) * param_new
    return (param_new, first_new, second_new, avg_new)

def reference(node_feat, out_cot, node_type, node_count, edge_src, edge_dst, edge_time, edge_count, type_weight, type_first, type_second, type_avg, edge_weight, edge_first, edge_second, edge_avg, norm_params, norm_first, norm_second, norm_avg, mix_params, mix_first, mix_second, mix_avg):
    feat_all = node_feat.astype(jnp.float32).reshape(BLOCKS, NODE_DEV, D)
    kinds = node_type.reshape(BLOCKS, NODE_DEV)
    live_counts = node_count.reshape(BLOCKS, 1)
    src_all = edge_src.reshape(BLOCKS, REL, EDGE_REL)
    dst_all = edge_dst.reshape(BLOCKS, REL, EDGE_REL)
    time_all = edge_time.reshape(BLOCKS, REL, EDGE_REL)
    count_all = edge_count.reshape(BLOCKS, REL)
    emb_table = time_table()
    block_fn = jax.checkpoint(device_block)

    def whole(params, feats):
        weights = tuple((low(param) for param in params))
        emb_low = low(emb_table)

        def one_block(items):
            return block_fn(weights, emb_low, *items)
        return lax.map(one_block, (feats, kinds, live_counts, src_all, dst_all, time_all, count_all))
    params = (type_weight, edge_weight, norm_params, mix_params)
    outputs, back_fn = jax.vjp(whole, params, feat_all)
    grads, feat_grad = back_fn(out_cot.astype(jnp.float32).reshape(BLOCKS, NODE_DEV, D))
    layer_out = outputs.reshape(NODES, D).astype(jnp.bfloat16)
    input_grad = feat_grad.reshape(NODES, D).astype(jnp.bfloat16)
    type_new = adam_step(type_weight, type_first, type_second, type_avg, grads[0], rate_type)
    edge_new = adam_step(edge_weight, edge_first, edge_second, edge_avg, grads[1], rate_edge)
    norm_new = adam_step(norm_params, norm_first, norm_second, norm_avg, grads[2], rate_norm)
    mix_new = adam_step(mix_params, mix_first, mix_second, mix_avg, grads[3], rate_mix)
    return (layer_out, input_grad, type_new[0], type_new[1], type_new[2], type_new[3], edge_new[0], edge_new[1], edge_new[2], edge_new[3], norm_new[0], norm_new[1], norm_new[2], norm_new[3], mix_new[0], mix_new[1], mix_new[2], mix_new[3])
```

```python
import functools

import jax
import jax.numpy as jnp
import numpy as np
from jax import lax
from jax.experimental import pallas as pl
from jax.experimental.pallas import tpu as pltpu
from jax.sharding import PartitionSpec as P

D, H, DK, TYPES, REL, TB = 256, 8, 32, 4, 8, 240
N = 1024
EC = 512
SUB = 256
NSUB = EC // SUB
NC = 256
bf16 = jnp.bfloat16
f32 = jnp.float32
norm_eps = 1e-5
STEP = 10
beta_one = 0.9
beta_two = 0.999
adam_eps = 1e-08
decay_rate = 0.01
ema_keep = 0.7
rates = (0.2, 0.2, 0.6, 0.6)


def nn(a, b):
    return jnp.dot(a, b, preferred_element_type=f32)


def nt(a, b):
    return lax.dot_general(a, b, (((1,), (1,)), ((), ())), preferred_element_type=f32)


def one_hot_rows(row, count):
    wide = row.shape[1]
    base = lax.broadcasted_iota(jnp.int32, (256, wide), 0).astype(bf16)
    one, zero = jnp.ones((), bf16), jnp.zeros((), bf16)
    return jnp.concatenate(
        [jnp.where(base == (row - 256 * g).astype(bf16), one, zero) for g in range(count // 256)], axis=0
    )


def head_sum(x):
    return jnp.sum(x.reshape(H, DK, x.shape[1]), axis=1)


def head_wide(x):
    return jnp.broadcast_to(x[:, None, :], (H, DK, x.shape[1])).reshape(D, x.shape[1])


def hi_lo(x):
    high = x.astype(bf16).astype(f32)
    return jnp.concatenate([high, x - high], axis=0).astype(bf16)


def eye():
    return (
        lax.broadcasted_iota(jnp.int32, (256, 256), 0) == lax.broadcasted_iota(jnp.int32, (256, 256), 1)
    ).astype(f32).astype(bf16)


def pick(masks, wide):
    out = wide[0] * masks[0:1]
    for s in range(1, TYPES):
        out = jnp.where(masks[s:s + 1] > 0, wide[s], out)
    return out


def kernel(
    blocks,
    place_ref, live_ref, cnt_ref, skip_ref,
    kinds_ref, kinds8_ref, src_ref, dst_ref, tim_ref,
    feat_ref, cot_ref, mu_ref, emb_ref, own_ref, *rest,
):
    near_refs, far_refs, rest = rest[:blocks - 1], rest[blocks - 1:2 * blocks - 2], rest[2 * blocks - 2:]
    (
        out_ref, ig_ref, keep_ref, send_ref,
        lst_r, lst_o, lst_c,
        wpk, gpack, gout, gnorm_acc, gskip_acc,
        bkt, wt, xcat, kvt, tkvt, qt, rte,
        bda, bdat, bdm, bdmt, ga, gm, dmu,
        kve, qe, katt, msg, wexp, raws,
        num, dnum, dq, dkv, dtkv, skp,
    ) = rest
    trows, erows = TYPES * D // blocks, D // blocks
    part = trows + erows
    half = part // 2
    me, core = place_ref[0], place_ref[1]

    wpk[pl.ds(pl.multiple_of(me * part, 16), part), :] = own_ref[...]
    for m in range(1, blocks):
        base = jnp.bitwise_xor(me, m) * part
        wpk[pl.ds(pl.multiple_of(base + core * half, 16), half), :] = near_refs[m - 1][...]
        wpk[pl.ds(pl.multiple_of(base + (1 - core) * half, 16), half), :] = far_refs[m - 1][...]

    def rows_at(pieces):
        return pieces[0] if len(pieces) == 1 else jnp.concatenate(pieces, axis=0)

    def type_part(s, c0, c1):
        lo, hi = s * D // trows, max((s + 1) * D // trows, s * D // trows + 1)
        return rows_at([
            wpk[f * part + max(s * D - f * trows, 0):f * part + min((s + 1) * D - f * trows, trows), c0:c1]
            for f in range(lo, hi)
        ])

    def edge_part(c0, c1):
        return rows_at([wpk[f * part + trows:(f + 1) * part, c0:c1] for f in range(blocks)])

    def norm_part():
        wide = D // blocks
        full = jnp.concatenate(
            [wpk[f * part + trows:f * part + trows + 16, 768:768 + wide].astype(f32) for f in range(blocks)], axis=1
        )
        return full.astype(bf16)

    def put_type(s, value):
        lo, hi = s * D // trows, max((s + 1) * D // trows, s * D // trows + 1)
        for f in range(lo, hi):
            a, b = max(s * D, f * trows), min((s + 1) * D, (f + 1) * trows)
            gpack[f * part + a - f * trows:f * part + b - f * trows, :] = value[a - s * D:b - s * D].astype(bf16)

    def put_edge(c0, value):
        for f in range(blocks):
            gpack[f * part + trows:(f + 1) * part, c0:c0 + value.shape[1]] = value[f * erows:(f + 1) * erows].astype(bf16)

    ident = eye()
    def per_rel(r, k):
        c = cnt_ref[r]
        def one(j, k):
            lst_r[k] = r
            lst_o[k] = j
            lst_c[k] = c - j * SUB
            return k + 1
        return lax.fori_loop(0, (c + SUB - 1) // SUB, one, k)
    total = lax.fori_loop(0, REL, per_rel, 0)
    for extra in range(NSUB - 1):
        lst_r[total + extra] = 0
        lst_o[total + extra] = 0
        lst_c[total + extra] = 0
    chunks = (total + NSUB - 1) // NSUB

    src = src_ref[...]
    for j in range(N // 128):
        idx = src[:, j * 128:(j + 1) * 128]
        low = jnp.bitwise_and(idx, 127)
        high = jnp.right_shift(idx, 7)
        acc = jnp.zeros((8, 128), jnp.int32)
        for k in range(N // 128):
            row = jnp.broadcast_to(kinds8_ref[k:k + 1, :], (8, 128))
            acc = jnp.where(high == k, jnp.take_along_axis(row, low, axis=1), acc)
        bkt[:, j * 128:(j + 1) * 128] = acc * 256 + tim_ref[:, j * 128:(j + 1) * 128]

    lane = lax.broadcasted_iota(jnp.int32, (D, 128), 1)
    rowi = lax.broadcasted_iota(jnp.int32, (D, 128), 0)
    on_diag = (lane // DK) == (rowi // DK) % 4
    for p in range(4):
        x = edge_part(p * 128, (p + 1) * 128).astype(f32)
        rolled = [x if k == 0 else pltpu.roll(x, 32 * k, 1) for k in range(4)]
        for g in range(4):
            r, m = 2 * p + g // 2, g % 2
            t = jnp.concatenate([rolled[(h % 4 - g) % 4][h * 32:(h + 1) * 32] for h in range(H)], axis=0)
            t = jnp.where(on_diag, t, 0.0)
            z = jnp.zeros((128, 128), f32)
            full = jnp.concatenate(
                [jnp.concatenate([t[:128], z], axis=1), jnp.concatenate([z, t[128:]], axis=1)], axis=0
            ).astype(bf16)
            (bdm if m else bda)[r] = full
            (bdmt if m else bdat)[r] = nt(ident, full).astype(bf16)

    for cb in range(4):
        for s in range(4):
            wt[cb * 256:(cb + 1) * 256, s * 256:(s + 1) * 256] = nt(
                ident, type_part(s, cb * 256, (cb + 1) * 256)
            ).astype(bf16)
    kinds = kinds_ref[...]
    masks = (lax.broadcasted_iota(jnp.int32, (8, N), 0) == kinds).astype(f32)
    featt = nt(ident, feat_ref[...])
    for s in range(TYPES):
        xcat[s * D:(s + 1) * D, :] = (featt * masks[s:s + 1]).astype(bf16)
    qt[...] = nn(wt[:D, :], xcat[...]).astype(bf16)
    kvt[...] = nn(wt[D:3 * D, :], xcat[...]).astype(bf16)
    wet = nt(ident, edge_part(512, 768)).astype(bf16)
    rte[...] = nt(wet, emb_ref[...]).astype(bf16)
    for s in range(TYPES):
        tkvt[:, s * 256:(s + 1) * 256] = nn(wt[D:3 * D, s * 256:(s + 1) * 256], rte[...]).astype(bf16)

    num[...] = jnp.zeros_like(num)
    dq[...] = jnp.zeros_like(dq)
    dkv[...] = jnp.zeros_like(dkv)
    dtkv[...] = jnp.zeros_like(dtkv)
    ga[...] = jnp.zeros_like(ga)
    gm[...] = jnp.zeros_like(gm)
    dmu[...] = jnp.zeros_like(dmu)

    def rows_of(ref, c):
        return jnp.concatenate(
            [ref[pl.ds(lst_r[c * NSUB + k], 1), pl.ds(pl.multiple_of(lst_o[c * NSUB + k] * SUB, SUB), SUB)] for k in range(NSUB)],
            axis=1,
        )

    def mu_of(c):
        return jnp.concatenate([mu_ref[lst_r[c * NSUB + k // 2]] for k in range(2 * NSUB)], axis=1)

    def forward(c, _):
        at = pl.ds(pl.multiple_of(c * EC, EC), EC)
        ohs = one_hot_rows(rows_of(src_ref, c), N)
        ohb = one_hot_rows(rows_of(bkt, c), N)
        ohd = one_hot_rows(rows_of(dst_ref, c), N)
        kv_e = (nn(kvt[...], ohs) + nn(tkvt[...], ohb)).astype(bf16)
        kve[:, at] = kv_e
        q_e = nn(qt[...], ohd)
        qe[:, at] = q_e.astype(bf16)
        ks, ms = [], []
        for k in range(NSUB):
            r = lst_r[c * NSUB + k]
            ks.append(nn(bdat[r], kv_e[:D, k * SUB:(k + 1) * SUB]))
            ms.append(nn(bdmt[r], kv_e[D:, k * SUB:(k + 1) * SUB]))
        ka = jnp.concatenate(ks, axis=1)
        me = jnp.concatenate(ms, axis=1)
        katt[:, at] = ka.astype(bf16)
        msg[:, at] = me.astype(bf16)
        raw = head_sum(ka * q_e)
        raws[:, at] = raw
        lanes = lax.broadcasted_iota(jnp.int32, (H, SUB), 1)
        valid = jnp.concatenate([lanes < lst_c[c * NSUB + k] for k in range(NSUB)], axis=1)
        w = jnp.where(valid, jnp.exp(raw * mu_of(c)), 0.0)
        wexp[:, at] = w
        wm = (head_wide(w) * me).astype(bf16)
        num[...] += nt(jnp.concatenate([wm, hi_lo(w)], axis=0), ohd)
        return 0

    lax.fori_loop(0, chunks, forward, 0)

    nwt = nt(ident, norm_part())
    gnorm_acc[...] = jnp.zeros_like(gnorm_acc)
    gskip_acc[...] = jnp.zeros_like(gskip_acc)
    gout[...] = jnp.zeros((TYPES * D, D), f32)

    def nodes(c, _):
        at = pl.ds(pl.multiple_of(c * NC, NC), NC)
        mk = (lax.broadcasted_iota(jnp.int32, (8, NC), 0) == kinds_ref[:, at]).astype(f32)
        live = (lax.broadcasted_iota(jnp.int32, (1, NC), 1) + c * NC < live_ref[0]).astype(f32)
        den = num[D:D + H, at] + num[D + H:, at] + (1.0 - live)
        denw = head_wide(den)
        agg = num[:D, at] / denw
        phi = 0.5 * (1.0 + lax.erf(agg * (0.5 ** 0.5)))
        act = (agg * phi).astype(bf16).astype(f32)
        acat = jnp.concatenate([(act * mk[s:s + 1]).astype(bf16) for s in range(TYPES)], axis=0)
        trans = nn(wt[3 * D:, :], acat)
        skip = jnp.zeros((1, NC), f32)
        for s in range(TYPES):
            skip = skip + mk[s:s + 1] * skip_ref[s]
        alpha = 1.0 / (1.0 + jnp.exp(-skip))
        ft = nt(ident, feat_ref[at, :])
        res = alpha * trans + (1.0 - alpha) * ft
        mean = jnp.mean(res, axis=0, keepdims=True)
        cen = res - mean
        inv = lax.rsqrt(jnp.mean(cen * cen, axis=0, keepdims=True) + norm_eps)
        nrm = cen * inv
        gain = nwt[:, 0:1] * mk[0:1]
        bias = nwt[:, 4:5] * mk[0:1]
        for s in range(1, TYPES):
            gain = gain + nwt[:, s:s + 1] * mk[s:s + 1]
            bias = bias + nwt[:, 4 + s:5 + s] * mk[s:s + 1]
        out_ref[at, :] = (live * (nrm * gain + bias)).T.astype(bf16)
        dy = live * nt(ident, cot_ref[at, :])
        oh16 = jnp.concatenate([mk, jnp.zeros((8, NC), f32)], axis=0).astype(bf16)
        dyn = dy * nrm
        dyn_hi = dyn.astype(bf16)
        dyn_lo = (dyn - dyn_hi.astype(f32)).astype(bf16)
        gnorm_acc[0:4, :] += (nt(oh16, dyn_hi) + nt(oh16, dyn_lo))[0:4]
        gnorm_acc[4:8, :] += nt(oh16, dy.astype(bf16))[0:4]
        dn = dy * gain
        dres = inv * (dn - jnp.mean(dn, axis=0, keepdims=True) - nrm * jnp.mean(dn * nrm, axis=0, keepdims=True))
        dtr = (alpha * dres).astype(bf16)
        skp[:, at] = (1.0 - alpha) * dres
        dal = jnp.sum(dres * (trans - ft), axis=0, keepdims=True) * alpha * (1.0 - alpha)
        gskip_acc[...] += jnp.broadcast_to(jnp.sum(mk * dal, axis=1, keepdims=True), (8, 128))
        gout[...] += nt(acat, dtr)
        dact = pick(mk, [nn(type_part(s, 3 * D, 4 * D), dtr) for s in range(TYPES)])
        dagg = dact * (phi + agg * (jnp.exp(-0.5 * agg * agg) * (0.5 / np.pi) ** 0.5))
        dnum[0:D, at] = (dagg / denw).astype(bf16)
        dnum[D:, at] = hi_lo(-head_sum(dagg * agg) / den)
        return 0

    lax.fori_loop(0, N // NC, nodes, 0)

    def backward(c, _):
        at = pl.ds(pl.multiple_of(c * EC, EC), EC)
        ohs = one_hot_rows(rows_of(src_ref, c), N)
        ohb = one_hot_rows(rows_of(bkt, c), N)
        ohd = one_hot_rows(rows_of(dst_ref, c), N)
        dn_all = nn(dnum[...], ohd)
        dn_e = dn_all[:D]
        w = wexp[:, at]
        dw = head_sum(dn_e * msg[:, at].astype(f32)) + dn_all[D:D + H] + dn_all[D + H:]
        ds = dw * w
        dsr = ds * raws[:, at]
        ss = head_wide(ds * mu_of(c))
        dka = (ss * qe[:, at].astype(f32)).astype(bf16)
        dms = (head_wide(w) * dn_e).astype(bf16)
        dq[...] += nt((ss * katt[:, at].astype(f32)).astype(bf16), ohd)
        ds_, = ([],)
        for k in range(NSUB):
            r = lst_r[c * NSUB + k]
            sl = slice(k * SUB, (k + 1) * SUB)
            ds_.append(jnp.concatenate([nn(bda[r], dka[:, sl]), nn(bdm[r], dms[:, sl])], axis=0).astype(bf16))
            at_k = pl.ds(pl.multiple_of(c * EC + k * SUB, SUB), SUB)
            gak = nt(kve[0:D, at_k], dka[:, sl])
            gmk = nt(kve[D:, at_k], dms[:, sl])
            ga[r, 0:128] += gak[0:128, 0:128]
            ga[r, 128:] += gak[128:, 128:]
            gm[r, 0:128] += gmk[0:128, 0:128]
            gm[r, 128:] += gmk[128:, 128:]
            dmu[r] += dsr[:, k * SUB:k * SUB + 128] + dsr[:, k * SUB + 128:(k + 1) * SUB]
        dkve = jnp.concatenate(ds_, axis=1)
        dkv[...] += nt(dkve, ohs)
        dtkv[...] += nt(dkve, ohb)
        return 0

    lax.fori_loop(0, chunks, backward, 0)

    dqkv = jnp.concatenate([dq[...].astype(bf16), dkv[...].astype(bf16)], axis=0)
    dt = dtkv[...].astype(bf16)
    for s in range(TYPES):
        g = nt(xcat[s * D:(s + 1) * D, :], dqkv)
        g_kv = g[:, D:] + nt(rte[...], dt[:, s * 256:(s + 1) * 256])
        put_type(s, jnp.concatenate([g[:, :D], g_kv, gout[s * D:(s + 1) * D, :]], axis=1))
    drte = nn(type_part(0, D, 3 * D), dt[:, 0:256])
    for s in range(1, TYPES):
        drte = drte + nn(type_part(s, D, 3 * D), dt[:, s * 256:(s + 1) * 256])
    embt = nt(ident, emb_ref[...]).astype(bf16)
    put_edge(512, nt(embt, drte.astype(bf16)))
    for c in range(N // NC):
        at = slice(c * NC, (c + 1) * NC)
        proj = pick(masks[:, at], [nn(type_part(s, 0, 3 * D), dqkv[:, at]) for s in range(TYPES)])
        ig_ref[at, :] = (proj + skp[:, at]).T.astype(bf16)
    for p in range(4):
        acc = jnp.zeros((D, 128), f32)
        for g in range(4):
            r, m = 2 * p + g // 2, g % 2
            t = jnp.where(on_diag, (gm if m else ga)[r], 0.0)
            rolled = [t if k == 0 else pltpu.roll(t, 32 * k, 1) for k in range(4)]
            acc = acc + jnp.concatenate([rolled[(g - h % 4) % 4][h * 32:(h + 1) * 32] for h in range(H)], axis=0)
        put_edge(p * 128, acc)
    gmu = jnp.sum(dmu[...], axis=2) * DK ** (-0.5)
    gnorm = gnorm_acc[...]
    wide = D // blocks
    for f in range(blocks):
        small = jnp.concatenate(
            [
                jnp.concatenate([gnorm[:, f * wide:(f + 1) * wide], jnp.zeros((8, 256 - wide), f32)], axis=1),
                jnp.concatenate([gmu, jnp.zeros((8, 248), f32)], axis=1),
                jnp.concatenate([gskip_acc[...], jnp.zeros((8, 128), f32)], axis=1),
                jnp.zeros((erows - 24, 256), f32),
            ],
            axis=0,
        )
        gpack[f * part + trows:(f + 1) * part, 768:] = small.astype(bf16)
    for m in range(blocks):
        base = jnp.bitwise_xor(me, m) * part
        keep_ref[m] = gpack[pl.ds(pl.multiple_of(base + core * half, 16), half), :]
        send_ref[m] = gpack[pl.ds(pl.multiple_of(base + (1 - core) * half, 16), half), :]


def emb_table():
    steps = np.arange(TB, dtype=np.float32)[:, None]
    col = np.arange(D)
    freq = np.exp(-np.log(np.float32(10000.0)) * (2 * (col // 2)).astype(np.float32) / np.float32(D)).astype(np.float32)
    angle = steps * freq[None]
    tab = np.where(col[None] % 2 == 0, np.sin(angle), np.cos(angle)).astype(np.float32)
    return np.concatenate([tab, np.zeros((256 - TB, D), np.float32)], axis=0)


def run_block(blocks, place, live, cnt, skip, kinds, src, dst, tim, feat, cot, mu, own, near, far):
    S = jax.ShapeDtypeStruct
    smem = pl.BlockSpec(memory_space=pltpu.SMEM)
    vmem = pl.BlockSpec(memory_space=pltpu.VMEM)
    V = pltpu.VMEM
    part = (TYPES * D + D) // blocks
    return pl.pallas_call(
        functools.partial(kernel, blocks),
        out_shape=(
            S((N, D), bf16), S((N, D), bf16),
            S((blocks, part // 2, 1024), bf16), S((blocks, part // 2, 1024), bf16),
        ),
        in_specs=[smem] * 4 + [vmem] * (10 + 2 * (blocks - 1)),
        out_specs=[vmem] * 4,
        scratch_shapes=[
            pltpu.SMEM((40,), jnp.int32), pltpu.SMEM((40,), jnp.int32), pltpu.SMEM((40,), jnp.int32),
            V((blocks * part, 1024), bf16), V((blocks * part, 1024), bf16), V((TYPES * D, D), f32),
            V((8, D), f32), V((8, 128), f32),
            V((8, N), jnp.int32), V((1024, 1024), bf16), V((1024, N), bf16), V((512, N), bf16), V((512, 1024), bf16),
            V((D, N), bf16), V((D, 256), bf16),
            V((8, 256, 256), bf16), V((8, 256, 256), bf16), V((8, 256, 256), bf16), V((8, 256, 256), bf16),
            V((8, 256, 128), f32), V((8, 256, 128), f32), V((8, 8, 128), f32),
            V((512, 8192), bf16), V((D, 8192), bf16), V((D, 8192), bf16), V((D, 8192), bf16), V((8, 8192), f32), V((8, 8192), f32),
            V((D + 16, N), f32), V((D + 16, N), bf16), V((D, N), f32), V((512, N), f32), V((512, 1024), f32), V((D, N), f32),
        ],
        compiler_params=pltpu.CompilerParams(vmem_limit_bytes=63 << 20),
        name="layer",
    )(
        place, live, cnt, skip, kinds.reshape(1, N), kinds.reshape(8, 128), src, dst, tim,
        feat, cot, mu, jnp.asarray(emb_table(), bf16), own, *near, *far,
    )


def tree(terms):
    while len(terms) > 1:
        terms = [terms[i] + terms[i + 1] for i in range(0, len(terms), 2)]
    return terms[0]


def add_core_kernel(blocks, keep_ref, got_ref, *outs):
    for m in range(blocks):
        outs[m][...] = (keep_ref[m].astype(f32) + got_ref[m].astype(f32)).astype(bf16)


def add_core(blocks, keep, got):
    rows = keep.shape[1]
    return pl.pallas_call(
        functools.partial(add_core_kernel, blocks),
        out_shape=[jax.ShapeDtypeStruct((rows, 1024), bf16)] * blocks,
        name="add_core",
    )(keep, got)


def add_parts_kernel(lines, zi_ref, *refs):
    ins, outs = refs[:-lines], refs[-lines:]
    total = tree([r[...].astype(f32) for r in ins]).astype(bf16)
    wide = 1024 // lines
    pieces = [total[:, j * wide:(j + 1) * wide] for j in range(lines)]
    for k in range(lines):
        want = jnp.bitwise_xor(zi_ref[0], k)
        for j in range(lines):
            @pl.when(want == j)
            def _():
                outs[k][...] = pieces[j]


def add_parts(lines, zi, terms):
    rows = terms[0].shape[0]
    return pl.pallas_call(
        functools.partial(add_parts_kernel, lines),
        out_shape=[jax.ShapeDtypeStruct((rows, 1024 // lines), bf16)] * lines,
        in_specs=[pl.BlockSpec(memory_space=pltpu.SMEM)] + [pl.BlockSpec(memory_space=pltpu.VMEM)] * len(terms),
        name="add_parts",
    )(zi, *terms)


def add_lines_kernel(*refs):
    refs[-1][...] = tree([r[...].astype(f32) for r in refs[:-1]]).astype(bf16)


def add_lines(terms):
    return pl.pallas_call(
        add_lines_kernel, out_shape=jax.ShapeDtypeStruct(terms[0].shape, bf16), name="add_lines"
    )(*terms)


def adam(param, first, second, avg, grad, rate):
    first_new = beta_one * first + (1.0 - beta_one) * grad
    second_new = beta_two * second + (1.0 - beta_two) * grad * grad
    first_hat = first_new / (1.0 - beta_one**STEP)
    second_hat = second_new / (1.0 - beta_two**STEP)
    param_new = param - rate * (first_hat / (jnp.sqrt(second_hat) + adam_eps) + decay_rate * param)
    avg_new = ema_keep * avg + (1.0 - ema_keep) * param_new
    return (param_new, first_new, second_new, avg_new)


def update_kernel(lines, trows, erows, place_ref, *refs):
    pieces, refs = refs[:2 * lines], refs[2 * lines:]
    states, outs, gsum = refs[:16], refs[16:32], refs[32]
    core, zi = place_ref[1], place_ref[2]
    half = (trows + erows) // 2
    wide = 1024 // lines
    for side in range(2):
        at = pl.ds(pl.multiple_of(jnp.bitwise_xor(core, side) * half, 16), half)
        for k in range(lines):
            want = jnp.bitwise_xor(zi, k)
            for j in range(lines):
                @pl.when(want == j)
                def _():
                    gsum[at, j * wide:(j + 1) * wide] = pieces[side * lines + k][...]
    nwide = states[8].shape[1]
    grads = (
        gsum[0:trows, :].astype(f32),
        gsum[trows:trows + erows, 0:768].astype(f32),
        gsum[trows:trows + 16, 768:768 + nwide].astype(f32)[0:8],
    )
    for i in range(3):
        new = adam(*[states[4 * i + j][...] for j in range(4)], grads[i], rates[i])
        for j in range(4):
            outs[4 * i + j][...] = new[j]
    mix = gsum[trows:trows + 32, 768:896].astype(f32)
    lanes = lax.broadcasted_iota(jnp.int32, (8, 128), 1)
    grad_mu = jnp.where(lanes < 8, mix[8:16], 0.0)
    grad_skip = jnp.where(lanes < 8, mix[16:24], 0.0)
    grad_mix = jnp.concatenate([grad_mu, grad_skip], axis=0)
    new = adam(*[states[12 + j][...] for j in range(4)], grad_mix, rates[3])
    for j in range(4):
        outs[12 + j][...] = new[j]


def update(lines, place, pieces, states):
    trows, erows = states[0].shape[0], states[4].shape[0]
    return pl.pallas_call(
        functools.partial(update_kernel, lines, trows, erows),
        out_shape=[jax.ShapeDtypeStruct(x.shape, f32) for x in states],
        in_specs=[pl.BlockSpec(memory_space=pltpu.SMEM)]
        + [pl.BlockSpec(memory_space=pltpu.VMEM)] * (len(pieces) + 16),
        scratch_shapes=[pltpu.VMEM((trows + erows, 1024), bf16)],
        compiler_params=pltpu.CompilerParams(vmem_limit_bytes=40 << 20),
        name="update",
    )(place, *pieces, *states)


def wide_mix(mix):
    mu = jnp.pad(mix[:64].reshape(8, 8), ((0, 0), (0, 120)))
    skip = jnp.pad(jnp.broadcast_to(mix[64:, None], (4, 128)), ((0, 4), (0, 0)))
    return jnp.concatenate([mu, skip], axis=0)


def narrow_mix(wide):
    return jnp.concatenate([wide[:8, :8].reshape(64), wide[8:12, 0]], axis=0)


def shards(dp, fsdp, *args):
    (
        node_feat, out_cot, node_type, node_count, edge_src, edge_dst, edge_time, edge_count,
        type_weight, type_first, type_second, type_avg,
        edge_weight, edge_first, edge_second, edge_avg,
        norm_params, norm_first, norm_second, norm_avg,
        mix_params, mix_first, mix_second, mix_avg,
    ) = args
    lines = dp // 2
    dp_at, fsdp_at = lax.axis_index("dp"), lax.axis_index("fsdp")
    core, zi = dp_at % 2, dp_at // 2
    place = jnp.stack([fsdp_at, core, zi]).astype(jnp.int32)

    def swap(x, axis, mask):
        size = dp if axis == "dp" else fsdp
        return lax.ppermute(x, axis, [(i, i ^ mask) for i in range(size)])

    trows, erows = type_weight.shape[0], edge_weight.shape[0]
    nwide = norm_params.shape[1]
    half = (trows + erows) // 2
    corner = jnp.pad(norm_params, ((0, erows - 8), (0, 256 - nwide)))
    own = jnp.concatenate([type_weight, jnp.concatenate([edge_weight, corner], axis=1)], axis=0).astype(bf16)
    mine = lax.dynamic_slice_in_dim(own, core * half, half, 0)
    near = [swap(mine, "fsdp", m) for m in range(1, fsdp)]
    far = [swap(x, "dp", 1) for x in near]
    mix = lax.optimization_barrier(mix_params.astype(bf16)).astype(f32)
    mu = jnp.broadcast_to((mix[:64] * DK ** (-0.5)).reshape(REL, H, 1), (REL, H, 128))
    layer_out, input_grad, keep, send = run_block(
        fsdp, place, node_count, edge_count, mix[64:], node_type, edge_src, edge_dst, edge_time,
        node_feat, out_cot, mu, own, near, far,
    )
    sums = add_core(fsdp, keep, swap(send, "dp", 1))
    pieces = add_parts(lines, place[2:], [sums[0]] + [swap(sums[m], "fsdp", m) for m in range(1, fsdp)])
    total = add_lines([pieces[0]] + [swap(pieces[k], "dp", 2 * k) for k in range(1, lines)])
    totals = [total] + [swap(total, "dp", 2 * k) for k in range(1, lines)]
    others = [swap(x, "dp", 1) for x in totals]
    states = [
        type_weight, type_first, type_second, type_avg,
        edge_weight, edge_first, edge_second, edge_avg,
        norm_params, norm_first, norm_second, norm_avg,
    ] + [wide_mix(x) for x in (mix_params, mix_first, mix_second, mix_avg)]
    new = update(lines, place, totals + others, states)
    return (layer_out, input_grad, *new[:12], *[narrow_mix(x) for x in new[12:]])


def solution(mesh):
    whole = P(("dp", "fsdp"), None)
    flat = P(("dp", "fsdp"))
    state = [P("fsdp", None)] * 8 + [P(None, "fsdp")] * 4 + [P()] * 4
    return jax.shard_map(
        functools.partial(shards, mesh.shape["dp"], mesh.shape["fsdp"]),
        mesh=mesh,
        in_specs=tuple([whole, whole, flat, flat, whole, whole, whole, flat] + state),
        out_specs=tuple([whole, whole] + state),
        check_vma=False,
    )
```

```python
import functools

import jax
import jax.numpy as jnp
import numpy as np
from jax import lax
from jax.experimental import pallas as pl
from jax.experimental.pallas import tpu as pltpu
from jax.sharding import PartitionSpec as P

D, H, DK, TYPES, REL, TB = 256, 8, 32, 4, 8, 240
N = 1024
SLOTS = 1024
EC = 512
SUB = 128
NSUB = EC // SUB
NC = 256
EDGES = REL * SLOTS + EC
bf16 = jnp.bfloat16
f32 = jnp.float32
norm_eps = 1e-5
STEP = 10
beta_one = 0.9
beta_two = 0.999
adam_eps = 1e-08
decay_rate = 0.01
ema_keep = 0.7
rates = (0.2, 0.2, 0.6, 0.6)
score_scale = DK ** (-0.5)

SMEM = pl.BlockSpec(memory_space=pltpu.SMEM)
VMEM = pl.BlockSpec(memory_space=pltpu.VMEM)
ANY = pl.BlockSpec(memory_space=pl.ANY)
S = jax.ShapeDtypeStruct
V = pltpu.VMEM
MIB = 1 << 20
SOURCE, TARGET, TIME, TYPE, BUCKET = range(5)
LAYER_VMEM = 60 * MIB
GROUP = 4
WIDE = 1024 // GROUP


def nn(a, b):
    return jnp.dot(a, b, preferred_element_type=f32)


def nt(a, b):
    return lax.dot_general(a, b, (((1,), (1,)), ((), ())), preferred_element_type=f32)


def one_hot_rows(row, count):
    wide = row.shape[1]
    base = lax.broadcasted_iota(jnp.int32, (256, wide), 0).astype(bf16)
    one, zero = jnp.ones((), bf16), jnp.zeros((), bf16)
    return jnp.concatenate(
        [jnp.where(base == (row - 256 * g).astype(bf16), one, zero) for g in range(count // 256)], axis=0
    )


def head_sum(x):
    return jnp.sum(x.reshape(H, DK, x.shape[1]), axis=1)


def head_wide(x):
    return jnp.broadcast_to(x[:, None, :], (H, DK, x.shape[1])).reshape(D, x.shape[1])


def hi_lo(x):
    high = x.astype(bf16).astype(f32)
    return jnp.concatenate([high, x - high], axis=0).astype(bf16)


def eye():
    return (
        lax.broadcasted_iota(jnp.int32, (256, 256), 0) == lax.broadcasted_iota(jnp.int32, (256, 256), 1)
    ).astype(f32).astype(bf16)


def pick(masks, wide):
    out = wide[0] * masks[0:1]
    for s in range(1, TYPES):
        out = jnp.where(masks[s:s + 1] > 0, wide[s], out)
    return out


def stack(pieces):
    return pieces[0] if len(pieces) == 1 else jnp.concatenate(pieces, axis=0)


class Layout:
    def __init__(self, blocks):
        self.blocks = blocks
        self.trows, self.erows = TYPES * D // blocks, D // blocks
        self.part = self.trows + self.erows
        self.half = self.part // 2
        self.wide = D // blocks

    def type_rows(self, s):
        for f in range(self.blocks):
            a, b = max(s * D, f * self.trows), min((s + 1) * D, (f + 1) * self.trows)
            if a < b:
                yield f, f * self.part + a - f * self.trows, f * self.part + b - f * self.trows, a - s * D, b - s * D

    def get_type(self, ref, s, c0, c1):
        return stack([ref[a:b, c0:c1] for _, a, b, _, _ in self.type_rows(s)])

    def get_edge(self, ref, c0, c1):
        return stack([ref[f * self.part + self.trows:(f + 1) * self.part, c0:c1] for f in range(self.blocks)])

    def get_norm(self, ref):
        rows = [f * self.part + self.trows for f in range(self.blocks)]
        return jnp.concatenate([ref[a:a + 16, 768:768 + self.wide].astype(f32) for a in rows], axis=1).astype(bf16)

    def weight_copies(self, me, core, own, near, far, wpk, sems):
        out = [pltpu.make_async_copy(own, wpk.at[pl.ds(pl.multiple_of(me * self.part, 16), self.part)], sems.at[0])]
        for m in range(1, self.blocks):
            base = jnp.bitwise_xor(me, m) * self.part
            for i, (ref, side) in enumerate(((near[m - 1], core), (far[m - 1], 1 - core))):
                at = pl.ds(pl.multiple_of(base + side * self.half, 16), self.half)
                out.append(pltpu.make_async_copy(ref, wpk.at[at], sems.at[2 * m - 1 + i]))
        return out


def position():
    return lax.axis_index("fsdp"), lax.rem(lax.axis_index("dp"), 2), lax.div(lax.axis_index("dp"), 2)


def list_blocks(cnt_ref, lst_r, lst_o, lst_c):
    def put(k, r, j, c):
        lst_r[k] = r
        lst_o[k] = j
        lst_c[k] = c - j * SUB

    def pairs(r, k):
        c = cnt_ref[r]

        def one(j, k):
            put(k, r, 2 * j, c)
            put(k + 1, r, 2 * j + 1, c)
            return k + 2
        return lax.fori_loop(0, (c + SUB - 1) // SUB // 2, one, k)

    def odd(r, k):
        c = cnt_ref[r]
        blocks = (c + SUB - 1) // SUB
        put(k, r, jnp.minimum(blocks, SLOTS // SUB) - 1, c)
        return k + lax.rem(blocks, 2)
    paired = lax.fori_loop(0, REL, pairs, 0)
    total = lax.fori_loop(0, REL, odd, paired)
    for extra in range(2 * NSUB):
        put(total + extra, 0, 0, 0)
    return paired // NSUB, (total + NSUB - 1) // NSUB


def rows_of(ref, lst_r, lst_o, c):
    pieces = []
    for k in range(NSUB):
        r, j = lst_r[c * NSUB + k], lst_o[c * NSUB + k]
        pair = ref[pl.ds(r, 1), pl.ds(pl.multiple_of(lax.div(j, 2) * 2 * SUB, 2 * SUB), 2 * SUB)]
        pieces.append(jnp.where(lax.rem(j, 2) == 0, pair[:, :SUB], pair[:, SUB:]))
    return jnp.concatenate(pieces, axis=1)


def place(c):
    return pl.ds(pl.multiple_of(c * EC, EC), EC)


LISTS = [pltpu.SMEM((REL * SLOTS // SUB + 2 * NSUB,), jnp.int32)] * 3


def pack_half_kernel(lay, type_ref, edge_ref, norm_ref, mine_ref, buf, sems):
    _, core, _ = position()
    rest = lay.half - lay.erows
    for side in range(2):
        @pl.when(core == side)
        def _():
            rows = lay.half if side == 0 else rest
            first = pltpu.make_async_copy(
                type_ref.at[pl.ds(side * lay.half, rows)], buf.at[pl.ds(0, rows)], sems.at[0]
            )
            first.start()
            if side == 1:
                second = pltpu.make_async_copy(edge_ref, buf.at[pl.ds(rest, lay.erows), pl.ds(0, 768)], sems.at[1])
                second.start()
                corner = jnp.concatenate([norm_ref[...], jnp.zeros((8, 256 - lay.wide), f32)], axis=1)
                buf[rest:, 768:] = jnp.concatenate([corner, jnp.zeros((lay.erows - 8, 256), f32)], axis=0)
                second.wait()
            first.wait()
    mine_ref[...] = buf[...].astype(bf16)


def pack_half(lay, type_weight, edge_weight, norm_params):
    return pl.pallas_call(
        functools.partial(pack_half_kernel, lay),
        out_shape=S((lay.half, 1024), bf16),
        in_specs=[ANY, ANY, VMEM],
        scratch_shapes=[V((lay.half, 1024), f32), pltpu.SemaphoreType.DMA((2,))],
        compiler_params=pltpu.CompilerParams(vmem_limit_bytes=63 * MIB),
        name="pack_half",
    )(type_weight, edge_weight, norm_params)


def pack_kernel(lay, type_ref, edge_ref, norm_ref, own_ref):
    own_ref[0:lay.trows, :] = type_ref[...].astype(bf16)
    own_ref[lay.trows:, 0:768] = edge_ref[...].astype(bf16)
    corner = jnp.concatenate([norm_ref[...], jnp.zeros((8, 256 - lay.wide), f32)], axis=1)
    own_ref[lay.trows:, 768:] = jnp.concatenate([corner, jnp.zeros((lay.erows - 8, 256), f32)], axis=0).astype(bf16)


def pack(lay, type_weight, edge_weight, norm_params):
    return pl.pallas_call(
        functools.partial(pack_kernel, lay),
        out_shape=S((lay.part, 1024), bf16),
        compiler_params=pltpu.CompilerParams(vmem_limit_bytes=63 * MIB),
        name="pack",
    )(type_weight, edge_weight, norm_params)


def before_kernel(cnt_ref, kinds_ref, src_ref, dst_ref, tim_ref, feat_ref, idx_ref, xg_ref, typ_ref, lst_r, lst_o, lst_c):
    _, chunks = list_blocks(cnt_ref, lst_r, lst_o, lst_c)
    src = src_ref[...]
    for j in range(SLOTS // 128):
        idx = src[:, j * 128:(j + 1) * 128]
        low = jnp.bitwise_and(idx, 127)
        high = jnp.right_shift(idx, 7)
        acc = jnp.zeros((8, 128), jnp.int32)
        for k in range(N // 128):
            row = jnp.broadcast_to(kinds_ref[:, k * 128:(k + 1) * 128], (8, 128))
            acc = jnp.where(high == k, jnp.take_along_axis(row, low, axis=1), acc)
        typ_ref[:, j * 128:(j + 1) * 128] = acc
    ft = nt(eye(), feat_ref[...]).astype(bf16)

    def one(c, _):
        src, dst, tim, typ = [rows_of(ref, lst_r, lst_o, c) for ref in (src_ref, dst_ref, tim_ref, typ_ref)]
        idx_ref[pl.ds(pl.multiple_of(c * 8, 8), 8), :] = jnp.concatenate(
            [src, dst, tim, typ, typ * 256 + tim, src, src, src], axis=0
        )
        xg_ref[:, place(c)] = nn(ft, one_hot_rows(src, N)).astype(bf16)
        return 0

    lax.fori_loop(0, chunks, one, 0)


def before(cnt, kinds, src, dst, tim, feat):
    return pl.pallas_call(
        before_kernel,
        out_shape=(S((EDGES // EC * 8, EC), jnp.int32), S((D, EDGES), bf16)),
        in_specs=[SMEM] + [VMEM] * 5,
        scratch_shapes=[V((REL, SLOTS), jnp.int32)] + LISTS,
        compiler_params=pltpu.CompilerParams(vmem_limit_bytes=63 * MIB),
        cost_estimate=pl.CostEstimate(flops=2 * D * N * EDGES, bytes_accessed=6 * MIB, transcendentals=0),
        name="before",
    )(cnt, kinds, src, dst, tim, feat)


def layer_kernel(lay, *refs):
    nb = lay.blocks - 1
    (
        live_ref, cnt_ref, kinds_ref, mix_ref, idx_ref, emb_ref, cot_hbm, feat_hbm, own_ref,
    ) = refs[:9]
    near, far, xg_hbm = refs[9:9 + nb], refs[9 + nb:9 + 2 * nb], refs[9 + 2 * nb]
    (
        out_ref, dqkv_ref, skp_ref, keep_ref, send_ref,
        lst_r, lst_o, lst_c,
        wpk, gpack, gout, gnorm, gskip, xg, outs, low, cot_ref, feat_ref,
        wt, xcat, qt, rte, dn_buf, dkve_buf, mu,
        bda, bdat, bdm, bdmt, ga, gm, dmu,
        kve, qe, msg, wexp, raws,
        num, dnum, dqkv, dtkv, skp,
        wsem, xsem, osem, gsem,
    ) = refs[10 + 2 * nb:]
    me, core, zi = position()
    zi = lax.rem(zi, GROUP)
    feat_copy = pltpu.make_async_copy(feat_hbm, feat_ref, xsem.at[1])
    feat_copy.start()
    weights = lay.weight_copies(me, core, own_ref, near, far, wpk, wsem)
    for copy in weights:
        copy.start()
    xg_copy = pltpu.make_async_copy(xg_hbm, xg, xsem.at[0])
    xg_copy.start()
    cot_copy = pltpu.make_async_copy(cot_hbm, cot_ref, xsem.at[2])

    ident = eye()
    whole, chunks = list_blocks(cnt_ref, lst_r, lst_o, lst_c)

    def row(c, k):
        return idx_ref[pl.ds(pl.multiple_of(c * 8, 8), 8), :][k:k + 1]

    for ref in (num, dqkv, dtkv, ga, gm, dmu, gnorm, gskip, gout):
        ref[...] = jnp.zeros_like(ref)
    dkve_buf[...] = jnp.zeros_like(dkve_buf)

    mix = jnp.broadcast_to(mix_ref[...].astype(bf16).astype(f32), (8, 68))
    lanes68 = lax.broadcasted_iota(jnp.int32, (8, 68), 1)
    line68 = lax.broadcasted_iota(jnp.int32, (8, 68), 0)

    def column(first):
        return jnp.sum(jnp.where(lanes68 == first + line68, mix, 0.0), axis=1, keepdims=True)

    for r in range(REL):
        mu[r] = jnp.broadcast_to(column(r * H) * score_scale, (H, 128))
    skip_col = column(REL * H)

    kinds = kinds_ref[...]
    masks = (lax.broadcasted_iota(jnp.int32, (8, N), 0) == kinds).astype(f32)
    feat_copy.wait()
    featt = nt(ident, feat_ref[...])
    for s in range(TYPES):
        xcat[s * D:(s + 1) * D, :] = (featt * masks[s:s + 1]).astype(bf16)
    for copy in weights:
        copy.wait()
    cot_copy.start()

    lane = lax.broadcasted_iota(jnp.int32, (D, 128), 1)
    rowi = lax.broadcasted_iota(jnp.int32, (D, 128), 0)
    on_diag = (lane // DK) == (rowi // DK) % 4
    zeros = jnp.zeros((128, 128), f32)
    for p in range(4):
        x = lay.get_edge(wpk, p * 128, (p + 1) * 128).astype(f32)
        rolled = [x if k == 0 else pltpu.roll(x, 32 * k, 1) for k in range(4)]
        for g in range(4):
            r, m = 2 * p + g // 2, g % 2
            t = jnp.concatenate([rolled[(h % 4 - g) % 4][h * 32:(h + 1) * 32] for h in range(H)], axis=0)
            t = jnp.where(on_diag, t, 0.0)
            for ref, a, b in (
                (bdm if m else bda, t[:128], t[128:]), (bdmt if m else bdat, t[:128].T, t[128:].T)
            ):
                ref[r] = jnp.concatenate(
                    [jnp.concatenate([a, zeros], axis=1), jnp.concatenate([zeros, b], axis=1)], axis=0
                ).astype(bf16)

    for cb in range(4):
        for s in range(4):
            wt[cb * 256:(cb + 1) * 256, s * 256:(s + 1) * 256] = nt(
                ident, lay.get_type(wpk, s, cb * 256, (cb + 1) * 256)
            ).astype(bf16)
    qt[...] = nn(wt[:D, :], xcat[...]).astype(bf16)
    wet = nt(ident, lay.get_edge(wpk, 512, 768)).astype(bf16)
    rte[...] = nt(wet, emb_ref[...]).astype(bf16)

    def mu_of(c):
        return jnp.concatenate([mu[lst_r[c * NSUB + k]] for k in range(NSUB)], axis=1)

    def blocks_of(c, wide):
        return [(lst_r[c * NSUB + k * (wide // SUB)], slice(k * wide, (k + 1) * wide)) for k in range(EC // wide)]

    def lookup(c):
        rt = nn(rte[...], one_hot_rows(row(c, TIME), 256))
        return (xg[:, place(c)].astype(f32) + rt).astype(bf16)

    def lookup_q(c):
        qe[:, place(c)] = nn(qt[...], one_hot_rows(row(c, TARGET), N)).astype(bf16)

    def project(c, xe):
        cu = row(c, TYPE)
        zero = jnp.zeros((), bf16)
        xm = jnp.concatenate([jnp.where(cu == s, xe, zero) for s in range(TYPES)], axis=0)
        kve[:, place(c)] = nn(wt[D:3 * D, :], xm).astype(bf16)

    def forward(wide, c, _):
        at = place(c)
        kv_e = kve[:, at]
        q_e = qe[:, at].astype(f32)
        ks, ms = [], []
        for r, sl in blocks_of(c, wide):
            ks.append(nn(bdat[r], kv_e[:D, sl]))
            ms.append(nn(bdmt[r], kv_e[D:, sl]))
        ka = jnp.concatenate(ks, axis=1)
        me_ = jnp.concatenate(ms, axis=1)
        xe = lookup(c + 1)
        xg[:, at] = ka.astype(bf16)
        msg[:, at] = me_.astype(bf16)
        raw = head_sum(ka * q_e)
        raws[:, at] = raw
        lanes = lax.broadcasted_iota(jnp.int32, (H, SUB), 1)
        w = jnp.exp(raw * mu_of(c))
        w = jnp.concatenate(
            [jnp.where(lanes < lst_c[c * NSUB + k], w[:, k * SUB:(k + 1) * SUB], 0.0) for k in range(NSUB)], axis=1
        )
        wexp[:, at] = w
        wm = (head_wide(w) * me_).astype(bf16)
        lookup_q(c + 1)
        num[...] += nt(jnp.concatenate([wm, hi_lo(w)], axis=0), one_hot_rows(row(c, TARGET), N))
        project(c + 1, xe)
        return 0

    xg_copy.wait()
    project(0, lookup(0))
    lookup_q(0)
    lax.fori_loop(0, whole, functools.partial(forward, 2 * SUB), 0)
    lax.fori_loop(whole, chunks, functools.partial(forward, SUB), 0)

    cot_copy.wait()
    nwt = nt(ident, lay.get_norm(wpk))

    def nodes(c):
        at = pl.ds(pl.multiple_of(c * NC, NC), NC)
        mk = (lax.broadcasted_iota(jnp.int32, (8, NC), 0) == kinds_ref[:, at]).astype(f32)
        live = (lax.broadcasted_iota(jnp.int32, (1, NC), 1) + c * NC < live_ref[0]).astype(f32)
        den = num[D:D + H, at] + num[D + H:, at] + (1.0 - live)
        denw = head_wide(den)
        agg = num[:D, at] / denw
        phi = 0.5 * (1.0 + lax.erf(agg * (0.5 ** 0.5)))
        act = (agg * phi).astype(bf16).astype(f32)
        acat = jnp.concatenate([(act * mk[s:s + 1]).astype(bf16) for s in range(TYPES)], axis=0)
        yield
        trans = nn(wt[3 * D:, :], acat)
        yield
        alpha = 1.0 / (1.0 + jnp.exp(-jnp.sum(mk * skip_col, axis=0, keepdims=True)))
        ft = nt(ident, feat_ref[at, :])
        res = alpha * trans + (1.0 - alpha) * ft
        mean = jnp.mean(res, axis=0, keepdims=True)
        cen = res - mean
        inv = lax.rsqrt(jnp.mean(cen * cen, axis=0, keepdims=True) + norm_eps)
        nrm = cen * inv
        gain = nwt[:, 0:1] * mk[0:1]
        bias = nwt[:, 4:5] * mk[0:1]
        for s in range(1, TYPES):
            gain = gain + nwt[:, s:s + 1] * mk[s:s + 1]
            bias = bias + nwt[:, 4 + s:5 + s] * mk[s:s + 1]
        outs[at, :] = (live * (nrm * gain + bias)).T.astype(bf16)
        dy = live * nt(ident, cot_ref[at, :])
        oh16 = jnp.concatenate([mk, jnp.zeros((8, NC), f32)], axis=0).astype(bf16)
        dyn = dy * nrm
        dyn_hi = dyn.astype(bf16)
        dyn_lo = (dyn - dyn_hi.astype(f32)).astype(bf16)
        gnorm[0:4, :] += (nt(oh16, dyn_hi) + nt(oh16, dyn_lo))[0:4]
        gnorm[4:8, :] += nt(oh16, dy.astype(bf16))[0:4]
        dn = dy * gain
        dres = inv * (dn - jnp.mean(dn, axis=0, keepdims=True) - nrm * jnp.mean(dn * nrm, axis=0, keepdims=True))
        dtr = (alpha * dres).astype(bf16)
        yield
        dact = pick(mk, [nn(lay.get_type(wpk, s, 3 * D, 4 * D), dtr) for s in range(TYPES)])
        yield
        skp[:, at] = (1.0 - alpha) * dres
        dal = jnp.sum(dres * (trans - ft), axis=0, keepdims=True) * alpha * (1.0 - alpha)
        gskip[...] += jnp.broadcast_to(jnp.sum(mk * dal, axis=1, keepdims=True), (8, 128))
        gout[...] += nt(acat, dtr)
        dagg = dact * (phi + agg * (jnp.exp(-0.5 * agg * agg) * (0.5 / np.pi) ** 0.5))
        dnum[0:D, at] = (dagg / denw).astype(bf16)
        dnum[D:, at] = hi_lo(-head_sum(dagg * agg) / den)
        yield

    def node_steps(c, _):
        for _ in zip(nodes(2 * c), nodes(2 * c + 1)):
            pass
        return 0

    lax.fori_loop(0, N // NC // 2, node_steps, 0)
    finish = [
        pltpu.make_async_copy(outs, out_ref, osem.at[0]),
        pltpu.make_async_copy(skp, skp_ref, osem.at[1]),
    ]
    for copy in finish:
        copy.start()

    def gather_back(c):
        dn_buf[...] = nn(dnum[...], one_hot_rows(row(c, TARGET), N))

    def scatter_back(c):
        dkve = dkve_buf[...]
        dqkv[:, D:] += nt(one_hot_rows(row(c, SOURCE), N), dkve)
        dtkv[...] += nt(one_hot_rows(row(c, BUCKET), 1024), dkve)

    def backward(wide, c, _):
        at = place(c)
        scatter_back(jnp.maximum(c - 1, 0))
        dn_e = dn_buf[:D]
        w = wexp[:, at]
        dw = head_sum(dn_e * msg[:, at].astype(f32)) + dn_buf[D:D + H] + dn_buf[D + H:]
        ds = dw * w
        dsr = ds * raws[:, at]
        ss = head_wide(ds * mu_of(c))
        dka = (ss * qe[:, at].astype(f32)).astype(bf16)
        dms = (head_wide(w) * dn_e).astype(bf16)
        dqe = (ss * xg[:, at].astype(f32)).astype(bf16)
        gather_back(c + 1)
        for r, sl in blocks_of(c, wide):
            dkve_buf[0:D, sl] = nn(bda[r], dka[:, sl]).astype(bf16)
            dkve_buf[D:, sl] = nn(bdm[r], dms[:, sl]).astype(bf16)
        for r, sl in blocks_of(c, wide):
            at_k = pl.ds(pl.multiple_of(c * EC + sl.start, SUB), wide)
            gak = nt(kve[0:D, at_k], dka[:, sl])
            gmk = nt(kve[D:, at_k], dms[:, sl])
            ga[r, 0:128] += gak[0:128, 0:128]
            ga[r, 128:] += gak[128:, 128:]
            gm[r, 0:128] += gmk[0:128, 0:128]
            gm[r, 128:] += gmk[128:, 128:]
            dmu[r] += sum(dsr[:, k:k + 128] for k in range(sl.start, sl.stop, 128))
        dqkv[:, :D] += nt(one_hot_rows(row(c, TARGET), N), dqe)
        return 0

    gather_back(0)
    lax.fori_loop(0, whole, functools.partial(backward, 2 * SUB), 0)
    lax.fori_loop(whole, chunks, functools.partial(backward, SUB), 0)
    scatter_back(chunks - 1)

    low[...] = dqkv[...].astype(bf16)
    last = pltpu.make_async_copy(low, dqkv_ref, osem.at[2])
    last.start()
    finish.append(last)
    dt = dtkv[...].astype(bf16)
    drte = jnp.zeros((D, 256), f32)
    for s in range(TYPES):
        drte = drte + nt(lay.get_type(wpk, s, D, 3 * D), dt[s * 256:(s + 1) * 256, :])

    def put_edge(c0, value):
        for f in range(lay.blocks):
            gpack[f * lay.part + lay.trows:(f + 1) * lay.part, c0:c0 + value.shape[1]] = value[
                f * lay.erows:(f + 1) * lay.erows
            ].astype(bf16)

    for p in range(4):
        acc = jnp.zeros((D, 128), f32)
        for g in range(4):
            r, m = 2 * p + g // 2, g % 2
            t = jnp.where(on_diag, (gm if m else ga)[r], 0.0)
            rolled = [t if k == 0 else pltpu.roll(t, 32 * k, 1) for k in range(4)]
            acc = acc + jnp.concatenate([rolled[(g - h % 4) % 4][h * 32:(h + 1) * 32] for h in range(H)], axis=0)
        put_edge(p * 128, acc)
    embt = nt(ident, emb_ref[...]).astype(bf16)
    put_edge(512, nt(embt, drte.astype(bf16)))

    lane8 = lax.broadcasted_iota(jnp.int32, (8, 256), 1)
    line8 = lax.broadcasted_iota(jnp.int32, (8, 256), 0)
    mixg = jnp.where(lane8 == REL * H + line8, gskip[:, 0:1], 0.0)
    for r in range(REL):
        col = jnp.sum(dmu[r], axis=1, keepdims=True) * score_scale
        mixg = mixg + jnp.where(lane8 == r * H + line8, col, 0.0)
    mixg = jnp.broadcast_to(jnp.sum(mixg, axis=0, keepdims=True), (8, 256))
    for f in range(lay.blocks):
        corner = jnp.concatenate(
            [gnorm[:, f * lay.wide:(f + 1) * lay.wide], jnp.zeros((8, 256 - lay.wide), f32)], axis=1
        )
        small = jnp.concatenate([corner, mixg, jnp.zeros((lay.erows - 16, 256), f32)], axis=0)
        gpack[f * lay.part + lay.trows:(f + 1) * lay.part, 768:] = small.astype(bf16)

    done = 0
    for s in range(TYPES):
        g = nn(xcat[s * D:(s + 1) * D, :], low[...])
        g_kv = g[:, D:] + nn(rte[...], dt[s * 256:(s + 1) * 256, :])
        value = jnp.concatenate([g[:, :D], g_kv, gout[s * D:(s + 1) * D, :]], axis=1).astype(bf16)
        for _, a, b, c, d in lay.type_rows(s):
            gpack[a:b, :] = value[c:d]
        while done < lay.blocks and (done + 1) * lay.trows <= (s + 1) * D:
            m = jnp.bitwise_xor(me, done)
            for i, (ref, side) in enumerate(((send_ref, 1 - core), (keep_ref, core))):
                at = pl.ds(pl.multiple_of(done * lay.part + side * lay.half, 16), lay.half)
                for j in range(GROUP):
                    copy = pltpu.make_async_copy(
                        gpack.at[at, pl.ds(j * WIDE, WIDE)], ref.at[m, jnp.bitwise_xor(zi, j)],
                        gsem.at[(2 * done + i) * GROUP + j],
                    )
                    copy.start()
                    finish.append(copy)
            done += 1
    for copy in finish:
        copy.wait()


def emb_table():
    steps = np.arange(TB, dtype=np.float32)[:, None]
    col = np.arange(D)
    freq = np.exp(-np.log(np.float32(10000.0)) * (2 * (col // 2)).astype(np.float32) / np.float32(D)).astype(np.float32)
    angle = steps * freq[None]
    tab = np.where(col[None] % 2 == 0, np.sin(angle), np.cos(angle)).astype(np.float32)
    return np.concatenate([tab, np.zeros((256 - TB, D), np.float32)], axis=0)


def layer(lay, live, cnt, kinds, mix, idx, cot, feat, own, near, far, xg):
    sums = S((lay.blocks, GROUP, lay.half, WIDE), bf16)
    edges = lambda rows, kind: V((rows, EDGES), kind)
    return pl.pallas_call(
        functools.partial(layer_kernel, lay),
        out_shape=[S((N, D), bf16), S((N, 3 * D), bf16), S((D, N), f32), sums, sums],
        in_specs=[SMEM, SMEM] + [VMEM] * 4 + [ANY] * (2 * lay.blocks + 2),
        out_specs=[ANY] * 5,
        scratch_shapes=LISTS + [
            V((lay.blocks * lay.part, 1024), bf16), V((lay.blocks * lay.part, 1024), bf16), V((TYPES * D, D), f32),
            V((8, D), f32), V((8, 128), f32), edges(D, bf16), V((N, D), bf16), V((N, 3 * D), bf16), V((N, D), bf16), V((N, D), bf16),
            V((4 * D, TYPES * D), bf16), V((TYPES * D, N), bf16), V((D, N), bf16), V((D, 256), bf16),
            V((D + 16, EC), f32), V((2 * D, EC), bf16), V((REL, H, 128), f32),
            V((8, D, D), bf16), V((8, D, D), bf16), V((8, D, D), bf16), V((8, D, D), bf16),
            V((8, D, 128), f32), V((8, D, 128), f32), V((8, 8, 128), f32),
            edges(2 * D, bf16), edges(D, bf16), V((D, REL * SLOTS), bf16),
            V((H, REL * SLOTS), f32), V((H, REL * SLOTS), f32),
            V((D + 16, N), f32), V((D + 16, N), bf16), V((N, 3 * D), f32), V((TYPES * 256, 2 * D), f32), V((D, N), f32),
            pltpu.SemaphoreType.DMA((2 * lay.blocks - 1,)), pltpu.SemaphoreType.DMA((3,)),
            pltpu.SemaphoreType.DMA((3,)), pltpu.SemaphoreType.DMA((2 * lay.blocks * GROUP,)),
        ],
        compiler_params=pltpu.CompilerParams(vmem_limit_bytes=LAYER_VMEM),
        cost_estimate=pl.CostEstimate(flops=60 * 10**9, bytes_accessed=16 * MIB, transcendentals=0),
        name="layer",
    )(live, cnt, kinds, mix, idx, jnp.asarray(emb_table(), bf16), cot, feat, own, *near, *far, xg)


def input_kernel(lay, *refs):
    nb = lay.blocks - 1
    kinds_ref, dqkv_ref, skp_ref, own_ref = refs[:4]
    near, far = refs[4:4 + nb], refs[4 + nb:4 + 2 * nb]
    out_ref, wpk, sems = refs[4 + 2 * nb:]
    me, core, _ = position()
    weights = lay.weight_copies(me, core, own_ref, near, far, wpk, sems)
    for copy in weights:
        copy.start()
    masks = (lax.broadcasted_iota(jnp.int32, (8, N), 0) == kinds_ref[...]).astype(f32)
    for copy in weights:
        copy.wait()
    for c in range(N // NC):
        at = slice(c * NC, (c + 1) * NC)
        proj = pick(masks[:, at], [nt(lay.get_type(wpk, s, 0, 3 * D), dqkv_ref[at, :]) for s in range(TYPES)])
        out_ref[at, :] = (proj + skp_ref[:, at]).T.astype(bf16)


def input_gradient(lay, kinds, dqkv, skp, own, near, far):
    return pl.pallas_call(
        functools.partial(input_kernel, lay),
        out_shape=S((N, D), bf16),
        in_specs=[VMEM] * 3 + [ANY] * (2 * lay.blocks - 1),
        scratch_shapes=[V((lay.blocks * lay.part, 1024), bf16), pltpu.SemaphoreType.DMA((2 * lay.blocks - 1,))],
        compiler_params=pltpu.CompilerParams(vmem_limit_bytes=63 * MIB),
        cost_estimate=pl.CostEstimate(flops=2 * N * D * D * 12, bytes_accessed=6 * MIB, transcendentals=0),
        name="input_gradient",
    )(kinds, dqkv, skp, own, *near, *far)


def tree(terms):
    while len(terms) > 1:
        terms = [terms[i] + terms[i + 1] for i in range(0, len(terms), 2)]
    return terms[0]


def add_core_kernel(blocks, keep_ref, got_ref, *refs):
    outs, keep, got, isem, osem = refs[:blocks - 1], *refs[blocks - 1:]
    loads = []
    for m in range(1, blocks):
        pair = [
            pltpu.make_async_copy(keep_ref.at[m], keep.at[m - 1], isem.at[2 * m - 2]),
            pltpu.make_async_copy(got_ref.at[m], got.at[m - 1], isem.at[2 * m - 1]),
        ]
        for copy in pair:
            copy.start()
        loads.append(pair)
    stores = []
    for m in range(1, blocks):
        for copy in loads[m - 1]:
            copy.wait()
        keep[m - 1] = (keep[m - 1].astype(f32) + got[m - 1].astype(f32)).astype(bf16)
        store = pltpu.make_async_copy(keep.at[m - 1], outs[m - 1], osem.at[m - 1])
        store.start()
        stores.append(store)
    for copy in stores:
        copy.wait()


def add_core(blocks, keep, got):
    buf = V((blocks - 1, *keep.shape[1:]), bf16)
    return pl.pallas_call(
        functools.partial(add_core_kernel, blocks),
        out_shape=[S(keep.shape[1:], bf16)] * (blocks - 1),
        in_specs=[ANY, ANY],
        out_specs=[ANY] * (blocks - 1),
        scratch_shapes=[
            buf, buf, pltpu.SemaphoreType.DMA((2 * blocks - 2,)), pltpu.SemaphoreType.DMA((blocks - 1,)),
        ],
        compiler_params=pltpu.CompilerParams(vmem_limit_bytes=63 * MIB),
        name="add_core",
    )(keep, got)


def summed(terms):
    return tree([x.astype(f32) for x in terms]).astype(bf16)


def adam(param, first, second, avg, grad, rate):
    first_new = beta_one * first + (1.0 - beta_one) * grad
    second_new = beta_two * second + (1.0 - beta_two) * grad * grad
    first_hat = first_new / (1.0 - beta_one**STEP)
    second_hat = second_new / (1.0 - beta_two**STEP)
    param_new = param - rate * (first_hat / (jnp.sqrt(second_hat) + adam_eps) + decay_rate * param)
    avg_new = ema_keep * avg + (1.0 - ema_keep) * param_new
    return (param_new, first_new, second_new, avg_new)


def update_kernel(jobs, count, *refs):
    pieces, refs = refs[:2 * GROUP], refs[2 * GROUP:]
    states, outs, refs = refs[:count], refs[count:2 * count], refs[2 * count:]
    gsum, bufs, news, isem, osem = refs[0], refs[1:1 + 4 * len(jobs)], refs[1 + 4 * len(jobs):-2], refs[-2], refs[-1]

    def view(ref, row, rows):
        return ref if rows == ref.shape[0] else ref.at[pl.ds(row, rows)]

    loads = [
        pltpu.make_async_copy(view(states[4 * job[0] + j], job[1], job[2]), bufs[4 * i + j], isem.at[4 * i + j])
        for i, job in enumerate(jobs) for j in range(4)
    ]
    for copy in loads:
        copy.start()
    _, core, zi = position()
    zi = lax.rem(zi, GROUP)
    high = gsum.shape[0] // 2
    for side in range(2):
        at = pl.ds(pl.multiple_of(jnp.bitwise_xor(core, side) * high, 16), high)
        for k in range(GROUP):
            want = jnp.bitwise_xor(zi, k)
            for j in range(GROUP):
                @pl.when(want == j)
                def _():
                    gsum[at, j * WIDE:(j + 1) * WIDE] = pieces[side * GROUP + k][...]
    stores = []
    for i, (group, row, rows, lanes, first, lane, rate) in enumerate(jobs):
        base = first // 16 * 16
        grad = gsum[base:base + max(16, rows), lane:lane + max(lanes, 128)].astype(f32)
        grad = grad[first - base:first - base + rows, :lanes]
        for j in range(4):
            loads[4 * i + j].wait()
        new = adam(*[bufs[4 * i + j][...] for j in range(4)], grad, rate)
        for j in range(4):
            news[4 * i + j][...] = new[j]
            copy = pltpu.make_async_copy(news[4 * i + j], view(outs[4 * group + j], row, rows), osem.at[4 * i + j])
            copy.start()
            stores.append(copy)
    for copy in stores:
        copy.wait()


def update(jobs, pieces, sets):
    states = [x for group in sets for x in group]
    bufs = [V((job[2], job[3]), f32) for job in jobs for _ in range(4)]
    return pl.pallas_call(
        functools.partial(update_kernel, jobs, len(states)),
        out_shape=[S(x.shape, f32) for x in states],
        in_specs=[VMEM] * len(pieces) + [ANY] * len(states),
        out_specs=[ANY] * len(states),
        scratch_shapes=[V((2 * pieces[0].shape[0], 1024), bf16)] + bufs + bufs
        + [pltpu.SemaphoreType.DMA((len(bufs),))] * 2,
        compiler_params=pltpu.CompilerParams(vmem_limit_bytes=63 * MIB),
        name="update",
    )(*pieces, *states)


def shards(dp, fsdp, *args):
    (
        node_feat, out_cot, node_type, node_count, edge_src, edge_dst, edge_time, edge_count,
        type_weight, type_first, type_second, type_avg,
        edge_weight, edge_first, edge_second, edge_avg,
        norm_params, norm_first, norm_second, norm_avg,
        mix_params, mix_first, mix_second, mix_avg,
    ) = args
    lines = dp // 2
    lay = Layout(fsdp)

    def swap(x, axis, mask):
        size = dp if axis == "dp" else fsdp
        return lax.ppermute(x, axis, [(i, i ^ mask) for i in range(size)])

    mine = pack_half(lay, type_weight, edge_weight, norm_params)
    near = [swap(mine, "fsdp", m) for m in range(1, fsdp)]
    kinds = node_type.reshape(1, N)
    own = pack(lay, type_weight, edge_weight, norm_params)
    idx, xg = before(edge_count, kinds, edge_src, edge_dst, edge_time, node_feat)
    own, idx, xg, near[0] = lax.optimization_barrier((own, idx, xg, near[0]))
    far = [swap(x, "dp", 1) for x in near]
    mixes = [x.reshape(1, 68) for x in (mix_params, mix_first, mix_second, mix_avg)]
    layer_out, dqkv, skp, keep, send = layer(
        lay, node_count, edge_count, kinds, mixes[0], idx, out_cot, node_feat,
        own, near, far, xg,
    )
    got = swap(send, "dp", 1)
    chip = add_core(fsdp, keep, got)
    parts = [summed([keep[0], got[0]])] + [swap(chip[m - 1], "fsdp", m) for m in range(1, fsdp)]
    input_grad = input_gradient(lay, kinds, dqkv, skp, own, near, far)
    input_grad, *parts = lax.optimization_barrier((input_grad, *parts))
    pieces = [summed([x[k] for x in parts]) for k in range(GROUP)]
    total = summed([pieces[0]] + [swap(pieces[k], "dp", 2 * k) for k in range(1, GROUP)])
    step = GROUP
    while step < lines:
        total = summed([total, swap(total, "dp", 2 * step)])
        step *= 2
    totals = [total] + [swap(total, "dp", 2 * k) for k in range(1, GROUP)]
    totals = totals + [swap(x, "dp", 1) for x in totals]
    trows, erows = lay.trows, lay.erows
    jobs = [(0, row, erows, 1024, row, 0, rates[0]) for row in range(0, trows, erows)] + [
        (1, 0, erows, 768, trows, 0, rates[1]), (2, 0, 8, lay.wide, trows, 768, rates[2]),
        (3, 0, 1, 68, trows + 8, 768, rates[3]),
    ]
    new = update(jobs, totals, [
        [type_weight, type_first, type_second, type_avg], [edge_weight, edge_first, edge_second, edge_avg],
        [norm_params, norm_first, norm_second, norm_avg], mixes,
    ])
    return (layer_out, input_grad, *new[:12], *[x.reshape(68) for x in new[12:]])


def solution(mesh):
    whole = P(("dp", "fsdp"), None)
    flat = P(("dp", "fsdp"))
    state = [P("fsdp", None)] * 8 + [P(None, "fsdp")] * 4 + [P()] * 4
    return jax.shard_map(
        functools.partial(shards, mesh.shape["dp"], mesh.shape["fsdp"]),
        mesh=mesh,
        in_specs=tuple([whole, whole, flat, flat, whole, whole, whole, flat] + state),
        out_specs=tuple([whole, whole] + state),
        check_vma=False,
    )
```

```python
import functools

import jax
import jax.numpy as jnp
import numpy as np
from jax import lax
from jax.experimental import pallas as pl
from jax.experimental.pallas import tpu as pltpu
from jax.sharding import PartitionSpec as P

D, H, DK, TYPES, REL, TB = 256, 8, 32, 4, 8, 240
N = 1024
SLOTS = 1024
EC = 512
SUB = 128
NSUB = EC // SUB
NC = 256
NODE_STEPS = 4
EDGES = REL * SLOTS + EC
bf16 = jnp.bfloat16
f32 = jnp.float32
norm_eps = 1e-5
STEP = 10
beta_one = 0.9
beta_two = 0.999
adam_eps = 1e-08
decay_rate = 0.01
ema_keep = 0.7
rates = (0.2, 0.2, 0.6, 0.6)
score_scale = DK ** (-0.5)

SMEM = pl.BlockSpec(memory_space=pltpu.SMEM)
VMEM = pl.BlockSpec(memory_space=pltpu.VMEM)
ANY = pl.BlockSpec(memory_space=pl.ANY)
S = jax.ShapeDtypeStruct
V = pltpu.VMEM
MIB = 1 << 20
SOURCE, TARGET, TIME, TYPE, BUCKET = range(5)
LAYER_VMEM = 63 * MIB
GROUP = 4
WIDE = 1024 // GROUP


def nn(a, b):
    return jnp.dot(a, b, preferred_element_type=f32)


def nt(a, b):
    return lax.dot_general(a, b, (((1,), (1,)), ((), ())), preferred_element_type=f32)


def one_hot_rows(row, count):
    wide = row.shape[1]
    base = lax.broadcasted_iota(jnp.int16, (256, wide), 0)
    one, zero = jnp.ones((), bf16), jnp.zeros((), bf16)
    return jnp.concatenate(
        [jnp.where(base == (row - 256 * g).astype(jnp.int16), one, zero) for g in range(count // 256)], axis=0
    )


def head_sum(x):
    return jnp.sum(x.reshape(H, DK, x.shape[1]), axis=1)


def head_wide(x):
    return jnp.broadcast_to(x[:, None, :], (H, DK, x.shape[1])).reshape(D, x.shape[1])


def hi_lo(x):
    high = x.astype(bf16).astype(f32)
    return jnp.concatenate([high, x - high], axis=0).astype(bf16)


def eye():
    return (
        lax.broadcasted_iota(jnp.int32, (256, 256), 0) == lax.broadcasted_iota(jnp.int32, (256, 256), 1)
    ).astype(f32).astype(bf16)


def pick(masks, wide):
    out = wide[0] * masks[0:1]
    for s in range(1, TYPES):
        out = jnp.where(masks[s:s + 1] > 0, wide[s], out)
    return out


def stack(pieces):
    return pieces[0] if len(pieces) == 1 else jnp.concatenate(pieces, axis=0)


class Layout:
    def __init__(self, blocks):
        self.blocks = blocks
        self.trows, self.erows = TYPES * D // blocks, D // blocks
        self.part = self.trows + self.erows
        self.half = self.part // 2
        self.wide = D // blocks

    def type_rows(self, s):
        for f in range(self.blocks):
            a, b = max(s * D, f * self.trows), min((s + 1) * D, (f + 1) * self.trows)
            if a < b:
                yield f, f * self.part + a - f * self.trows, f * self.part + b - f * self.trows, a - s * D, b - s * D

    def get_type(self, ref, s, c0, c1):
        return stack([ref[a:b, c0:c1] for _, a, b, _, _ in self.type_rows(s)])

    def get_edge(self, ref, c0, c1):
        return stack([ref[f * self.part + self.trows:(f + 1) * self.part, c0:c1] for f in range(self.blocks)])

    def get_norm(self, ref):
        rows = [f * self.part + self.trows for f in range(self.blocks)]
        return jnp.concatenate([ref[a:a + 16, 768:768 + self.wide].astype(f32) for a in rows], axis=1).astype(bf16)

    def weight_copies(self, me, core, own, near, far, wpk, sems):
        out = [pltpu.make_async_copy(own, wpk.at[pl.ds(pl.multiple_of(me * self.part, 16), self.part)], sems.at[0])]
        for m in range(1, self.blocks):
            base = jnp.bitwise_xor(me, m) * self.part
            for i, (ref, side) in enumerate(((near[m - 1], core), (far[m - 1], 1 - core))):
                at = pl.ds(pl.multiple_of(base + side * self.half, 16), self.half)
                out.append(pltpu.make_async_copy(ref, wpk.at[at], sems.at[2 * m - 1 + i]))
        return out


def position():
    return lax.axis_index("fsdp"), lax.rem(lax.axis_index("dp"), 2), lax.div(lax.axis_index("dp"), 2)


def list_blocks(cnt_ref, lst_r, lst_o, lst_c):
    def put(k, r, j, c):
        lst_r[k] = r
        lst_o[k] = j
        lst_c[k] = c - j * SUB

    def pairs(r, k):
        c = cnt_ref[r]

        def one(j, k):
            put(k, r, 2 * j, c)
            put(k + 1, r, 2 * j + 1, c)
            return k + 2
        return lax.fori_loop(0, (c + SUB - 1) // SUB // 2, one, k)

    def odd(r, k):
        c = cnt_ref[r]
        blocks = (c + SUB - 1) // SUB
        put(k, r, jnp.minimum(blocks, SLOTS // SUB) - 1, c)
        return k + lax.rem(blocks, 2)
    paired = lax.fori_loop(0, REL, pairs, 0)
    total = lax.fori_loop(0, REL, odd, paired)
    for extra in range(2 * NSUB):
        put(total + extra, 0, 0, 0)
    return paired // NSUB, (total + NSUB - 1) // NSUB


def rows_of(ref, lst_r, lst_o, c):
    pieces = []
    for k in range(NSUB):
        r, j = lst_r[c * NSUB + k], lst_o[c * NSUB + k]
        pair = ref[pl.ds(r, 1), pl.ds(pl.multiple_of(lax.div(j, 2) * 2 * SUB, 2 * SUB), 2 * SUB)]
        pieces.append(jnp.where(lax.rem(j, 2) == 0, pair[:, :SUB], pair[:, SUB:]))
    return jnp.concatenate(pieces, axis=1)


def place(c):
    return pl.ds(pl.multiple_of(c * EC, EC), EC)


LISTS = [pltpu.SMEM((REL * SLOTS // SUB + 2 * NSUB,), jnp.int32)] * 3


def pack_half_kernel(lay, type_ref, edge_ref, norm_hbm, mine_ref, buf, low, norm_ref, isem, osem):
    _, core, _ = position()
    norm = pltpu.make_async_copy(norm_hbm, norm_ref, isem.at[5])
    norm.start()
    rows = lay.half // 5
    for side in range(2):
        @pl.when(core == side)
        def _():
            loads = []
            for i in range(5):
                if side == 1 and i >= 3:
                    source, to = edge_ref.at[pl.ds((i - 3) * rows, rows)], buf.at[pl.ds(i * rows, rows), pl.ds(0, 768)]
                else:
                    source, to = type_ref.at[pl.ds(side * lay.half + i * rows, rows)], buf.at[pl.ds(i * rows, rows)]
                loads.append(pltpu.make_async_copy(source, to, isem.at[i]))
                loads[-1].start()
            norm.wait()
            if side == 1:
                corner = jnp.concatenate([norm_ref[...], jnp.zeros((8, 256 - lay.wide), f32)], axis=1)
                buf[3 * rows:, 768:] = jnp.concatenate([corner, jnp.zeros((lay.erows - 8, 256), f32)], axis=0)
            stores = []
            for i in range(5):
                loads[i].wait()
                at = slice(i * rows, (i + 1) * rows)
                low[at] = buf[at].astype(bf16)
                stores.append(pltpu.make_async_copy(low.at[pl.ds(i * rows, rows)], mine_ref.at[pl.ds(i * rows, rows)], osem.at[i]))
                stores[-1].start()
            for copy in stores:
                copy.wait()


def pack_half(lay, type_weight, edge_weight, norm_params):
    return pl.pallas_call(
        functools.partial(pack_half_kernel, lay),
        out_shape=S((lay.half, 1024), bf16),
        in_specs=[ANY] * 3,
        out_specs=ANY,
        scratch_shapes=[
            V((lay.half, 1024), f32), V((lay.half, 1024), bf16), V((8, lay.wide), f32),
            pltpu.SemaphoreType.DMA((6,)), pltpu.SemaphoreType.DMA((5,)),
        ],
        compiler_params=pltpu.CompilerParams(vmem_limit_bytes=63 * MIB),
        name="pack_half",
    )(type_weight, edge_weight, norm_params)


def pack_kernel(lay, type_ref, edge_ref, norm_ref, own_ref):
    own_ref[0:lay.trows, :] = type_ref[...].astype(bf16)
    own_ref[lay.trows:, 0:768] = edge_ref[...].astype(bf16)
    corner = jnp.concatenate([norm_ref[...], jnp.zeros((8, 256 - lay.wide), f32)], axis=1)
    own_ref[lay.trows:, 768:] = jnp.concatenate([corner, jnp.zeros((lay.erows - 8, 256), f32)], axis=0).astype(bf16)


def pack(lay, type_weight, edge_weight, norm_params):
    return pl.pallas_call(
        functools.partial(pack_kernel, lay),
        out_shape=S((lay.part, 1024), bf16),
        compiler_params=pltpu.CompilerParams(vmem_limit_bytes=63 * MIB),
        name="pack",
    )(type_weight, edge_weight, norm_params)


def before_kernel(cnt_ref, kinds_ref, src_ref, dst_ref, tim_ref, feat_ref, idx_ref, xg_ref, typ_ref, lst_r, lst_o, lst_c):
    _, chunks = list_blocks(cnt_ref, lst_r, lst_o, lst_c)
    src = src_ref[...]
    for j in range(SLOTS // 128):
        idx = src[:, j * 128:(j + 1) * 128]
        low = jnp.bitwise_and(idx, 127)
        high = jnp.right_shift(idx, 7)
        acc = jnp.zeros((8, 128), jnp.int32)
        for k in range(N // 128):
            row = jnp.broadcast_to(kinds_ref[:, k * 128:(k + 1) * 128], (8, 128))
            acc = jnp.where(high == k, jnp.take_along_axis(row, low, axis=1), acc)
        typ_ref[:, j * 128:(j + 1) * 128] = acc
    ft = nt(eye(), feat_ref[...]).astype(bf16)

    def one(c, _):
        src, dst, tim, typ = [rows_of(ref, lst_r, lst_o, c) for ref in (src_ref, dst_ref, tim_ref, typ_ref)]
        idx_ref[pl.ds(pl.multiple_of(c * 8, 8), 8), :] = jnp.concatenate(
            [src, dst, tim, typ, typ * 256 + tim, src, src, src], axis=0
        )
        xg_ref[:, place(c)] = nn(ft, one_hot_rows(src, N)).astype(bf16)
        return 0

    lax.fori_loop(0, chunks, one, 0)


def before(cnt, kinds, src, dst, tim, feat):
    return pl.pallas_call(
        before_kernel,
        out_shape=(S((EDGES // EC * 8, EC), jnp.int32), S((D, EDGES), bf16)),
        in_specs=[SMEM] + [VMEM] * 5,
        scratch_shapes=[V((REL, SLOTS), jnp.int32)] + LISTS,
        compiler_params=pltpu.CompilerParams(vmem_limit_bytes=63 * MIB),
        cost_estimate=pl.CostEstimate(flops=2 * D * N * EDGES, bytes_accessed=6 * MIB, transcendentals=0),
        name="before",
    )(cnt, kinds, src, dst, tim, feat)


def layer_kernel(lay, *refs):
    nb = lay.blocks - 1
    (
        live_ref, cnt_ref, kinds_hbm, mix_hbm, idx_hbm, emb_hbm, cot_hbm, feat_hbm, own_ref,
    ) = refs[:9]
    near, far, xg_hbm = refs[9:9 + nb], refs[9 + nb:9 + 2 * nb], refs[9 + 2 * nb]
    (
        out_ref, dqkv_ref, skp_ref, keep_ref, send_ref,
        lst_r, lst_o, lst_c,
        wpk, gpack, gout, gnorm, gskip, xg, low, cot_ref, feat_ref, kinds_ref, mix_ref, idx_ref, emb_ref,
        wt, xcat, qt, rte, dn_buf, dkve_buf, mu,
        bda, bdat, bdm, bdmt, ga, gm, dmu,
        kve, qe, msg, wexp, raws,
        num, dnum, dqkv, dtkv, skp,
        wsem, xsem, osem, gsem,
    ) = refs[10 + 2 * nb:]
    me, core, zi = position()
    zi = lax.rem(zi, GROUP)
    small = [
        pltpu.make_async_copy(source, to, xsem.at[3 + i])
        for i, (source, to) in enumerate(
            ((kinds_hbm, kinds_ref), (mix_hbm, mix_ref), (feat_hbm, feat_ref), (idx_hbm, idx_ref), (emb_hbm, emb_ref))
        )
    ]
    weights = lay.weight_copies(me, core, own_ref, near, far, wpk, wsem)
    for copy in small + weights:
        copy.start()
    xg_copy = pltpu.make_async_copy(xg_hbm, xg, xsem.at[0])
    xg_copy.start()
    cot_copy = pltpu.make_async_copy(cot_hbm, cot_ref, xsem.at[2])

    ident = eye()
    whole, chunks = list_blocks(cnt_ref, lst_r, lst_o, lst_c)

    def row(c, k):
        return idx_ref[pl.ds(pl.multiple_of(c * 8, 8), 8), :][k:k + 1]

    for ref in (num, dqkv, dtkv, ga, gm, dmu, gnorm, gskip, gout):
        ref[...] = jnp.zeros_like(ref)
    dkve_buf[...] = jnp.zeros_like(dkve_buf)

    small[0].wait()
    small[1].wait()
    mix = jnp.broadcast_to(mix_ref[...].astype(bf16).astype(f32), (8, 68))
    lanes68 = lax.broadcasted_iota(jnp.int32, (8, 68), 1)
    line68 = lax.broadcasted_iota(jnp.int32, (8, 68), 0)

    def column(first):
        return jnp.sum(jnp.where(lanes68 == first + line68, mix, 0.0), axis=1, keepdims=True)

    for r in range(REL):
        mu[r] = jnp.broadcast_to(column(r * H) * score_scale, (H, 128))
    skip_col = column(REL * H)

    kinds = kinds_ref[...]
    masks = (lax.broadcasted_iota(jnp.int32, (8, N), 0) == kinds).astype(f32)
    small[2].wait()
    featt = nt(ident, feat_ref[...])
    for s in range(TYPES):
        xcat[s * D:(s + 1) * D, :] = (featt * masks[s:s + 1]).astype(bf16)
    for copy in weights + small[3:]:
        copy.wait()
    cot_copy.start()

    lane = lax.broadcasted_iota(jnp.int32, (D, 128), 1)
    rowi = lax.broadcasted_iota(jnp.int32, (D, 128), 0)
    on_diag = (lane // DK) == (rowi // DK) % 4
    zeros = jnp.zeros((128, 128), f32)
    for p in range(4):
        x = lay.get_edge(wpk, p * 128, (p + 1) * 128).astype(f32)
        rolled = [x if k == 0 else pltpu.roll(x, 32 * k, 1) for k in range(4)]
        for g in range(4):
            r, m = 2 * p + g // 2, g % 2
            t = jnp.concatenate([rolled[(h % 4 - g) % 4][h * 32:(h + 1) * 32] for h in range(H)], axis=0)
            t = jnp.where(on_diag, t, 0.0)
            for ref, a, b in (
                (bdm if m else bda, t[:128], t[128:]), (bdmt if m else bdat, t[:128].T, t[128:].T)
            ):
                ref[r] = jnp.concatenate(
                    [jnp.concatenate([a, zeros], axis=1), jnp.concatenate([zeros, b], axis=1)], axis=0
                ).astype(bf16)

    for cb in range(4):
        for s in range(4):
            wt[cb * 256:(cb + 1) * 256, s * 256:(s + 1) * 256] = nt(
                ident, lay.get_type(wpk, s, cb * 256, (cb + 1) * 256)
            ).astype(bf16)
    qt[...] = nn(wt[:D, :], xcat[...]).astype(bf16)
    wet = nt(ident, lay.get_edge(wpk, 512, 768)).astype(bf16)
    rte[...] = nt(wet, emb_ref[...]).astype(bf16)

    def mu_of(c):
        return jnp.concatenate([mu[lst_r[c * NSUB + k]] for k in range(NSUB)], axis=1)

    def blocks_of(c, wide):
        return [(lst_r[c * NSUB + k * (wide // SUB)], slice(k * wide, (k + 1) * wide)) for k in range(EC // wide)]

    def lookup(c):
        rt = nn(rte[...], one_hot_rows(row(c, TIME), 256))
        return (xg[:, place(c)].astype(f32) + rt).astype(bf16)

    def lookup_q(c):
        qe[:, place(c)] = nn(qt[...], one_hot_rows(row(c, TARGET), N)).astype(bf16)

    def project(c, xe):
        cu = row(c, TYPE)
        zero = jnp.zeros((), bf16)
        xm = jnp.concatenate([jnp.where(cu == s, xe, zero) for s in range(TYPES)], axis=0)
        kve[:, place(c)] = nn(wt[D:3 * D, :], xm).astype(bf16)

    def forward(wide, c, _):
        at = place(c)
        kv_e = kve[:, at]
        q_e = qe[:, at].astype(f32)
        ks, ms = [], []
        for r, sl in blocks_of(c, wide):
            ks.append(nn(bdat[r], kv_e[:D, sl]))
            ms.append(nn(bdmt[r], kv_e[D:, sl]))
        ka = jnp.concatenate(ks, axis=1)
        me_ = jnp.concatenate(ms, axis=1)
        xe = lookup(c + 1)
        xg[:, at] = ka.astype(bf16)
        msg[:, at] = me_.astype(bf16)
        raw = head_sum(ka * q_e)
        raws[:, at] = raw
        lanes = lax.broadcasted_iota(jnp.int32, (H, SUB), 1)
        w = jnp.exp(raw * mu_of(c))
        w = jnp.concatenate(
            [jnp.where(lanes < lst_c[c * NSUB + k], w[:, k * SUB:(k + 1) * SUB], 0.0) for k in range(NSUB)], axis=1
        )
        wexp[:, at] = w
        wm = (head_wide(w) * me_).astype(bf16)
        lookup_q(c + 1)
        num[...] += nt(jnp.concatenate([wm, hi_lo(w)], axis=0), one_hot_rows(row(c, TARGET), N))
        project(c + 1, xe)
        return 0

    xg_copy.wait()
    project(0, lookup(0))
    lookup_q(0)
    lax.fori_loop(0, whole, functools.partial(forward, 2 * SUB), 0)
    lax.fori_loop(whole, chunks, functools.partial(forward, SUB), 0)

    cot_copy.wait()
    nwt = nt(ident, lay.get_norm(wpk)).astype(bf16)
    out_rows = jnp.concatenate([lay.get_type(wpk, s, 3 * D, 4 * D) for s in range(TYPES)], axis=1)

    def nodes(c):
        at = pl.ds(pl.multiple_of(c * NC, NC), NC)
        mk = (lax.broadcasted_iota(jnp.int32, (8, NC), 0) == kinds_ref[:, at]).astype(f32)
        live = (lax.broadcasted_iota(jnp.int32, (1, NC), 1) + c * NC < live_ref[0]).astype(f32)
        den = num[D:D + H, at] + num[D + H:, at] + (1.0 - live)
        inv_den = head_wide(1.0 / den)
        agg = num[:D, at] * inv_den
        phi = 0.5 * (1.0 + lax.erf(agg * (0.5 ** 0.5)))
        act = (agg * phi).astype(bf16)
        mkl = mk.astype(bf16)
        acat = jnp.concatenate([act * mkl[s:s + 1] for s in range(TYPES)], axis=0)
        yield
        trans = nn(wt[3 * D:, :], acat)
        yield
        alpha = 1.0 / (1.0 + jnp.exp(-jnp.sum(mk * skip_col, axis=0, keepdims=True)))
        ft = nt(ident, feat_ref[at, :])
        none = jnp.zeros((4, NC), f32)
        oh16 = jnp.concatenate([mk[0:4], none, none, none], axis=0).astype(bf16)
        gain = nn(nwt, oh16)
        bias = nn(nwt, jnp.concatenate([none, mk[0:4], none, none], axis=0).astype(bf16))
        dy = live * nt(ident, cot_ref[at, :])
        res = alpha * trans + (1.0 - alpha) * ft
        mean = jnp.mean(res, axis=0, keepdims=True)
        cen = res - mean
        inv = lax.rsqrt(jnp.mean(cen * cen, axis=0, keepdims=True) + norm_eps)
        nrm = cen * inv
        cot_ref[at, :] = (live * (nrm * gain + bias)).T.astype(bf16)
        dyn = dy * nrm
        dyn_hi = dyn.astype(bf16)
        dyn_lo = (dyn - dyn_hi.astype(f32)).astype(bf16)
        gnorm[0:4, :] += (nt(oh16, dyn_hi) + nt(oh16, dyn_lo))[0:4]
        gnorm[4:8, :] += nt(oh16, dy.astype(bf16))[0:4]
        dn = dy * gain
        dres = inv * (dn - jnp.mean(dn, axis=0, keepdims=True) - nrm * jnp.mean(dn * nrm, axis=0, keepdims=True))
        dtr = (alpha * dres).astype(bf16)
        yield
        dact = nn(out_rows, jnp.concatenate([dtr * mkl[s:s + 1] for s in range(TYPES)], axis=0))
        yield
        skp[:, at] = (1.0 - alpha) * dres
        dal = jnp.sum(dres * (trans - ft), axis=0, keepdims=True) * alpha * (1.0 - alpha)
        gskip[...] += jnp.broadcast_to(jnp.sum(mk * dal, axis=1, keepdims=True), (8, 128))
        gout[...] += nt(acat, dtr)
        dagg = dact * (phi + agg * (jnp.exp(-0.5 * agg * agg) * (0.5 / np.pi) ** 0.5))
        dnum[0:D, at] = (dagg * inv_den).astype(bf16)
        dnum[D:, at] = hi_lo(-head_sum(dagg * agg) / den)
        yield

    def node_steps(c, _):
        for _ in zip(*[nodes(NODE_STEPS * c + i) for i in range(NODE_STEPS)]):
            pass
        return 0

    lax.fori_loop(0, N // NC // NODE_STEPS, node_steps, 0)
    finish = [
        pltpu.make_async_copy(cot_ref, out_ref, osem.at[0]),
        pltpu.make_async_copy(skp, skp_ref, osem.at[1]),
    ]
    for copy in finish:
        copy.start()

    def gather_back(c):
        dn_buf[...] = nn(dnum[...], one_hot_rows(row(c, TARGET), N))

    def scatter_back(c):
        dkve = dkve_buf[...]
        dqkv[:, D:] += nt(one_hot_rows(row(c, SOURCE), N), dkve)
        dtkv[...] += nt(one_hot_rows(row(c, BUCKET), 1024), dkve)

    def backward(wide, c, _):
        at = place(c)
        scatter_back(jnp.maximum(c - 1, 0))
        dn_e = dn_buf[:D]
        w = wexp[:, at]
        dw = head_sum(dn_e * msg[:, at].astype(f32)) + dn_buf[D:D + H] + dn_buf[D + H:]
        ds = dw * w
        dsr = ds * raws[:, at]
        ss = head_wide(ds * mu_of(c))
        dka = (ss * qe[:, at].astype(f32)).astype(bf16)
        dms = (head_wide(w) * dn_e).astype(bf16)
        dqe = (ss * xg[:, at].astype(f32)).astype(bf16)
        gather_back(c + 1)
        for r, sl in blocks_of(c, wide):
            dkve_buf[0:D, sl] = nn(bda[r], dka[:, sl]).astype(bf16)
            dkve_buf[D:, sl] = nn(bdm[r], dms[:, sl]).astype(bf16)
        for r, sl in blocks_of(c, wide):
            at_k = pl.ds(pl.multiple_of(c * EC + sl.start, SUB), wide)
            gak = nt(kve[0:D, at_k], dka[:, sl])
            gmk = nt(kve[D:, at_k], dms[:, sl])
            ga[r, 0:128] += gak[0:128, 0:128]
            ga[r, 128:] += gak[128:, 128:]
            gm[r, 0:128] += gmk[0:128, 0:128]
            gm[r, 128:] += gmk[128:, 128:]
            dmu[r] += sum(dsr[:, k:k + 128] for k in range(sl.start, sl.stop, 128))
        dqkv[:, :D] += nt(one_hot_rows(row(c, TARGET), N), dqe)
        return 0

    gather_back(0)
    def backward_pair(c, _):
        backward(2 * SUB, 2 * c, 0)
        backward(2 * SUB, 2 * c + 1, 0)
        return 0

    lax.fori_loop(0, whole // 2, backward_pair, 0)
    lax.fori_loop(whole // 2 * 2, whole, functools.partial(backward, 2 * SUB), 0)
    lax.fori_loop(whole, chunks, functools.partial(backward, SUB), 0)
    scatter_back(chunks - 1)

    low[...] = dqkv[...].astype(bf16)
    last = pltpu.make_async_copy(low, dqkv_ref, osem.at[2])
    last.start()
    finish.append(last)
    dt = dtkv[...].astype(bf16)
    drte = jnp.zeros((D, 256), f32)
    for s in range(TYPES):
        drte = drte + nt(lay.get_type(wpk, s, D, 3 * D), dt[s * 256:(s + 1) * 256, :])

    def put_edge(c0, value):
        for f in range(lay.blocks):
            gpack[f * lay.part + lay.trows:(f + 1) * lay.part, c0:c0 + value.shape[1]] = value[
                f * lay.erows:(f + 1) * lay.erows
            ].astype(bf16)

    for p in range(4):
        acc = jnp.zeros((D, 128), f32)
        for g in range(4):
            r, m = 2 * p + g // 2, g % 2
            t = jnp.where(on_diag, (gm if m else ga)[r], 0.0)
            rolled = [t if k == 0 else pltpu.roll(t, 32 * k, 1) for k in range(4)]
            acc = acc + jnp.concatenate([rolled[(g - h % 4) % 4][h * 32:(h + 1) * 32] for h in range(H)], axis=0)
        put_edge(p * 128, acc)
    embt = nt(ident, emb_ref[...]).astype(bf16)
    put_edge(512, nt(embt, drte.astype(bf16)))

    lane8 = lax.broadcasted_iota(jnp.int32, (8, 256), 1)
    line8 = lax.broadcasted_iota(jnp.int32, (8, 256), 0)
    mixg = jnp.where(lane8 == REL * H + line8, gskip[:, 0:1], 0.0)
    for r in range(REL):
        col = jnp.sum(dmu[r], axis=1, keepdims=True) * score_scale
        mixg = mixg + jnp.where(lane8 == r * H + line8, col, 0.0)
    mixg = jnp.broadcast_to(jnp.sum(mixg, axis=0, keepdims=True), (8, 256))
    for f in range(lay.blocks):
        corner = jnp.concatenate(
            [gnorm[:, f * lay.wide:(f + 1) * lay.wide], jnp.zeros((8, 256 - lay.wide), f32)], axis=1
        )
        small = jnp.concatenate([corner, mixg, jnp.zeros((lay.erows - 16, 256), f32)], axis=0)
        gpack[f * lay.part + lay.trows:(f + 1) * lay.part, 768:] = small.astype(bf16)

    done = 0
    for s in range(TYPES):
        g = nn(xcat[s * D:(s + 1) * D, :], low[...])
        g_kv = g[:, D:] + nn(rte[...], dt[s * 256:(s + 1) * 256, :])
        value = jnp.concatenate([g[:, :D], g_kv, gout[s * D:(s + 1) * D, :]], axis=1).astype(bf16)
        for _, a, b, c, d in lay.type_rows(s):
            gpack[a:b, :] = value[c:d]
        while done < lay.blocks and (done + 1) * lay.trows <= (s + 1) * D:
            m = jnp.bitwise_xor(me, done)
            for i, (ref, side) in enumerate(((send_ref, 1 - core), (keep_ref, core))):
                at = pl.ds(pl.multiple_of(done * lay.part + side * lay.half, 16), lay.half)
                for j in range(GROUP):
                    copy = pltpu.make_async_copy(
                        gpack.at[at, pl.ds(j * WIDE, WIDE)], ref.at[m, jnp.bitwise_xor(zi, j)],
                        gsem.at[(2 * done + i) * GROUP + j],
                    )
                    copy.start()
                    finish.append(copy)
            done += 1
    for copy in finish:
        copy.wait()


def emb_table():
    steps = np.arange(TB, dtype=np.float32)[:, None]
    col = np.arange(D)
    freq = np.exp(-np.log(np.float32(10000.0)) * (2 * (col // 2)).astype(np.float32) / np.float32(D)).astype(np.float32)
    angle = steps * freq[None]
    tab = np.where(col[None] % 2 == 0, np.sin(angle), np.cos(angle)).astype(np.float32)
    return np.concatenate([tab, np.zeros((256 - TB, D), np.float32)], axis=0)


def layer(lay, live, cnt, kinds, mix, idx, cot, feat, own, near, far, xg):
    sums = S((lay.blocks, GROUP, lay.half, WIDE), bf16)
    edges = lambda rows, kind: V((rows, EDGES), kind)
    return pl.pallas_call(
        functools.partial(layer_kernel, lay),
        out_shape=[S((N, D), bf16), S((N, 3 * D), bf16), S((D, N), f32), sums, sums],
        in_specs=[SMEM, SMEM] + [ANY] * (2 * lay.blocks + 6),
        out_specs=[ANY] * 5,
        scratch_shapes=LISTS + [
            V((lay.blocks * lay.part, 1024), bf16), V((lay.blocks * lay.part, 1024), bf16), V((TYPES * D, D), f32),
            V((8, D), f32), V((8, 128), f32), edges(D, bf16), V((N, 3 * D), bf16), V((N, D), bf16), V((N, D), bf16),
            V(kinds.shape, jnp.int32), V(mix.shape, f32), V(idx.shape, jnp.int32), V((256, D), bf16),
            V((4 * D, TYPES * D), bf16), V((TYPES * D, N), bf16), V((D, N), bf16), V((D, 256), bf16),
            V((D + 16, EC), f32), V((2 * D, EC), bf16), V((REL, H, 128), f32),
            V((8, D, D), bf16), V((8, D, D), bf16), V((8, D, D), bf16), V((8, D, D), bf16),
            V((8, D, 128), f32), V((8, D, 128), f32), V((8, 8, 128), f32),
            edges(2 * D, bf16), edges(D, bf16), V((D, REL * SLOTS), bf16),
            V((H, REL * SLOTS), f32), V((H, REL * SLOTS), f32),
            V((D + 16, N), f32), V((D + 16, N), bf16), V((N, 3 * D), f32), V((TYPES * 256, 2 * D), f32), V((D, N), f32),
            pltpu.SemaphoreType.DMA((2 * lay.blocks - 1,)), pltpu.SemaphoreType.DMA((8,)),
            pltpu.SemaphoreType.DMA((3,)), pltpu.SemaphoreType.DMA((2 * lay.blocks * GROUP,)),
        ],
        compiler_params=pltpu.CompilerParams(vmem_limit_bytes=LAYER_VMEM),
        cost_estimate=pl.CostEstimate(flops=60 * 10**9, bytes_accessed=16 * MIB, transcendentals=0),
        name="layer",
    )(live, cnt, kinds, mix, idx, jnp.asarray(emb_table(), bf16), cot, feat, own, *near, *far, xg)


def input_kernel(lay, *refs):
    nb = lay.blocks - 1
    kinds_ref, dqkv_ref, skp_ref, own_ref = refs[:4]
    near, far = refs[4:4 + nb], refs[4 + nb:4 + 2 * nb]
    out_ref, wpk, sems = refs[4 + 2 * nb:]
    me, core, _ = position()
    weights = lay.weight_copies(me, core, own_ref, near, far, wpk, sems)
    for copy in weights:
        copy.start()
    masks = (lax.broadcasted_iota(jnp.int32, (8, N), 0) == kinds_ref[...]).astype(f32)
    for copy in weights:
        copy.wait()
    for c in range(N // NC):
        at = slice(c * NC, (c + 1) * NC)
        proj = pick(masks[:, at], [nt(lay.get_type(wpk, s, 0, 3 * D), dqkv_ref[at, :]) for s in range(TYPES)])
        out_ref[at, :] = (proj + skp_ref[:, at]).T.astype(bf16)


def input_gradient(lay, kinds, dqkv, skp, own, near, far):
    return pl.pallas_call(
        functools.partial(input_kernel, lay),
        out_shape=S((N, D), bf16),
        in_specs=[VMEM] * 3 + [ANY] * (2 * lay.blocks - 1),
        scratch_shapes=[V((lay.blocks * lay.part, 1024), bf16), pltpu.SemaphoreType.DMA((2 * lay.blocks - 1,))],
        compiler_params=pltpu.CompilerParams(vmem_limit_bytes=63 * MIB),
        cost_estimate=pl.CostEstimate(flops=2 * N * D * D * 12, bytes_accessed=6 * MIB, transcendentals=0),
        name="input_gradient",
    )(kinds, dqkv, skp, own, *near, *far)


def tree(terms):
    while len(terms) > 1:
        terms = [terms[i] + terms[i + 1] for i in range(0, len(terms), 2)]
    return terms[0]


def add_core_kernel(blocks, keep_ref, got_ref, *refs):
    outs, keep, got, isem, osem = refs[:blocks - 1], *refs[blocks - 1:]
    loads = []
    for m in range(1, blocks):
        pair = [
            pltpu.make_async_copy(keep_ref.at[m], keep.at[m - 1], isem.at[2 * m - 2]),
            pltpu.make_async_copy(got_ref.at[m], got.at[m - 1], isem.at[2 * m - 1]),
        ]
        for copy in pair:
            copy.start()
        loads.append(pair)
    stores = []
    for m in range(1, blocks):
        for copy in loads[m - 1]:
            copy.wait()
        keep[m - 1] = (keep[m - 1].astype(f32) + got[m - 1].astype(f32)).astype(bf16)
        store = pltpu.make_async_copy(keep.at[m - 1], outs[m - 1], osem.at[m - 1])
        store.start()
        stores.append(store)
    for copy in stores:
        copy.wait()


def add_core(blocks, keep, got):
    buf = V((blocks - 1, *keep.shape[1:]), bf16)
    return pl.pallas_call(
        functools.partial(add_core_kernel, blocks),
        out_shape=[S(keep.shape[1:], bf16)] * (blocks - 1),
        in_specs=[ANY, ANY],
        out_specs=[ANY] * (blocks - 1),
        scratch_shapes=[
            buf, buf, pltpu.SemaphoreType.DMA((2 * blocks - 2,)), pltpu.SemaphoreType.DMA((blocks - 1,)),
        ],
        compiler_params=pltpu.CompilerParams(vmem_limit_bytes=63 * MIB),
        name="add_core",
    )(keep, got)


def summed(terms):
    return tree([x.astype(f32) for x in terms]).astype(bf16)


def adam(param, first, second, avg, grad, rate):
    root = (1.0 - beta_two**STEP) ** 0.5
    first_new = beta_one * first + (1.0 - beta_one) * grad
    second_new = beta_two * second + (1.0 - beta_two) * (grad * grad)
    below = jnp.sqrt(second_new) + adam_eps * root
    guess = pl.reciprocal(below, approx=True)
    guess = guess * (2.0 - below * guess)
    param_new = (1.0 - rate * decay_rate) * param - (rate * root / (1.0 - beta_one**STEP)) * (first_new * guess)
    avg_new = ema_keep * avg + (1.0 - ema_keep) * param_new
    return (param_new, first_new, second_new, avg_new)


def update_kernel(jobs, count, *refs):
    pieces, refs = refs[:2 * GROUP], refs[2 * GROUP:]
    states, outs, refs = refs[:count], refs[count:2 * count], refs[2 * count:]
    gsum, bufs, news, isem, osem = refs[0], refs[1:1 + 4 * len(jobs)], refs[1 + 4 * len(jobs):-2], refs[-2], refs[-1]

    def view(ref, row, rows):
        return ref if rows == ref.shape[0] else ref.at[pl.ds(row, rows)]

    loads = [
        pltpu.make_async_copy(view(states[4 * job[0] + j], job[1], job[2]), bufs[4 * i + j], isem.at[4 * i + j])
        for i, job in enumerate(jobs) for j in range(4)
    ]
    for copy in loads:
        copy.start()
    _, core, zi = position()
    zi = lax.rem(zi, GROUP)
    high = gsum.shape[0] // 2
    for side in range(2):
        at = pl.ds(pl.multiple_of(jnp.bitwise_xor(core, side) * high, 16), high)
        for k in range(GROUP):
            want = jnp.bitwise_xor(zi, k)
            for j in range(GROUP):
                @pl.when(want == j)
                def _():
                    gsum[at, j * WIDE:(j + 1) * WIDE] = pieces[side * GROUP + k][...]
    stores = []
    for i, (group, row, rows, lanes, first, lane, rate) in enumerate(jobs):
        base = first // 16 * 16
        grad = gsum[base:base + max(16, rows), lane:lane + max(lanes, 128)].astype(f32)
        grad = grad[first - base:first - base + rows, :lanes]
        for j in range(4):
            loads[4 * i + j].wait()
        new = adam(*[bufs[4 * i + j][...] for j in range(4)], grad, rate)
        for j in range(4):
            news[4 * i + j][...] = new[j]
            copy = pltpu.make_async_copy(news[4 * i + j], view(outs[4 * group + j], row, rows), osem.at[4 * i + j])
            copy.start()
            stores.append(copy)
    for copy in stores:
        copy.wait()


def update(jobs, pieces, sets):
    states = [x for group in sets for x in group]
    bufs = [V((job[2], job[3]), f32) for job in jobs for _ in range(4)]
    return pl.pallas_call(
        functools.partial(update_kernel, jobs, len(states)),
        out_shape=[S(x.shape, f32) for x in states],
        in_specs=[VMEM] * len(pieces) + [ANY] * len(states),
        out_specs=[ANY] * len(states),
        scratch_shapes=[V((2 * pieces[0].shape[0], 1024), bf16)] + bufs + bufs
        + [pltpu.SemaphoreType.DMA((len(bufs),))] * 2,
        compiler_params=pltpu.CompilerParams(vmem_limit_bytes=63 * MIB),
        name="update",
    )(*pieces, *states)


def shards(dp, fsdp, *args):
    (
        node_feat, out_cot, node_type, node_count, edge_src, edge_dst, edge_time, edge_count,
        type_weight, type_first, type_second, type_avg,
        edge_weight, edge_first, edge_second, edge_avg,
        norm_params, norm_first, norm_second, norm_avg,
        mix_params, mix_first, mix_second, mix_avg,
    ) = args
    lines = dp // 2
    lay = Layout(fsdp)

    def swap(x, axis, mask):
        size = dp if axis == "dp" else fsdp
        return lax.ppermute(x, axis, [(i, i ^ mask) for i in range(size)])

    mine = pack_half(lay, type_weight, edge_weight, norm_params)
    near = [swap(mine, "fsdp", m) for m in range(1, fsdp)]
    kinds = node_type.reshape(1, N)
    own = pack(lay, type_weight, edge_weight, norm_params)
    idx, xg = before(edge_count, kinds, edge_src, edge_dst, edge_time, node_feat)
    own, idx, xg, near[0] = lax.optimization_barrier((own, idx, xg, near[0]))
    far = [swap(x, "dp", 1) for x in near]
    mixes = [x.reshape(1, 68) for x in (mix_params, mix_first, mix_second, mix_avg)]
    layer_out, dqkv, skp, keep, send = layer(
        lay, node_count, edge_count, kinds, mixes[0], idx, out_cot, node_feat,
        own, near, far, xg,
    )
    got = swap(send, "dp", 1)
    chip = add_core(fsdp, keep, got)
    parts = [summed([keep[0], got[0]])] + [swap(chip[m - 1], "fsdp", m) for m in range(1, fsdp)]
    input_grad = input_gradient(lay, kinds, dqkv, skp, own, near, far)
    input_grad, *parts = lax.optimization_barrier((input_grad, *parts))
    pieces = [summed([x[k] for x in parts]) for k in range(GROUP)]
    total = summed([pieces[0]] + [swap(pieces[k], "dp", 2 * k) for k in range(1, GROUP)])
    step = GROUP
    while step < lines:
        total = summed([total, swap(total, "dp", 2 * step)])
        step *= 2
    totals = [total] + [swap(total, "dp", 2 * k) for k in range(1, GROUP)]
    totals = totals + [swap(x, "dp", 1) for x in totals]
    trows, erows = lay.trows, lay.erows
    jobs = [(0, row, erows, 1024, row, 0, rates[0]) for row in range(0, trows, erows)] + [
        (1, 0, erows, 768, trows, 0, rates[1]), (2, 0, 8, lay.wide, trows, 768, rates[2]),
        (3, 0, 1, 68, trows + 8, 768, rates[3]),
    ]
    new = update(jobs, totals, [
        [type_weight, type_first, type_second, type_avg], [edge_weight, edge_first, edge_second, edge_avg],
        [norm_params, norm_first, norm_second, norm_avg], mixes,
    ])
    return (layer_out, input_grad, *new[:12], *[x.reshape(68) for x in new[12:]])


def solution(mesh):
    whole = P(("dp", "fsdp"), None)
    flat = P(("dp", "fsdp"))
    state = [P("fsdp", None)] * 8 + [P(None, "fsdp")] * 4 + [P()] * 4
    return jax.shard_map(
        functools.partial(shards, mesh.shape["dp"], mesh.shape["fsdp"]),
        mesh=mesh,
        in_specs=tuple([whole, whole, flat, flat, whole, whole, whole, flat] + state),
        out_specs=tuple([whole, whole] + state),
        check_vma=False,
    )
```

```python
import functools

import jax
import jax.numpy as jnp
import numpy as np
from jax import lax
from jax.experimental import pallas as pl
from jax.experimental.pallas import tpu as pltpu
from jax.sharding import PartitionSpec as P

D, H, DK, TYPES, REL, TB = 256, 8, 32, 4, 8, 240
N = 1024
SLOTS = 1024
EC = 512
SUB = 128
NSUB = EC // SUB
NC = 256
NODE_STEPS = 4
EDGES = REL * SLOTS + EC
bf16 = jnp.bfloat16
f32 = jnp.float32
norm_eps = 1e-5
STEP = 10
beta_one = 0.9
beta_two = 0.999
adam_eps = 1e-08
decay_rate = 0.01
ema_keep = 0.7
rates = (0.2, 0.2, 0.6, 0.6)
score_scale = DK ** (-0.5)

SMEM = pl.BlockSpec(memory_space=pltpu.SMEM)
VMEM = pl.BlockSpec(memory_space=pltpu.VMEM)
ANY = pl.BlockSpec(memory_space=pl.ANY)
S = jax.ShapeDtypeStruct
V = pltpu.VMEM
MIB = 1 << 20
INPUT_VMEM = 62 * MIB
SECOND = 3
SOURCE, TARGET, TIME, TYPE, BUCKET = range(5)
LAYER_VMEM = 63 * MIB
GROUP = 4
WIDE = 1024 // GROUP


def nn(a, b):
    return jnp.dot(a, b, preferred_element_type=f32)


def nt(a, b):
    return lax.dot_general(a, b, (((1,), (1,)), ((), ())), preferred_element_type=f32)


def one_hot_rows(row, count):
    wide = row.shape[1]
    base = lax.broadcasted_iota(jnp.int16, (256, wide), 0)
    one, zero = jnp.ones((), bf16), jnp.zeros((), bf16)
    return jnp.concatenate(
        [jnp.where(base == (row - 256 * g).astype(jnp.int16), one, zero) for g in range(count // 256)], axis=0
    )


def head_sum(x):
    return jnp.sum(x.reshape(H, DK, x.shape[1]), axis=1)


def head_wide(x):
    return jnp.broadcast_to(x[:, None, :], (H, DK, x.shape[1])).reshape(D, x.shape[1])


def hi_lo(x):
    high = x.astype(bf16).astype(f32)
    return jnp.concatenate([high, x - high], axis=0).astype(bf16)


def eye():
    return (
        lax.broadcasted_iota(jnp.int32, (256, 256), 0) == lax.broadcasted_iota(jnp.int32, (256, 256), 1)
    ).astype(f32).astype(bf16)


def pick(masks, wide):
    out = wide[0] * masks[0:1]
    for s in range(1, TYPES):
        out = jnp.where(masks[s:s + 1] > 0, wide[s], out)
    return out


def stack(pieces):
    return pieces[0] if len(pieces) == 1 else jnp.concatenate(pieces, axis=0)


class Layout:
    def __init__(self, blocks):
        self.blocks = blocks
        self.trows, self.erows = TYPES * D // blocks, D // blocks
        self.part = self.trows + self.erows
        self.half = self.part // 2
        self.wide = D // blocks
        self.second = self.half * SECOND // 10 // 16 * 16
        self.first = self.half - self.second

    def type_rows(self, s):
        for f in range(self.blocks):
            a, b = max(s * D, f * self.trows), min((s + 1) * D, (f + 1) * self.trows)
            if a < b:
                yield f, f * self.part + a - f * self.trows, f * self.part + b - f * self.trows, a - s * D, b - s * D

    def get_type(self, ref, s, c0, c1):
        return stack([ref[a:b, c0:c1] for _, a, b, _, _ in self.type_rows(s)])

    def get_edge(self, ref, c0, c1):
        return stack([ref[f * self.part + self.trows:(f + 1) * self.part, c0:c1] for f in range(self.blocks)])

    def get_norm(self, ref):
        rows = [f * self.part + self.trows for f in range(self.blocks)]
        return jnp.concatenate([ref[a:a + 16, 768:768 + self.wide].astype(f32) for a in rows], axis=1).astype(bf16)

    def weight_copies(self, me, core, own, near, far, wpk, sems):
        out = [pltpu.make_async_copy(own, wpk.at[pl.ds(pl.multiple_of(me * self.part, 16), self.part)], sems.at[0])]
        for m in range(1, self.blocks):
            base = jnp.bitwise_xor(me, m) * self.part
            for i, (ref, side) in enumerate(((near[m - 1], core), (far[m - 1], 1 - core))):
                at = pl.ds(pl.multiple_of(base + side * self.half, 16), self.half)
                out.append(pltpu.make_async_copy(ref, wpk.at[at], sems.at[2 * m - 1 + i]))
        return out


def position():
    return lax.axis_index("fsdp"), lax.rem(lax.axis_index("dp"), 2), lax.div(lax.axis_index("dp"), 2)


def list_blocks(cnt_ref, lst_r, lst_o, lst_c):
    def put(k, r, j, c):
        lst_r[k] = r
        lst_o[k] = j
        lst_c[k] = c - j * SUB

    def pairs(r, k):
        c = cnt_ref[r]

        def one(j, k):
            put(k, r, 2 * j, c)
            put(k + 1, r, 2 * j + 1, c)
            return k + 2
        return lax.fori_loop(0, (c + SUB - 1) // SUB // 2, one, k)

    def odd(r, k):
        c = cnt_ref[r]
        blocks = (c + SUB - 1) // SUB
        put(k, r, jnp.minimum(blocks, SLOTS // SUB) - 1, c)
        return k + lax.rem(blocks, 2)
    paired = lax.fori_loop(0, REL, pairs, 0)
    total = lax.fori_loop(0, REL, odd, paired)
    for extra in range(2 * NSUB):
        put(total + extra, 0, 0, 0)
    return paired // NSUB, (total + NSUB - 1) // NSUB


def rows_of(ref, lst_r, lst_o, c):
    pieces = []
    for k in range(NSUB):
        r, j = lst_r[c * NSUB + k], lst_o[c * NSUB + k]
        pair = ref[pl.ds(r, 1), pl.ds(pl.multiple_of(lax.div(j, 2) * 2 * SUB, 2 * SUB), 2 * SUB)]
        pieces.append(jnp.where(lax.rem(j, 2) == 0, pair[:, :SUB], pair[:, SUB:]))
    return jnp.concatenate(pieces, axis=1)


def place(c):
    return pl.ds(pl.multiple_of(c * EC, EC), EC)


LISTS = [pltpu.SMEM((REL * SLOTS // SUB + 2 * NSUB,), jnp.int32)] * 3


def pack_half_kernel(lay, type_ref, edge_ref, norm_hbm, mine_ref, buf, low, norm_ref, isem, osem):
    _, core, _ = position()
    norm = pltpu.make_async_copy(norm_hbm, norm_ref, isem.at[5])
    norm.start()
    rows = lay.half // 5
    for side in range(2):
        @pl.when(core == side)
        def _():
            loads = []
            for i in range(5):
                if side == 1 and i >= 3:
                    source, to = edge_ref.at[pl.ds((i - 3) * rows, rows)], buf.at[pl.ds(i * rows, rows), pl.ds(0, 768)]
                else:
                    source, to = type_ref.at[pl.ds(side * lay.half + i * rows, rows)], buf.at[pl.ds(i * rows, rows)]
                loads.append(pltpu.make_async_copy(source, to, isem.at[i]))
                loads[-1].start()
            norm.wait()
            if side == 1:
                corner = jnp.concatenate([norm_ref[...], jnp.zeros((8, 256 - lay.wide), f32)], axis=1)
                buf[3 * rows:, 768:] = jnp.concatenate([corner, jnp.zeros((lay.erows - 8, 256), f32)], axis=0)
            stores = []
            for i in range(5):
                loads[i].wait()
                at = slice(i * rows, (i + 1) * rows)
                low[at] = buf[at].astype(bf16)
                stores.append(pltpu.make_async_copy(low.at[pl.ds(i * rows, rows)], mine_ref.at[pl.ds(i * rows, rows)], osem.at[i]))
                stores[-1].start()
            for copy in stores:
                copy.wait()


def pack_half(lay, type_weight, edge_weight, norm_params):
    return pl.pallas_call(
        functools.partial(pack_half_kernel, lay),
        out_shape=S((lay.half, 1024), bf16),
        in_specs=[ANY] * 3,
        out_specs=ANY,
        scratch_shapes=[
            V((lay.half, 1024), f32), V((lay.half, 1024), bf16), V((8, lay.wide), f32),
            pltpu.SemaphoreType.DMA((6,)), pltpu.SemaphoreType.DMA((5,)),
        ],
        compiler_params=pltpu.CompilerParams(vmem_limit_bytes=63 * MIB),
        name="pack_half",
    )(type_weight, edge_weight, norm_params)


def pack_kernel(lay, type_ref, edge_ref, norm_ref, own_ref):
    own_ref[0:lay.trows, :] = type_ref[...].astype(bf16)
    own_ref[lay.trows:, 0:768] = edge_ref[...].astype(bf16)
    corner = jnp.concatenate([norm_ref[...], jnp.zeros((8, 256 - lay.wide), f32)], axis=1)
    own_ref[lay.trows:, 768:] = jnp.concatenate([corner, jnp.zeros((lay.erows - 8, 256), f32)], axis=0).astype(bf16)


def pack(lay, type_weight, edge_weight, norm_params):
    return pl.pallas_call(
        functools.partial(pack_kernel, lay),
        out_shape=S((lay.part, 1024), bf16),
        compiler_params=pltpu.CompilerParams(vmem_limit_bytes=63 * MIB),
        name="pack",
    )(type_weight, edge_weight, norm_params)


def before_kernel(cnt_ref, kinds_ref, src_ref, dst_ref, tim_ref, feat_ref, idx_ref, xg_ref, typ_ref, lst_r, lst_o, lst_c):
    _, chunks = list_blocks(cnt_ref, lst_r, lst_o, lst_c)
    src = src_ref[...]
    for j in range(SLOTS // 128):
        idx = src[:, j * 128:(j + 1) * 128]
        low = jnp.bitwise_and(idx, 127)
        high = jnp.right_shift(idx, 7)
        acc = jnp.zeros((8, 128), jnp.int32)
        for k in range(N // 128):
            row = jnp.broadcast_to(kinds_ref[:, k * 128:(k + 1) * 128], (8, 128))
            acc = jnp.where(high == k, jnp.take_along_axis(row, low, axis=1), acc)
        typ_ref[:, j * 128:(j + 1) * 128] = acc
    ft = nt(eye(), feat_ref[...]).astype(bf16)

    def one(c, _):
        src, dst, tim, typ = [rows_of(ref, lst_r, lst_o, c) for ref in (src_ref, dst_ref, tim_ref, typ_ref)]
        idx_ref[pl.ds(pl.multiple_of(c * 8, 8), 8), :] = jnp.concatenate(
            [src, dst, tim, typ, typ * 256 + tim, src, src, src], axis=0
        )
        xg_ref[:, place(c)] = nn(ft, one_hot_rows(src, N)).astype(bf16)
        return 0

    lax.fori_loop(0, chunks, one, 0)


def before(cnt, kinds, src, dst, tim, feat):
    return pl.pallas_call(
        before_kernel,
        out_shape=(S((EDGES // EC * 8, EC), jnp.int32), S((D, EDGES), bf16)),
        in_specs=[SMEM] + [VMEM] * 5,
        scratch_shapes=[V((REL, SLOTS), jnp.int32)] + LISTS,
        compiler_params=pltpu.CompilerParams(vmem_limit_bytes=63 * MIB),
        cost_estimate=pl.CostEstimate(flops=2 * D * N * EDGES, bytes_accessed=6 * MIB, transcendentals=0),
        name="before",
    )(cnt, kinds, src, dst, tim, feat)


def layer_kernel(lay, *refs):
    nb = lay.blocks - 1
    (
        live_ref, cnt_ref, kinds_hbm, mix_hbm, idx_hbm, emb_hbm, cot_hbm, feat_hbm, own_ref,
    ) = refs[:9]
    near, far, xg_hbm = refs[9:9 + nb], refs[9 + nb:9 + 2 * nb], refs[9 + 2 * nb]
    (
        out_ref, dqkv_ref, skp_ref, types_ref, keep_ref, send_ref,
        lst_r, lst_o, lst_c,
        wpk, gpack, gout, gnorm, gskip, xg, low, cot_ref, feat_ref, kinds_ref, mix_ref, idx_ref, emb_ref,
        wt, xcat, qt, rte, dn_buf, dkve_buf, mu,
        bda, bdat, bdm, bdmt, ga, gm, dmu,
        kve, qe, msg, wexp, raws,
        num, dnum, dqkv, dtkv, skp,
        wsem, xsem, osem, gsem,
    ) = refs[10 + 2 * nb:]
    me, core, zi = position()
    zi = lax.rem(zi, GROUP)
    small = [
        pltpu.make_async_copy(source, to, xsem.at[3 + i])
        for i, (source, to) in enumerate(
            ((kinds_hbm, kinds_ref), (mix_hbm, mix_ref), (feat_hbm, feat_ref), (idx_hbm, idx_ref), (emb_hbm, emb_ref))
        )
    ]
    weights = lay.weight_copies(me, core, own_ref, near, far, wpk, wsem)
    for copy in small + weights:
        copy.start()
    xg_copy = pltpu.make_async_copy(xg_hbm, xg, xsem.at[0])
    xg_copy.start()
    cot_copy = pltpu.make_async_copy(cot_hbm, cot_ref, xsem.at[2])

    ident = eye()
    whole, chunks = list_blocks(cnt_ref, lst_r, lst_o, lst_c)

    def row(c, k):
        return idx_ref[pl.ds(pl.multiple_of(c * 8, 8), 8), :][k:k + 1]

    for ref in (num, dqkv, dtkv, ga, gm, dmu, gnorm, gskip, gout):
        ref[...] = jnp.zeros_like(ref)
    dkve_buf[...] = jnp.zeros_like(dkve_buf)

    small[0].wait()
    small[1].wait()
    mix = jnp.broadcast_to(mix_ref[...].astype(bf16).astype(f32), (8, 68))
    lanes68 = lax.broadcasted_iota(jnp.int32, (8, 68), 1)
    line68 = lax.broadcasted_iota(jnp.int32, (8, 68), 0)

    def column(first):
        return jnp.sum(jnp.where(lanes68 == first + line68, mix, 0.0), axis=1, keepdims=True)

    for r in range(REL):
        mu[r] = jnp.broadcast_to(column(r * H) * score_scale, (H, 128))
    skip_col = column(REL * H)

    kinds = kinds_ref[...]
    masks = (lax.broadcasted_iota(jnp.int32, (8, N), 0) == kinds).astype(f32)
    small[2].wait()
    featt = nt(ident, feat_ref[...])
    for s in range(TYPES):
        xcat[s * D:(s + 1) * D, :] = (featt * masks[s:s + 1]).astype(bf16)
    for copy in weights + small[3:]:
        copy.wait()
    cot_copy.start()
    finish = [
        pltpu.make_async_copy(
            wpk.at[pl.ds(a, b - a), pl.ds(0, 3 * D)], types_ref.at[pl.ds(s * D + c, d - c)], osem.at[3 + f]
        )
        for s in range(TYPES) for f, a, b, c, d in lay.type_rows(s)
    ]
    for copy in finish:
        copy.start()

    lane = lax.broadcasted_iota(jnp.int32, (D, 128), 1)
    rowi = lax.broadcasted_iota(jnp.int32, (D, 128), 0)
    on_diag = (lane // DK) == (rowi // DK) % 4
    zeros = jnp.zeros((128, 128), f32)
    for p in range(4):
        x = lay.get_edge(wpk, p * 128, (p + 1) * 128).astype(f32)
        rolled = [x if k == 0 else pltpu.roll(x, 32 * k, 1) for k in range(4)]
        for g in range(4):
            r, m = 2 * p + g // 2, g % 2
            t = jnp.concatenate([rolled[(h % 4 - g) % 4][h * 32:(h + 1) * 32] for h in range(H)], axis=0)
            t = jnp.where(on_diag, t, 0.0)
            for ref, a, b in (
                (bdm if m else bda, t[:128], t[128:]), (bdmt if m else bdat, t[:128].T, t[128:].T)
            ):
                ref[r] = jnp.concatenate(
                    [jnp.concatenate([a, zeros], axis=1), jnp.concatenate([zeros, b], axis=1)], axis=0
                ).astype(bf16)

    for cb in range(4):
        for s in range(4):
            wt[cb * 256:(cb + 1) * 256, s * 256:(s + 1) * 256] = nt(
                ident, lay.get_type(wpk, s, cb * 256, (cb + 1) * 256)
            ).astype(bf16)
    qt[...] = nn(wt[:D, :], xcat[...]).astype(bf16)
    wet = nt(ident, lay.get_edge(wpk, 512, 768)).astype(bf16)
    rte[...] = nt(wet, emb_ref[...]).astype(bf16)

    def mu_of(c):
        return jnp.concatenate([mu[lst_r[c * NSUB + k]] for k in range(NSUB)], axis=1)

    def blocks_of(c, wide):
        return [(lst_r[c * NSUB + k * (wide // SUB)], slice(k * wide, (k + 1) * wide)) for k in range(EC // wide)]

    def lookup(c):
        rt = nn(rte[...], one_hot_rows(row(c, TIME), 256))
        return (xg[:, place(c)].astype(f32) + rt).astype(bf16)

    def lookup_q(c):
        qe[:, place(c)] = nn(qt[...], one_hot_rows(row(c, TARGET), N)).astype(bf16)

    def project(c, xe):
        cu = row(c, TYPE)
        zero = jnp.zeros((), bf16)
        xm = jnp.concatenate([jnp.where(cu == s, xe, zero) for s in range(TYPES)], axis=0)
        kve[:, place(c)] = nn(wt[D:3 * D, :], xm).astype(bf16)

    def forward(wide, c, _):
        at = place(c)
        kv_e = kve[:, at]
        q_e = qe[:, at].astype(f32)
        ks, ms = [], []
        for r, sl in blocks_of(c, wide):
            ks.append(nn(bdat[r], kv_e[:D, sl]))
            ms.append(nn(bdmt[r], kv_e[D:, sl]))
        ka = jnp.concatenate(ks, axis=1)
        me_ = jnp.concatenate(ms, axis=1)
        xe = lookup(c + 1)
        xg[:, at] = ka.astype(bf16)
        msg[:, at] = me_.astype(bf16)
        raw = head_sum(ka * q_e)
        raws[:, at] = raw
        lanes = lax.broadcasted_iota(jnp.int32, (H, SUB), 1)
        w = jnp.exp(raw * mu_of(c))
        w = jnp.concatenate(
            [jnp.where(lanes < lst_c[c * NSUB + k], w[:, k * SUB:(k + 1) * SUB], 0.0) for k in range(NSUB)], axis=1
        )
        wexp[:, at] = w
        wm = (head_wide(w) * me_).astype(bf16)
        lookup_q(c + 1)
        num[...] += nt(jnp.concatenate([wm, hi_lo(w)], axis=0), one_hot_rows(row(c, TARGET), N))
        project(c + 1, xe)
        return 0

    xg_copy.wait()
    project(0, lookup(0))
    lookup_q(0)
    lax.fori_loop(0, whole, functools.partial(forward, 2 * SUB), 0)
    lax.fori_loop(whole, chunks, functools.partial(forward, SUB), 0)

    cot_copy.wait()
    nwt = nt(ident, lay.get_norm(wpk)).astype(bf16)
    out_rows = jnp.concatenate([lay.get_type(wpk, s, 3 * D, 4 * D) for s in range(TYPES)], axis=1)

    def nodes(c):
        at = pl.ds(pl.multiple_of(c * NC, NC), NC)
        mk = (lax.broadcasted_iota(jnp.int32, (8, NC), 0) == kinds_ref[:, at]).astype(f32)
        live = (lax.broadcasted_iota(jnp.int32, (1, NC), 1) + c * NC < live_ref[0]).astype(f32)
        den = num[D:D + H, at] + num[D + H:, at] + (1.0 - live)
        inv_den = head_wide(1.0 / den)
        agg = num[:D, at] * inv_den
        phi = 0.5 * (1.0 + lax.erf(agg * (0.5 ** 0.5)))
        act = (agg * phi).astype(bf16)
        mkl = mk.astype(bf16)
        acat = jnp.concatenate([act * mkl[s:s + 1] for s in range(TYPES)], axis=0)
        yield
        trans = nn(wt[3 * D:, :], acat)
        yield
        alpha = 1.0 / (1.0 + jnp.exp(-jnp.sum(mk * skip_col, axis=0, keepdims=True)))
        ft = nt(ident, feat_ref[at, :])
        none = jnp.zeros((4, NC), f32)
        oh16 = jnp.concatenate([mk[0:4], none, none, none], axis=0).astype(bf16)
        gain = nn(nwt, oh16)
        bias = nn(nwt, jnp.concatenate([none, mk[0:4], none, none], axis=0).astype(bf16))
        dy = live * nt(ident, cot_ref[at, :])
        res = alpha * trans + (1.0 - alpha) * ft
        mean = jnp.mean(res, axis=0, keepdims=True)
        cen = res - mean
        inv = lax.rsqrt(jnp.mean(cen * cen, axis=0, keepdims=True) + norm_eps)
        nrm = cen * inv
        cot_ref[at, :] = (live * (nrm * gain + bias)).T.astype(bf16)
        dyn = dy * nrm
        dyn_hi = dyn.astype(bf16)
        dyn_lo = (dyn - dyn_hi.astype(f32)).astype(bf16)
        gnorm[0:4, :] += (nt(oh16, dyn_hi) + nt(oh16, dyn_lo))[0:4]
        gnorm[4:8, :] += nt(oh16, dy.astype(bf16))[0:4]
        dn = dy * gain
        dres = inv * (dn - jnp.mean(dn, axis=0, keepdims=True) - nrm * jnp.mean(dn * nrm, axis=0, keepdims=True))
        dtr = (alpha * dres).astype(bf16)
        yield
        dact = nn(out_rows, jnp.concatenate([dtr * mkl[s:s + 1] for s in range(TYPES)], axis=0))
        yield
        skp[:, at] = (1.0 - alpha) * dres
        dal = jnp.sum(dres * (trans - ft), axis=0, keepdims=True) * alpha * (1.0 - alpha)
        gskip[...] += jnp.broadcast_to(jnp.sum(mk * dal, axis=1, keepdims=True), (8, 128))
        gout[...] += nt(acat, dtr)
        dagg = dact * (phi + agg * (jnp.exp(-0.5 * agg * agg) * (0.5 / np.pi) ** 0.5))
        dnum[0:D, at] = (dagg * inv_den).astype(bf16)
        dnum[D:, at] = hi_lo(-head_sum(dagg * agg) / den)
        yield

    def node_steps(c, _):
        for _ in zip(*[nodes(NODE_STEPS * c + i) for i in range(NODE_STEPS)]):
            pass
        return 0

    lax.fori_loop(0, N // NC // NODE_STEPS, node_steps, 0)
    for i, (source, to) in enumerate(((cot_ref, out_ref), (skp, skp_ref))):
        finish.append(pltpu.make_async_copy(source, to, osem.at[i]))
        finish[-1].start()

    def gather_back(c):
        dn_buf[...] = nn(dnum[...], one_hot_rows(row(c, TARGET), N))

    def scatter_back(c):
        dkve = dkve_buf[...]
        dqkv[:, D:] += nt(one_hot_rows(row(c, SOURCE), N), dkve)
        dtkv[...] += nt(one_hot_rows(row(c, BUCKET), 1024), dkve)

    def backward(wide, c, _):
        at = place(c)
        scatter_back(jnp.maximum(c - 1, 0))
        dn_e = dn_buf[:D]
        w = wexp[:, at]
        dw = head_sum(dn_e * msg[:, at].astype(f32)) + dn_buf[D:D + H] + dn_buf[D + H:]
        ds = dw * w
        dsr = ds * raws[:, at]
        ss = head_wide(ds * mu_of(c))
        dka = (ss * qe[:, at].astype(f32)).astype(bf16)
        dms = (head_wide(w) * dn_e).astype(bf16)
        dqe = (ss * xg[:, at].astype(f32)).astype(bf16)
        gather_back(c + 1)
        for r, sl in blocks_of(c, wide):
            dkve_buf[0:D, sl] = nn(bda[r], dka[:, sl]).astype(bf16)
            dkve_buf[D:, sl] = nn(bdm[r], dms[:, sl]).astype(bf16)
        for r, sl in blocks_of(c, wide):
            at_k = pl.ds(pl.multiple_of(c * EC + sl.start, SUB), wide)
            gak = nt(kve[0:D, at_k], dka[:, sl])
            gmk = nt(kve[D:, at_k], dms[:, sl])
            ga[r, 0:128] += gak[0:128, 0:128]
            ga[r, 128:] += gak[128:, 128:]
            gm[r, 0:128] += gmk[0:128, 0:128]
            gm[r, 128:] += gmk[128:, 128:]
            dmu[r] += sum(dsr[:, k:k + 128] for k in range(sl.start, sl.stop, 128))
        dqkv[:, :D] += nt(one_hot_rows(row(c, TARGET), N), dqe)
        return 0

    gather_back(0)
    def backward_pair(c, _):
        backward(2 * SUB, 2 * c, 0)
        backward(2 * SUB, 2 * c + 1, 0)
        return 0

    lax.fori_loop(0, whole // 2, backward_pair, 0)
    lax.fori_loop(whole // 2 * 2, whole, functools.partial(backward, 2 * SUB), 0)
    lax.fori_loop(whole, chunks, functools.partial(backward, SUB), 0)
    scatter_back(chunks - 1)

    low[...] = dqkv[...].astype(bf16)
    last = pltpu.make_async_copy(low, dqkv_ref, osem.at[2])
    last.start()
    finish.append(last)
    dt = dtkv[...].astype(bf16)
    drte = jnp.zeros((D, 256), f32)
    for s in range(TYPES):
        drte = drte + nt(lay.get_type(wpk, s, D, 3 * D), dt[s * 256:(s + 1) * 256, :])

    spots = [jnp.bitwise_xor(zi, j) for j in range(GROUP)]

    def put_edge(c0, value):
        lanes = slice(c0 % WIDE, c0 % WIDE + value.shape[1])
        for f in range(lay.blocks):
            gpack[spots[c0 // WIDE], f * lay.part + lay.trows:(f + 1) * lay.part, lanes] = value[
                f * lay.erows:(f + 1) * lay.erows
            ].astype(bf16)

    for p in range(4):
        acc = jnp.zeros((D, 128), f32)
        for g in range(4):
            r, m = 2 * p + g // 2, g % 2
            t = jnp.where(on_diag, (gm if m else ga)[r], 0.0)
            rolled = [t if k == 0 else pltpu.roll(t, 32 * k, 1) for k in range(4)]
            acc = acc + jnp.concatenate([rolled[(g - h % 4) % 4][h * 32:(h + 1) * 32] for h in range(H)], axis=0)
        put_edge(p * 128, acc)
    embt = nt(ident, emb_ref[...]).astype(bf16)
    put_edge(512, nt(embt, drte.astype(bf16)))

    lane8 = lax.broadcasted_iota(jnp.int32, (8, 256), 1)
    line8 = lax.broadcasted_iota(jnp.int32, (8, 256), 0)
    mixg = jnp.where(lane8 == REL * H + line8, gskip[:, 0:1], 0.0)
    for r in range(REL):
        col = jnp.sum(dmu[r], axis=1, keepdims=True) * score_scale
        mixg = mixg + jnp.where(lane8 == r * H + line8, col, 0.0)
    mixg = jnp.broadcast_to(jnp.sum(mixg, axis=0, keepdims=True), (8, 256))
    for f in range(lay.blocks):
        corner = jnp.concatenate(
            [gnorm[:, f * lay.wide:(f + 1) * lay.wide], jnp.zeros((8, 256 - lay.wide), f32)], axis=1
        )
        small = jnp.concatenate([corner, mixg, jnp.zeros((lay.erows - 16, 256), f32)], axis=0)
        gpack[spots[3], f * lay.part + lay.trows:(f + 1) * lay.part, :] = small.astype(bf16)

    done = 0
    for s in range(TYPES):
        g = nn(xcat[s * D:(s + 1) * D, :], low[...])
        g_kv = g[:, D:] + nn(rte[...], dt[s * 256:(s + 1) * 256, :])
        values = [g[:, :D], g_kv[:, :D], g_kv[:, D:], gout[s * D:(s + 1) * D, :]]
        for _, a, b, c, d in lay.type_rows(s):
            for j in range(GROUP):
                gpack[spots[j], a:b, :] = values[j][c:d].astype(bf16)
        while done < lay.blocks and (done + 1) * lay.trows <= (s + 1) * D:
            m = jnp.bitwise_xor(me, done)
            for i, (ref, side) in enumerate(((send_ref, 1 - core), (keep_ref, core))):
                at = pl.ds(pl.multiple_of(done * lay.part + side * lay.half, 16), lay.half)
                copy = pltpu.make_async_copy(gpack.at[:, at], ref.at[m], gsem.at[2 * done + i])
                copy.start()
                finish.append(copy)
            done += 1
    for copy in finish:
        copy.wait()


def emb_table():
    steps = np.arange(TB, dtype=np.float32)[:, None]
    col = np.arange(D)
    freq = np.exp(-np.log(np.float32(10000.0)) * (2 * (col // 2)).astype(np.float32) / np.float32(D)).astype(np.float32)
    angle = steps * freq[None]
    tab = np.where(col[None] % 2 == 0, np.sin(angle), np.cos(angle)).astype(np.float32)
    return np.concatenate([tab, np.zeros((256 - TB, D), np.float32)], axis=0)


def layer(lay, live, cnt, kinds, mix, idx, cot, feat, own, near, far, xg):
    sums = S((lay.blocks, GROUP, lay.half, WIDE), bf16)
    edges = lambda rows, kind: V((rows, EDGES), kind)
    return pl.pallas_call(
        functools.partial(layer_kernel, lay),
        out_shape=[S((N, D), bf16), S((N, 3 * D), bf16), S((D, N), f32), S((TYPES * D, 3 * D), bf16), sums, sums],
        in_specs=[SMEM, SMEM] + [ANY] * (2 * lay.blocks + 6),
        out_specs=[ANY] * 6,
        scratch_shapes=LISTS + [
            V((lay.blocks * lay.part, 1024), bf16), V((GROUP, lay.blocks * lay.part, WIDE), bf16), V((TYPES * D, D), f32),
            V((8, D), f32), V((8, 128), f32), edges(D, bf16), V((N, 3 * D), bf16), V((N, D), bf16), V((N, D), bf16),
            V(kinds.shape, jnp.int32), V(mix.shape, f32), V(idx.shape, jnp.int32), V((256, D), bf16),
            V((4 * D, TYPES * D), bf16), V((TYPES * D, N), bf16), V((D, N), bf16), V((D, 256), bf16),
            V((D + 16, EC), f32), V((2 * D, EC), bf16), V((REL, H, 128), f32),
            V((8, D, D), bf16), V((8, D, D), bf16), V((8, D, D), bf16), V((8, D, D), bf16),
            V((8, D, 128), f32), V((8, D, 128), f32), V((8, 8, 128), f32),
            edges(2 * D, bf16), edges(D, bf16), V((D, REL * SLOTS), bf16),
            V((H, REL * SLOTS), f32), V((H, REL * SLOTS), f32),
            V((D + 16, N), f32), V((D + 16, N), bf16), V((N, 3 * D), f32), V((TYPES * 256, 2 * D), f32), V((D, N), f32),
            pltpu.SemaphoreType.DMA((2 * lay.blocks - 1,)), pltpu.SemaphoreType.DMA((8,)),
            pltpu.SemaphoreType.DMA((3 + lay.blocks,)), pltpu.SemaphoreType.DMA((2 * lay.blocks,)),
        ],
        compiler_params=pltpu.CompilerParams(vmem_limit_bytes=LAYER_VMEM),
        cost_estimate=pl.CostEstimate(flops=60 * 10**9, bytes_accessed=16 * MIB, transcendentals=0),
        name="layer",
    )(live, cnt, kinds, mix, idx, jnp.asarray(emb_table(), bf16), cot, feat, own, *near, *far, xg)


def input_kernel(kinds_ref, dqkv_ref, skp_ref, types_ref, out_ref):
    masks = (lax.broadcasted_iota(jnp.int32, (8, N), 0) == kinds_ref[...]).astype(f32)
    for c in range(N // NC):
        at = slice(c * NC, (c + 1) * NC)
        proj = pick(masks[:, at], [nt(types_ref[s * D:(s + 1) * D, :], dqkv_ref[at, :]) for s in range(TYPES)])
        out_ref[at, :] = (proj + skp_ref[:, at]).T.astype(bf16)


def input_gradient(kinds, dqkv, skp, types):
    return pl.pallas_call(
        input_kernel,
        out_shape=S((N, D), bf16),
        compiler_params=pltpu.CompilerParams(vmem_limit_bytes=INPUT_VMEM),
        cost_estimate=pl.CostEstimate(flops=2 * N * D * D * 12, bytes_accessed=6 * MIB, transcendentals=0),
        name="input_gradient",
    )(kinds, dqkv, skp, types)


def tree(terms):
    while len(terms) > 1:
        terms = [terms[i] + terms[i + 1] for i in range(0, len(terms), 2)]
    return terms[0]


def add_core_kernel(lay, keep_ref, got_ref, *refs):
    ways = ((lay.blocks, lambda ref, m: ref.at[m, :, pl.ds(0, lay.first)]),
            (GROUP, lambda ref, m: ref.at[:, m, pl.ds(lay.first, lay.second)]))
    jobs = [(way, m) for way in range(2) for m in range(1, ways[way][0])] + [(0, 0), (1, 0)]
    outs, bufs, isem, osem = refs[:len(jobs)], refs[len(jobs):-2], *refs[-2:]
    loads = []
    for k, (way, m) in enumerate(jobs):
        pair = [
            pltpu.make_async_copy(ways[way][1](source, m), bufs[2 * way + i].at[m], isem.at[2 * k + i])
            for i, source in enumerate((keep_ref, got_ref))
        ]
        for copy in pair:
            copy.start()
        loads.append(pair)
    stores = []
    for k, (way, m) in enumerate(jobs):
        for copy in loads[k]:
            copy.wait()
        keep, got = bufs[2 * way], bufs[2 * way + 1]
        keep[m] = (keep[m].astype(f32) + got[m].astype(f32)).astype(bf16)
        stores.append(pltpu.make_async_copy(keep.at[m], outs[k], osem.at[k]))
        stores[-1].start()
    for copy in stores:
        copy.wait()


def add_core(lay, keep, got):
    shapes = [(lay.blocks, GROUP, lay.first, WIDE)] * 2 + [(GROUP, lay.blocks, lay.second, WIDE)] * 2
    out_shape = [S(shape[1:], bf16) for shape in shapes[::2] for _ in range(shape[0] - 1)] + [S(shape[1:], bf16) for shape in shapes[::2]]
    outs = pl.pallas_call(
        functools.partial(add_core_kernel, lay),
        out_shape=out_shape,
        in_specs=[ANY] * 2,
        out_specs=[ANY] * len(out_shape),
        scratch_shapes=[V(shape, bf16) for shape in shapes]
        + [pltpu.SemaphoreType.DMA((2 * len(out_shape),)), pltpu.SemaphoreType.DMA((len(out_shape),))],
        compiler_params=pltpu.CompilerParams(vmem_limit_bytes=63 * MIB),
        name="add_core",
    )(keep, got)
    return [outs[-2], *outs[:lay.blocks - 1]], [outs[-1], *outs[lay.blocks - 1:-2]]


def summed(terms):
    return tree([x.astype(f32) for x in terms]).astype(bf16)


def adam(param, first, second, avg, grad, rate):
    root = (1.0 - beta_two**STEP) ** 0.5
    first_new = beta_one * first + (1.0 - beta_one) * grad
    second_new = beta_two * second + (1.0 - beta_two) * (grad * grad)
    below = jnp.sqrt(second_new) + adam_eps * root
    guess = pl.reciprocal(below, approx=True)
    guess = guess * (2.0 - below * guess)
    param_new = (1.0 - rate * decay_rate) * param - (rate * root / (1.0 - beta_one**STEP)) * (first_new * guess)
    avg_new = ema_keep * avg + (1.0 - ema_keep) * param_new
    return (param_new, first_new, second_new, avg_new)


def update_kernel(jobs, count, *refs):
    pieces, refs = refs[:2 * GROUP], refs[2 * GROUP:]
    states, outs, refs = refs[:count], refs[count:2 * count], refs[2 * count:]
    gsum, bufs, news, isem, osem = refs[0], refs[1:1 + 4 * len(jobs)], refs[1 + 4 * len(jobs):-2], refs[-2], refs[-1]

    def view(ref, row, rows):
        return ref if rows == ref.shape[0] else ref.at[pl.ds(row, rows)]

    loads = [
        pltpu.make_async_copy(view(states[4 * job[0] + j], job[1], job[2]), bufs[4 * i + j], isem.at[4 * i + j])
        for i, job in enumerate(jobs) for j in range(4)
    ]
    for copy in loads:
        copy.start()
    _, core, zi = position()
    zi = lax.rem(zi, GROUP)
    high = gsum.shape[0] // 2
    for side in range(2):
        at = pl.ds(pl.multiple_of(jnp.bitwise_xor(core, side) * high, 16), high)
        for k in range(GROUP):
            want = jnp.bitwise_xor(zi, k)
            for j in range(GROUP):
                @pl.when(want == j)
                def _():
                    gsum[at, j * WIDE:(j + 1) * WIDE] = pieces[side * GROUP + k][...]
    stores = []
    for i, (group, row, rows, lanes, first, lane, rate) in enumerate(jobs):
        base = first // 16 * 16
        grad = gsum[base:base + max(16, rows), lane:lane + max(lanes, 128)].astype(f32)
        grad = grad[first - base:first - base + rows, :lanes]
        for j in range(4):
            loads[4 * i + j].wait()
        new = adam(*[bufs[4 * i + j][...] for j in range(4)], grad, rate)
        for j in range(4):
            news[4 * i + j][...] = new[j]
            copy = pltpu.make_async_copy(news[4 * i + j], view(outs[4 * group + j], row, rows), osem.at[4 * i + j])
            copy.start()
            stores.append(copy)
    for copy in stores:
        copy.wait()


def update(jobs, pieces, sets):
    states = [x for group in sets for x in group]
    bufs = [V((job[2], job[3]), f32) for job in jobs for _ in range(4)]
    return pl.pallas_call(
        functools.partial(update_kernel, jobs, len(states)),
        out_shape=[S(x.shape, f32) for x in states],
        in_specs=[VMEM] * len(pieces) + [ANY] * len(states),
        out_specs=[ANY] * len(states),
        scratch_shapes=[V((2 * pieces[0].shape[0], 1024), bf16)] + bufs + bufs
        + [pltpu.SemaphoreType.DMA((len(bufs),))] * 2,
        compiler_params=pltpu.CompilerParams(vmem_limit_bytes=63 * MIB),
        name="update",
    )(*pieces, *states)


def shards(dp, fsdp, *args):
    (
        node_feat, out_cot, node_type, node_count, edge_src, edge_dst, edge_time, edge_count,
        type_weight, type_first, type_second, type_avg,
        edge_weight, edge_first, edge_second, edge_avg,
        norm_params, norm_first, norm_second, norm_avg,
        mix_params, mix_first, mix_second, mix_avg,
    ) = args
    lines = dp // 2
    lay = Layout(fsdp)

    def swap(x, axis, mask):
        size = dp if axis == "dp" else fsdp
        return lax.ppermute(x, axis, [(i, i ^ mask) for i in range(size)])

    mine = pack_half(lay, type_weight, edge_weight, norm_params)
    near = [swap(mine, "fsdp", m) for m in range(1, fsdp)]
    kinds = node_type.reshape(1, N)
    own = pack(lay, type_weight, edge_weight, norm_params)
    idx, xg = before(edge_count, kinds, edge_src, edge_dst, edge_time, node_feat)
    own, idx, xg, near[0] = lax.optimization_barrier((own, idx, xg, near[0]))
    far = [swap(x, "dp", 1) for x in near]
    mixes = [x.reshape(1, 68) for x in (mix_params, mix_first, mix_second, mix_avg)]
    layer_out, dqkv, skp, types, keep, send = layer(
        lay, node_count, edge_count, kinds, mixes[0], idx, out_cot, node_feat,
        own, near, far, xg,
    )
    got = swap(send, "dp", 1)
    chip_a, chip_b = add_core(lay, keep, got)
    dqkv, *chip_a = lax.optimization_barrier((dqkv, *chip_a))
    part_a = [chip_a[0]] + [swap(chip_a[m], "fsdp", m) for m in range(1, fsdp)]
    part_b = [chip_b[0]] + [swap(chip_b[k], "dp", 2 * k) for k in range(1, GROUP)]
    input_grad = input_gradient(kinds, dqkv, skp, types)
    input_grad, *part_a = lax.optimization_barrier((input_grad, *part_a))
    piece_a = [summed([x[k] for x in part_a]) for k in range(GROUP)]
    piece_b = [summed([x[m] for x in part_b]) for m in range(fsdp)]
    total_a = summed([piece_a[0]] + [swap(piece_a[k], "dp", 2 * k) for k in range(1, GROUP)])
    total_b = summed([piece_b[0]] + [swap(piece_b[m], "fsdp", m) for m in range(1, fsdp)])
    total = jnp.concatenate([total_a, total_b], axis=0)
    step = GROUP
    while step < lines:
        total = summed([total, swap(total, "dp", 2 * step)])
        step *= 2
    totals = [total] + [swap(total, "dp", 2 * k) for k in range(1, GROUP)]
    totals = totals + [swap(x, "dp", 1) for x in totals]
    trows, erows = lay.trows, lay.erows
    jobs = [(0, row, erows, 1024, row, 0, rates[0]) for row in range(0, trows, erows)] + [
        (1, 0, erows, 768, trows, 0, rates[1]), (2, 0, 8, lay.wide, trows, 768, rates[2]),
        (3, 0, 1, 68, trows + 8, 768, rates[3]),
    ]
    new = update(jobs, totals, [
        [type_weight, type_first, type_second, type_avg], [edge_weight, edge_first, edge_second, edge_avg],
        [norm_params, norm_first, norm_second, norm_avg], mixes,
    ])
    return (layer_out, input_grad, *new[:12], *[x.reshape(68) for x in new[12:]])


def solution(mesh):
    whole = P(("dp", "fsdp"), None)
    flat = P(("dp", "fsdp"))
    state = [P("fsdp", None)] * 8 + [P(None, "fsdp")] * 4 + [P()] * 4
    return jax.shard_map(
        functools.partial(shards, mesh.shape["dp"], mesh.shape["fsdp"]),
        mesh=mesh,
        in_specs=tuple([whole, whole, flat, flat, whole, whole, whole, flat] + state),
        out_specs=tuple([whole, whole] + state),
        check_vma=False,
    )
```

```python
import functools

import jax
import jax.numpy as jnp
import numpy as np
from jax import lax
from jax.experimental import pallas as pl
from jax.experimental.pallas import tpu as pltpu
from jax.sharding import PartitionSpec as P

D, H, DK, TYPES, REL, TB = 256, 8, 32, 4, 8, 240
N = 1024
SLOTS = 1024
EC = 512
SUB = 128
NSUB = EC // SUB
NC = 256
NODE_STEPS = 4
EDGES = REL * SLOTS
bf16 = jnp.bfloat16
f32 = jnp.float32
norm_eps = 1e-5
STEP = 10
beta_one = 0.9
beta_two = 0.999
adam_eps = 1e-08
decay_rate = 0.01
ema_keep = 0.7
rates = (0.2, 0.2, 0.6, 0.6)
score_scale = DK ** (-0.5)

SMEM = pl.BlockSpec(memory_space=pltpu.SMEM)
VMEM = pl.BlockSpec(memory_space=pltpu.VMEM)
ANY = pl.BlockSpec(memory_space=pl.ANY)
S = jax.ShapeDtypeStruct
V = pltpu.VMEM
MIB = 1 << 20
INPUT_VMEM = 62 * MIB
SECOND = 3
SOURCE, TARGET, TIME, TYPE, BUCKET = range(5)
LAYER_VMEM = 63 * MIB
GROUP = 4
WIDE = 1024 // GROUP


def nn(a, b):
    return jnp.dot(a, b, preferred_element_type=f32)


def nt(a, b):
    return lax.dot_general(a, b, (((1,), (1,)), ((), ())), preferred_element_type=f32)


def one_hot_rows(row, count):
    wide = row.shape[1]
    base = lax.broadcasted_iota(jnp.int16, (256, wide), 0)
    one, zero = jnp.ones((), bf16), jnp.zeros((), bf16)
    return jnp.concatenate(
        [jnp.where(base == (row - 256 * g).astype(jnp.int16), one, zero) for g in range(count // 256)], axis=0
    )


def head_sum(x):
    return jnp.sum(x.reshape(H, DK, x.shape[1]), axis=1)


def head_wide(x):
    return jnp.broadcast_to(x[:, None, :], (H, DK, x.shape[1])).reshape(D, x.shape[1])


def hi_lo(x):
    high = x.astype(bf16).astype(f32)
    return jnp.concatenate([high, x - high], axis=0).astype(bf16)


def eye():
    return (
        lax.broadcasted_iota(jnp.int32, (256, 256), 0) == lax.broadcasted_iota(jnp.int32, (256, 256), 1)
    ).astype(f32).astype(bf16)


def pick(masks, wide):
    out = wide[0] * masks[0:1]
    for s in range(1, TYPES):
        out = jnp.where(masks[s:s + 1] > 0, wide[s], out)
    return out


def stack(pieces):
    return pieces[0] if len(pieces) == 1 else jnp.concatenate(pieces, axis=0)


class Layout:
    def __init__(self, blocks):
        self.blocks = blocks
        self.trows, self.erows = TYPES * D // blocks, D // blocks
        self.part = self.trows + self.erows
        self.half = self.part // 2
        self.wide = D // blocks
        self.second = self.half * SECOND // 10 // 16 * 16
        self.first = self.half - self.second

    def type_rows(self, s):
        for f in range(self.blocks):
            a, b = max(s * D, f * self.trows), min((s + 1) * D, (f + 1) * self.trows)
            if a < b:
                yield f, f * self.part + a - f * self.trows, f * self.part + b - f * self.trows, a - s * D, b - s * D

    def get_type(self, ref, s, c0, c1):
        return stack([ref[a:b, c0:c1] for _, a, b, _, _ in self.type_rows(s)])

    def get_edge(self, ref, c0, c1):
        return stack([ref[f * self.part + self.trows:(f + 1) * self.part, c0:c1] for f in range(self.blocks)])

    def get_norm(self, ref):
        rows = [f * self.part + self.trows for f in range(self.blocks)]
        return jnp.concatenate([ref[a:a + 16, 768:768 + self.wide].astype(f32) for a in rows], axis=1).astype(bf16)

    def weight_copies(self, me, core, own, near, far, wpk, sems):
        out = [pltpu.make_async_copy(own, wpk.at[pl.ds(pl.multiple_of(me * self.part, 16), self.part)], sems.at[0])]
        for m in range(1, self.blocks):
            base = jnp.bitwise_xor(me, m) * self.part
            for i, (ref, side) in enumerate(((near[m - 1], core), (far[m - 1], 1 - core))):
                at = pl.ds(pl.multiple_of(base + side * self.half, 16), self.half)
                out.append(pltpu.make_async_copy(ref, wpk.at[at], sems.at[2 * m - 1 + i]))
        return out


def position():
    return lax.axis_index("fsdp"), lax.rem(lax.axis_index("dp"), 2), lax.div(lax.axis_index("dp"), 2)


def list_blocks(cnt_ref, lst_r, lst_o, lst_c):
    def put(k, r, j, c):
        lst_r[k] = r
        lst_o[k] = j
        lst_c[k] = c - j * SUB

    def pairs(r, k):
        c = cnt_ref[r]

        def one(j, k):
            put(k, r, 2 * j, c)
            put(k + 1, r, 2 * j + 1, c)
            return k + 2
        return lax.fori_loop(0, (c + SUB - 1) // SUB // 2, one, k)

    def odd(r, k):
        c = cnt_ref[r]
        blocks = (c + SUB - 1) // SUB
        put(k, r, jnp.minimum(blocks, SLOTS // SUB) - 1, c)
        return k + lax.rem(blocks, 2)
    paired = lax.fori_loop(0, REL, pairs, 0)
    total = lax.fori_loop(0, REL, odd, paired)
    for extra in range(2 * NSUB):
        put(total + extra, 0, 0, 0)
    return paired // NSUB, (total + NSUB - 1) // NSUB, total


def rows_of(ref, lst_r, lst_o, c):
    pieces = []
    for k in range(NSUB):
        r, j = lst_r[c * NSUB + k], lst_o[c * NSUB + k]
        pair = ref[pl.ds(r, 1), pl.ds(pl.multiple_of(lax.div(j, 2) * 2 * SUB, 2 * SUB), 2 * SUB)]
        pieces.append(jnp.where(lax.rem(j, 2) == 0, pair[:, :SUB], pair[:, SUB:]))
    return jnp.concatenate(pieces, axis=1)


def place(c, span=EC):
    return pl.ds(pl.multiple_of(c * EC, EC), span)


LISTS = [pltpu.SMEM((REL * SLOTS // SUB + 2 * NSUB,), jnp.int32)] * 3


def pack_half_kernel(lay, type_ref, edge_ref, norm_hbm, mine_ref, buf, low, norm_ref, isem, osem):
    _, core, _ = position()
    norm = pltpu.make_async_copy(norm_hbm, norm_ref, isem.at[5])
    norm.start()
    rows = lay.half // 5
    for side in range(2):
        @pl.when(core == side)
        def _():
            loads = []
            for i in range(5):
                if side == 1 and i >= 3:
                    source, to = edge_ref.at[pl.ds((i - 3) * rows, rows)], buf.at[pl.ds(i * rows, rows), pl.ds(0, 768)]
                else:
                    source, to = type_ref.at[pl.ds(side * lay.half + i * rows, rows)], buf.at[pl.ds(i * rows, rows)]
                loads.append(pltpu.make_async_copy(source, to, isem.at[i]))
                loads[-1].start()
            norm.wait()
            if side == 1:
                corner = jnp.concatenate([norm_ref[...], jnp.zeros((8, 256 - lay.wide), f32)], axis=1)
                buf[3 * rows:, 768:] = jnp.concatenate([corner, jnp.zeros((lay.erows - 8, 256), f32)], axis=0)
            stores = []
            for i in range(5):
                loads[i].wait()
                at = slice(i * rows, (i + 1) * rows)
                low[at] = buf[at].astype(bf16)
                stores.append(pltpu.make_async_copy(low.at[pl.ds(i * rows, rows)], mine_ref.at[pl.ds(i * rows, rows)], osem.at[i]))
                stores[-1].start()
            for copy in stores:
                copy.wait()


def pack_half(lay, type_weight, edge_weight, norm_params):
    return pl.pallas_call(
        functools.partial(pack_half_kernel, lay),
        out_shape=S((lay.half, 1024), bf16),
        in_specs=[ANY] * 3,
        out_specs=ANY,
        scratch_shapes=[
            V((lay.half, 1024), f32), V((lay.half, 1024), bf16), V((8, lay.wide), f32),
            pltpu.SemaphoreType.DMA((6,)), pltpu.SemaphoreType.DMA((5,)),
        ],
        compiler_params=pltpu.CompilerParams(vmem_limit_bytes=63 * MIB),
        name="pack_half",
    )(type_weight, edge_weight, norm_params)


def pack_kernel(lay, type_ref, edge_ref, norm_ref, own_ref):
    own_ref[0:lay.trows, :] = type_ref[...].astype(bf16)
    own_ref[lay.trows:, 0:768] = edge_ref[...].astype(bf16)
    corner = jnp.concatenate([norm_ref[...], jnp.zeros((8, 256 - lay.wide), f32)], axis=1)
    own_ref[lay.trows:, 768:] = jnp.concatenate([corner, jnp.zeros((lay.erows - 8, 256), f32)], axis=0).astype(bf16)


def pack(lay, type_weight, edge_weight, norm_params):
    return pl.pallas_call(
        functools.partial(pack_kernel, lay),
        out_shape=S((lay.part, 1024), bf16),
        compiler_params=pltpu.CompilerParams(vmem_limit_bytes=63 * MIB),
        name="pack",
    )(type_weight, edge_weight, norm_params)


def before_kernel(cnt_ref, kinds_ref, src_ref, dst_ref, tim_ref, feat_ref, idx_ref, xg_ref, typ_ref, lst_r, lst_o, lst_c):
    _, chunks, _ = list_blocks(cnt_ref, lst_r, lst_o, lst_c)
    src = src_ref[...]
    for j in range(SLOTS // 128):
        idx = src[:, j * 128:(j + 1) * 128]
        low = jnp.bitwise_and(idx, 127)
        high = jnp.right_shift(idx, 7)
        acc = jnp.zeros((8, 128), jnp.int32)
        for k in range(N // 128):
            row = jnp.broadcast_to(kinds_ref[:, k * 128:(k + 1) * 128], (8, 128))
            acc = jnp.where(high == k, jnp.take_along_axis(row, low, axis=1), acc)
        typ_ref[:, j * 128:(j + 1) * 128] = acc
    ft = nt(eye(), feat_ref[...]).astype(bf16)

    def one(c, _):
        src, dst, tim, typ = [rows_of(ref, lst_r, lst_o, c) for ref in (src_ref, dst_ref, tim_ref, typ_ref)]
        idx_ref[pl.ds(pl.multiple_of(c * 8, 8), 8), :] = jnp.concatenate(
            [src, dst, tim, typ, typ * 256 + tim, src, src, src], axis=0
        )
        xg_ref[:, place(c)] = nn(ft, one_hot_rows(src, N)).astype(bf16)
        return 0

    def two(c, _):
        one(2 * c, 0)
        one(2 * c + 1, 0)
        return 0

    lax.fori_loop(0, (chunks + 1) // 2, two, 0)


def before(cnt, kinds, src, dst, tim, feat):
    return pl.pallas_call(
        before_kernel,
        out_shape=(S((EDGES // EC * 8, EC), jnp.int32), S((D, EDGES), bf16)),
        in_specs=[SMEM] + [VMEM] * 5,
        scratch_shapes=[V((REL, SLOTS), jnp.int32)] + LISTS,
        compiler_params=pltpu.CompilerParams(vmem_limit_bytes=63 * MIB),
        cost_estimate=pl.CostEstimate(flops=2 * D * N * EDGES, bytes_accessed=6 * MIB, transcendentals=0),
        name="before",
    )(cnt, kinds, src, dst, tim, feat)


def layer_kernel(lay, *refs):
    nb = lay.blocks - 1
    (
        live_ref, cnt_ref, kinds_hbm, mix_hbm, idx_hbm, emb_hbm, cot_hbm, feat_hbm, own_ref,
    ) = refs[:9]
    near, far, xg_hbm = refs[9:9 + nb], refs[9 + nb:9 + 2 * nb], refs[9 + 2 * nb]
    (
        out_ref, dqkv_ref, skp_ref, types_ref, keep_ref, send_ref,
        lst_r, lst_o, lst_c,
        wpk, gpack, gout, gnorm, gskip, xg, low, cot_ref, feat_ref, kinds_ref, mix_ref, idx_ref, emb_ref,
        wt, xcat, qt, rte, dn_buf, dkve_buf, mu,
        bda, bdat, bdm, bdmt, ga, gm, dmu,
        kve, qe, msg, wexp, raws,
        num, dnum, dqkv, dtkv, skp,
        wsem, xsem, osem, gsem,
    ) = refs[10 + 2 * nb:]
    me, core, zi = position()
    zi = lax.rem(zi, GROUP)
    small = [
        pltpu.make_async_copy(source, to, xsem.at[3 + i])
        for i, (source, to) in enumerate(
            ((kinds_hbm, kinds_ref), (mix_hbm, mix_ref), (feat_hbm, feat_ref), (idx_hbm, idx_ref), (emb_hbm, emb_ref))
        )
    ]
    weights = lay.weight_copies(me, core, own_ref, near, far, wpk, wsem)
    for copy in small + weights:
        copy.start()
    xg_copy = pltpu.make_async_copy(xg_hbm, xg, xsem.at[0])
    xg_copy.start()
    cot_copy = pltpu.make_async_copy(cot_hbm, cot_ref, xsem.at[2])

    ident = eye()
    whole, chunks, total = list_blocks(cnt_ref, lst_r, lst_o, lst_c)

    def row(c, k):
        return idx_ref[pl.ds(pl.multiple_of(c * 8, 8), 8), :][k:k + 1]

    for ref in (num, dqkv, dtkv, ga, gm, dmu, gnorm, gskip, gout):
        ref[...] = jnp.zeros_like(ref)
    dkve_buf[...] = jnp.zeros_like(dkve_buf)

    small[0].wait()
    small[1].wait()
    mix = jnp.broadcast_to(mix_ref[...].astype(bf16).astype(f32), (8, 68))
    lanes68 = lax.broadcasted_iota(jnp.int32, (8, 68), 1)
    line68 = lax.broadcasted_iota(jnp.int32, (8, 68), 0)

    def column(first):
        return jnp.sum(jnp.where(lanes68 == first + line68, mix, 0.0), axis=1, keepdims=True)

    for r in range(REL):
        mu[r] = jnp.broadcast_to(column(r * H) * score_scale, (H, 128))
    skip_col = column(REL * H)

    kinds = kinds_ref[...]
    masks = (lax.broadcasted_iota(jnp.int32, (8, N), 0) == kinds).astype(f32)
    small[2].wait()
    featt = nt(ident, feat_ref[...])
    for s in range(TYPES):
        xcat[s * D:(s + 1) * D, :] = (featt * masks[s:s + 1]).astype(bf16)
    for copy in weights + small[3:]:
        copy.wait()
    cot_copy.start()
    finish = [
        pltpu.make_async_copy(
            wpk.at[pl.ds(a, b - a), pl.ds(0, 3 * D)], types_ref.at[pl.ds(s * D + c, d - c)], osem.at[3 + f]
        )
        for s in range(TYPES) for f, a, b, c, d in lay.type_rows(s)
    ]
    for copy in finish:
        copy.start()

    lane = lax.broadcasted_iota(jnp.int32, (D, 128), 1)
    rowi = lax.broadcasted_iota(jnp.int32, (D, 128), 0)
    on_diag = (lane // DK) == (rowi // DK) % 4
    zeros = jnp.zeros((128, 128), f32)
    for p in range(4):
        x = lay.get_edge(wpk, p * 128, (p + 1) * 128).astype(f32)
        rolled = [x if k == 0 else pltpu.roll(x, 32 * k, 1) for k in range(4)]
        for g in range(4):
            r, m = 2 * p + g // 2, g % 2
            t = jnp.concatenate([rolled[(h % 4 - g) % 4][h * 32:(h + 1) * 32] for h in range(H)], axis=0)
            t = jnp.where(on_diag, t, 0.0)
            for ref, a, b in (
                (bdm if m else bda, t[:128], t[128:]), (bdmt if m else bdat, t[:128].T, t[128:].T)
            ):
                ref[r] = jnp.concatenate(
                    [jnp.concatenate([a, zeros], axis=1), jnp.concatenate([zeros, b], axis=1)], axis=0
                ).astype(bf16)

    for cb in range(4):
        for s in range(4):
            wt[cb * 256:(cb + 1) * 256, s * 256:(s + 1) * 256] = nt(
                ident, lay.get_type(wpk, s, cb * 256, (cb + 1) * 256)
            ).astype(bf16)
    qt[...] = nn(wt[:D, :], xcat[...]).astype(bf16)
    wet = nt(ident, lay.get_edge(wpk, 512, 768)).astype(bf16)
    rte[...] = nt(wet, emb_ref[...]).astype(bf16)

    def mu_of(c, span):
        return jnp.concatenate([mu[lst_r[c * NSUB + k]] for k in range(span // SUB)], axis=1)

    def blocks_of(c, wide, span):
        return [(lst_r[c * NSUB + k * (wide // SUB)], slice(k * wide, (k + 1) * wide)) for k in range(span // wide)]

    def lookup(c):
        rt = nn(rte[...], one_hot_rows(row(c, TIME), 256))
        return (xg[:, place(c)].astype(f32) + rt).astype(bf16)

    def lookup_q(c):
        qe[:, place(c)] = nn(qt[...], one_hot_rows(row(c, TARGET), N)).astype(bf16)

    def project(c, xe):
        cu = row(c, TYPE)
        zero = jnp.zeros((), bf16)
        xm = jnp.concatenate([jnp.where(cu == s, xe, zero) for s in range(TYPES)], axis=0)
        kve[:, place(c)] = nn(wt[D:3 * D, :], xm).astype(bf16)

    def forward(wide, more, c, _, span=EC):
        at = place(c, span)
        kv_e = kve[:, at]
        q_e = qe[:, at].astype(f32)
        ks, ms = [], []
        for r, sl in blocks_of(c, wide, span):
            ks.append(nn(bdat[r], kv_e[:D, sl]))
            ms.append(nn(bdmt[r], kv_e[D:, sl]))
        ka = jnp.concatenate(ks, axis=1)
        me_ = jnp.concatenate(ms, axis=1)
        xe = lookup(c + 1) if more else None
        xg[:, at] = ka.astype(bf16)
        msg[:, at] = me_.astype(bf16)
        raw = head_sum(ka * q_e)
        raws[:, at] = raw
        lanes = lax.broadcasted_iota(jnp.int32, (H, SUB), 1)
        w = jnp.exp(raw * mu_of(c, span))
        w = jnp.concatenate(
            [jnp.where(lanes < lst_c[c * NSUB + k], w[:, k * SUB:(k + 1) * SUB], 0.0) for k in range(span // SUB)], axis=1
        )
        wexp[:, at] = w
        wm = (head_wide(w) * me_).astype(bf16)
        if more:
            lookup_q(c + 1)
        num[...] += nt(jnp.concatenate([wm, hi_lo(w)], axis=0), one_hot_rows(row(c, TARGET)[:, :span], N))
        if more:
            project(c + 1, xe)
        return 0

    xg_copy.wait()
    project(0, lookup(0))
    lookup_q(0)
    whole, last = jnp.minimum(whole, chunks - 1), chunks - 1
    lax.fori_loop(0, whole, functools.partial(forward, 2 * SUB, True), 0)
    lax.fori_loop(whole, last, functools.partial(forward, SUB, True), 0)
    few = total - last * NSUB <= NSUB // 2

    @pl.when(few)
    def _():
        forward(SUB, False, last, 0, EC // 2)

    @pl.when(jnp.logical_not(few))
    def _():
        forward(SUB, False, last, 0)

    cot_copy.wait()
    nwt = nt(ident, lay.get_norm(wpk)).astype(bf16)
    out_rows = jnp.concatenate([lay.get_type(wpk, s, 3 * D, 4 * D) for s in range(TYPES)], axis=1)

    def nodes(c):
        at = pl.ds(pl.multiple_of(c * NC, NC), NC)
        mk = (lax.broadcasted_iota(jnp.int32, (8, NC), 0) == kinds_ref[:, at]).astype(f32)
        live = (lax.broadcasted_iota(jnp.int32, (1, NC), 1) + c * NC < live_ref[0]).astype(f32)
        den = num[D:D + H, at] + num[D + H:, at] + (1.0 - live)
        inv_den = head_wide(1.0 / den)
        agg = num[:D, at] * inv_den
        phi = 0.5 * (1.0 + lax.erf(agg * (0.5 ** 0.5)))
        act = (agg * phi).astype(bf16)
        mkl = mk.astype(bf16)
        acat = jnp.concatenate([act * mkl[s:s + 1] for s in range(TYPES)], axis=0)
        yield
        trans = nn(wt[3 * D:, :], acat)
        yield
        alpha = 1.0 / (1.0 + jnp.exp(-jnp.sum(mk * skip_col, axis=0, keepdims=True)))
        ft = nt(ident, feat_ref[at, :])
        none = jnp.zeros((4, NC), f32)
        oh16 = jnp.concatenate([mk[0:4], none, none, none], axis=0).astype(bf16)
        gain = nn(nwt, oh16)
        bias = nn(nwt, jnp.concatenate([none, mk[0:4], none, none], axis=0).astype(bf16))
        dy = live * nt(ident, cot_ref[at, :])
        res = alpha * trans + (1.0 - alpha) * ft
        mean = jnp.mean(res, axis=0, keepdims=True)
        cen = res - mean
        inv = lax.rsqrt(jnp.mean(cen * cen, axis=0, keepdims=True) + norm_eps)
        nrm = cen * inv
        cot_ref[at, :] = (live * (nrm * gain + bias)).T.astype(bf16)
        dyn = dy * nrm
        dyn_hi = dyn.astype(bf16)
        dyn_lo = (dyn - dyn_hi.astype(f32)).astype(bf16)
        gnorm[0:4, :] += (nt(oh16, dyn_hi) + nt(oh16, dyn_lo))[0:4]
        gnorm[4:8, :] += nt(oh16, dy.astype(bf16))[0:4]
        dn = dy * gain
        dres = inv * (dn - jnp.mean(dn, axis=0, keepdims=True) - nrm * jnp.mean(dn * nrm, axis=0, keepdims=True))
        dtr = (alpha * dres).astype(bf16)
        yield
        dact = nn(out_rows, jnp.concatenate([dtr * mkl[s:s + 1] for s in range(TYPES)], axis=0))
        yield
        skp[:, at] = (1.0 - alpha) * dres
        dal = jnp.sum(dres * (trans - ft), axis=0, keepdims=True) * alpha * (1.0 - alpha)
        gskip[...] += jnp.broadcast_to(jnp.sum(mk * dal, axis=1, keepdims=True), (8, 128))
        gout[...] += nt(acat, dtr)
        dagg = dact * (phi + agg * (jnp.exp(-0.5 * agg * agg) * (0.5 / np.pi) ** 0.5))
        dnum[0:D, at] = (dagg * inv_den).astype(bf16)
        dnum[D:, at] = hi_lo(-head_sum(dagg * agg) / den)
        yield

    def node_steps(c, _):
        for _ in zip(*[nodes(NODE_STEPS * c + i) for i in range(NODE_STEPS)]):
            pass
        return 0

    lax.fori_loop(0, N // NC // NODE_STEPS, node_steps, 0)
    for i, (source, to) in enumerate(((cot_ref, out_ref), (skp, skp_ref))):
        finish.append(pltpu.make_async_copy(source, to, osem.at[i]))
        finish[-1].start()

    def gather_back(c):
        dn_buf[...] = nn(dnum[...], one_hot_rows(row(c, TARGET), N))

    def scatter_back(c, span=EC):
        dkve = dkve_buf[:, :span]
        dqkv[:, D:] += nt(one_hot_rows(row(c, SOURCE)[:, :span], N), dkve)
        dtkv[...] += nt(one_hot_rows(row(c, BUCKET)[:, :span], 1024), dkve)

    def backward(wide, more, c, _, span=EC):
        at = place(c, span)
        scatter_back(jnp.maximum(c - 1, 0))
        dn_e = dn_buf[:D, :span]
        w = wexp[:, at]
        dw = head_sum(dn_e * msg[:, at].astype(f32)) + dn_buf[D:D + H, :span] + dn_buf[D + H:, :span]
        ds = dw * w
        dsr = ds * raws[:, at]
        ss = head_wide(ds * mu_of(c, span))
        dka = (ss * qe[:, at].astype(f32)).astype(bf16)
        dms = (head_wide(w) * dn_e).astype(bf16)
        dqe = (ss * xg[:, at].astype(f32)).astype(bf16)
        if more:
            gather_back(c + 1)
        for r, sl in blocks_of(c, wide, span):
            dkve_buf[0:D, sl] = nn(bda[r], dka[:, sl]).astype(bf16)
            dkve_buf[D:, sl] = nn(bdm[r], dms[:, sl]).astype(bf16)
        for r, sl in blocks_of(c, wide, span):
            at_k = pl.ds(pl.multiple_of(c * EC + sl.start, SUB), wide)
            gak = nt(kve[0:D, at_k], dka[:, sl])
            gmk = nt(kve[D:, at_k], dms[:, sl])
            ga[r, 0:128] += gak[0:128, 0:128]
            ga[r, 128:] += gak[128:, 128:]
            gm[r, 0:128] += gmk[0:128, 0:128]
            gm[r, 128:] += gmk[128:, 128:]
            dmu[r] += sum(dsr[:, k:k + 128] for k in range(sl.start, sl.stop, 128))
        dqkv[:, :D] += nt(one_hot_rows(row(c, TARGET)[:, :span], N), dqe)
        return 0

    gather_back(0)
    def backward_pair(c, _):
        backward(2 * SUB, True, 2 * c, 0)
        backward(2 * SUB, True, 2 * c + 1, 0)
        return 0

    lax.fori_loop(0, whole // 2, backward_pair, 0)
    lax.fori_loop(whole // 2 * 2, whole, functools.partial(backward, 2 * SUB, True), 0)
    lax.fori_loop(whole, last, functools.partial(backward, SUB, True), 0)

    @pl.when(few)
    def _():
        backward(SUB, False, last, 0, EC // 2)
        scatter_back(last, EC // 2)

    @pl.when(jnp.logical_not(few))
    def _():
        backward(SUB, False, last, 0)
        scatter_back(last)


    low[...] = dqkv[...].astype(bf16)
    last = pltpu.make_async_copy(low, dqkv_ref, osem.at[2])
    last.start()
    finish.append(last)
    dt = dtkv[...].astype(bf16)
    drte = jnp.zeros((D, 256), f32)
    for s in range(TYPES):
        drte = drte + nt(lay.get_type(wpk, s, D, 3 * D), dt[s * 256:(s + 1) * 256, :])

    spots = [jnp.bitwise_xor(zi, j) for j in range(GROUP)]

    def put_edge(c0, value):
        lanes = slice(c0 % WIDE, c0 % WIDE + value.shape[1])
        for f in range(lay.blocks):
            gpack[spots[c0 // WIDE], f * lay.part + lay.trows:(f + 1) * lay.part, lanes] = value[
                f * lay.erows:(f + 1) * lay.erows
            ].astype(bf16)

    for p in range(4):
        acc = jnp.zeros((D, 128), f32)
        for g in range(4):
            r, m = 2 * p + g // 2, g % 2
            t = jnp.where(on_diag, (gm if m else ga)[r], 0.0)
            rolled = [t if k == 0 else pltpu.roll(t, 32 * k, 1) for k in range(4)]
            acc = acc + jnp.concatenate([rolled[(g - h % 4) % 4][h * 32:(h + 1) * 32] for h in range(H)], axis=0)
        put_edge(p * 128, acc)
    embt = nt(ident, emb_ref[...]).astype(bf16)
    put_edge(512, nt(embt, drte.astype(bf16)))

    lane8 = lax.broadcasted_iota(jnp.int32, (8, 256), 1)
    line8 = lax.broadcasted_iota(jnp.int32, (8, 256), 0)
    mixg = jnp.where(lane8 == REL * H + line8, gskip[:, 0:1], 0.0)
    for r in range(REL):
        col = jnp.sum(dmu[r], axis=1, keepdims=True) * score_scale
        mixg = mixg + jnp.where(lane8 == r * H + line8, col, 0.0)
    mixg = jnp.broadcast_to(jnp.sum(mixg, axis=0, keepdims=True), (8, 256))
    for f in range(lay.blocks):
        corner = jnp.concatenate(
            [gnorm[:, f * lay.wide:(f + 1) * lay.wide], jnp.zeros((8, 256 - lay.wide), f32)], axis=1
        )
        small = jnp.concatenate([corner, mixg, jnp.zeros((lay.erows - 16, 256), f32)], axis=0)
        gpack[spots[3], f * lay.part + lay.trows:(f + 1) * lay.part, :] = small.astype(bf16)

    done = 0
    for s in range(TYPES):
        g = nn(xcat[s * D:(s + 1) * D, :], low[...])
        g_kv = g[:, D:] + nn(rte[...], dt[s * 256:(s + 1) * 256, :])
        values = [g[:, :D], g_kv[:, :D], g_kv[:, D:], gout[s * D:(s + 1) * D, :]]
        for _, a, b, c, d in lay.type_rows(s):
            for j in range(GROUP):
                gpack[spots[j], a:b, :] = values[j][c:d].astype(bf16)
        while done < lay.blocks and (done + 1) * lay.trows <= (s + 1) * D:
            m = jnp.bitwise_xor(me, done)
            for i, (ref, side) in enumerate(((send_ref, 1 - core), (keep_ref, core))):
                at = pl.ds(pl.multiple_of(done * lay.part + side * lay.half, 16), lay.half)
                copy = pltpu.make_async_copy(gpack.at[:, at], ref.at[m], gsem.at[2 * done + i])
                copy.start()
                finish.append(copy)
            done += 1
    for copy in finish:
        copy.wait()


def emb_table():
    steps = np.arange(TB, dtype=np.float32)[:, None]
    col = np.arange(D)
    freq = np.exp(-np.log(np.float32(10000.0)) * (2 * (col // 2)).astype(np.float32) / np.float32(D)).astype(np.float32)
    angle = steps * freq[None]
    tab = np.where(col[None] % 2 == 0, np.sin(angle), np.cos(angle)).astype(np.float32)
    return np.concatenate([tab, np.zeros((256 - TB, D), np.float32)], axis=0)


def layer(lay, live, cnt, kinds, mix, idx, cot, feat, own, near, far, xg):
    sums = S((lay.blocks, GROUP, lay.half, WIDE), bf16)
    edges = lambda rows, kind: V((rows, EDGES), kind)
    return pl.pallas_call(
        functools.partial(layer_kernel, lay),
        out_shape=[S((N, D), bf16), S((N, 3 * D), bf16), S((D, N), f32), S((TYPES * D, 3 * D), bf16), sums, sums],
        in_specs=[SMEM, SMEM] + [ANY] * (2 * lay.blocks + 6),
        out_specs=[ANY] * 6,
        scratch_shapes=LISTS + [
            V((lay.blocks * lay.part, 1024), bf16), V((GROUP, lay.blocks * lay.part, WIDE), bf16), V((TYPES * D, D), f32),
            V((8, D), f32), V((8, 128), f32), edges(D, bf16), V((N, 3 * D), bf16), V((N, D), bf16), V((N, D), bf16),
            V(kinds.shape, jnp.int32), V(mix.shape, f32), V(idx.shape, jnp.int32), V((256, D), bf16),
            V((4 * D, TYPES * D), bf16), V((TYPES * D, N), bf16), V((D, N), bf16), V((D, 256), bf16),
            V((D + 16, EC), f32), V((2 * D, EC), bf16), V((REL, H, 128), f32),
            V((8, D, D), bf16), V((8, D, D), bf16), V((8, D, D), bf16), V((8, D, D), bf16),
            V((8, D, 128), f32), V((8, D, 128), f32), V((8, 8, 128), f32),
            edges(2 * D, bf16), edges(D, bf16), V((D, REL * SLOTS), bf16),
            V((H, REL * SLOTS), f32), V((H, REL * SLOTS), f32),
            V((D + 16, N), f32), V((D + 16, N), bf16), V((N, 3 * D), f32), V((TYPES * 256, 2 * D), f32), V((D, N), f32),
            pltpu.SemaphoreType.DMA((2 * lay.blocks - 1,)), pltpu.SemaphoreType.DMA((8,)),
            pltpu.SemaphoreType.DMA((3 + lay.blocks,)), pltpu.SemaphoreType.DMA((2 * lay.blocks,)),
        ],
        compiler_params=pltpu.CompilerParams(vmem_limit_bytes=LAYER_VMEM),
        cost_estimate=pl.CostEstimate(flops=60 * 10**9, bytes_accessed=16 * MIB, transcendentals=0),
        name="layer",
    )(live, cnt, kinds, mix, idx, jnp.asarray(emb_table(), bf16), cot, feat, own, *near, *far, xg)


def input_kernel(kinds_ref, dqkv_ref, skp_ref, types_ref, out_ref):
    masks = (lax.broadcasted_iota(jnp.int32, (8, N), 0) == kinds_ref[...]).astype(f32)
    for c in range(N // NC):
        at = slice(c * NC, (c + 1) * NC)
        proj = pick(masks[:, at], [nt(types_ref[s * D:(s + 1) * D, :], dqkv_ref[at, :]) for s in range(TYPES)])
        out_ref[at, :] = (proj + skp_ref[:, at]).T.astype(bf16)


def input_gradient(kinds, dqkv, skp, types):
    return pl.pallas_call(
        input_kernel,
        out_shape=S((N, D), bf16),
        compiler_params=pltpu.CompilerParams(vmem_limit_bytes=INPUT_VMEM),
        cost_estimate=pl.CostEstimate(flops=2 * N * D * D * 12, bytes_accessed=6 * MIB, transcendentals=0),
        name="input_gradient",
    )(kinds, dqkv, skp, types)


def tree(terms):
    while len(terms) > 1:
        terms = [terms[i] + terms[i + 1] for i in range(0, len(terms), 2)]
    return terms[0]


def add_core_kernel(lay, keep_ref, got_ref, *refs):
    ways = ((lay.blocks, lambda ref, m: ref.at[m, :, pl.ds(0, lay.first)]),
            (GROUP, lambda ref, m: ref.at[:, m, pl.ds(lay.first, lay.second)]))
    jobs = [(way, m) for way in range(2) for m in range(1, ways[way][0])] + [(0, 0), (1, 0)]
    outs, bufs, isem, osem = refs[:len(jobs)], refs[len(jobs):-2], *refs[-2:]
    loads = []
    for k, (way, m) in enumerate(jobs):
        pair = [
            pltpu.make_async_copy(ways[way][1](source, m), bufs[2 * way + i].at[m], isem.at[2 * k + i])
            for i, source in enumerate((keep_ref, got_ref))
        ]
        for copy in pair:
            copy.start()
        loads.append(pair)
    stores = []
    for k, (way, m) in enumerate(jobs):
        for copy in loads[k]:
            copy.wait()
        keep, got = bufs[2 * way], bufs[2 * way + 1]
        keep[m] = (keep[m].astype(f32) + got[m].astype(f32)).astype(bf16)
        stores.append(pltpu.make_async_copy(keep.at[m], outs[k], osem.at[k]))
        stores[-1].start()
    for copy in stores:
        copy.wait()


def add_core(lay, keep, got):
    shapes = [(lay.blocks, GROUP, lay.first, WIDE)] * 2 + [(GROUP, lay.blocks, lay.second, WIDE)] * 2
    out_shape = [S(shape[1:], bf16) for shape in shapes[::2] for _ in range(shape[0] - 1)] + [S(shape[1:], bf16) for shape in shapes[::2]]
    outs = pl.pallas_call(
        functools.partial(add_core_kernel, lay),
        out_shape=out_shape,
        in_specs=[ANY] * 2,
        out_specs=[ANY] * len(out_shape),
        scratch_shapes=[V(shape, bf16) for shape in shapes]
        + [pltpu.SemaphoreType.DMA((2 * len(out_shape),)), pltpu.SemaphoreType.DMA((len(out_shape),))],
        compiler_params=pltpu.CompilerParams(vmem_limit_bytes=63 * MIB),
        name="add_core",
    )(keep, got)
    return [outs[-2], *outs[:lay.blocks - 1]], [outs[-1], *outs[lay.blocks - 1:-2]]


def summed(terms):
    return tree([x.astype(f32) for x in terms]).astype(bf16)


def adam(param, first, second, avg, grad, rate):
    root = (1.0 - beta_two**STEP) ** 0.5
    first_new = beta_one * first + (1.0 - beta_one) * grad
    second_new = beta_two * second + (1.0 - beta_two) * (grad * grad)
    below = jnp.sqrt(second_new) + adam_eps * root
    guess = pl.reciprocal(below, approx=True)
    guess = guess * (2.0 - below * guess)
    param_new = (1.0 - rate * decay_rate) * param - (rate * root / (1.0 - beta_one**STEP)) * (first_new * guess)
    avg_new = ema_keep * avg + (1.0 - ema_keep) * param_new
    return (param_new, first_new, second_new, avg_new)


def update_kernel(jobs, count, *refs):
    pieces, refs = refs[:2 * GROUP], refs[2 * GROUP:]
    states, outs, refs = refs[:count], refs[count:2 * count], refs[2 * count:]
    gsum, bufs, news, isem, osem = refs[0], refs[1:1 + 4 * len(jobs)], refs[1 + 4 * len(jobs):-2], refs[-2], refs[-1]

    def view(ref, row, rows):
        return ref if rows == ref.shape[0] else ref.at[pl.ds(row, rows)]

    loads = [
        pltpu.make_async_copy(view(states[4 * job[0] + j], job[1], job[2]), bufs[4 * i + j], isem.at[4 * i + j])
        for i, job in enumerate(jobs) for j in range(4)
    ]
    for copy in loads:
        copy.start()
    _, core, zi = position()
    zi = lax.rem(zi, GROUP)
    high = gsum.shape[0] // 2
    for side in range(2):
        at = pl.ds(pl.multiple_of(jnp.bitwise_xor(core, side) * high, 16), high)
        for k in range(GROUP):
            want = jnp.bitwise_xor(zi, k)
            for j in range(GROUP):
                @pl.when(want == j)
                def _():
                    gsum[at, j * WIDE:(j + 1) * WIDE] = pieces[side * GROUP + k][...]
    stores = []
    for i, (group, row, rows, lanes, first, lane, rate) in enumerate(jobs):
        base = first // 16 * 16
        grad = gsum[base:base + max(16, rows), lane:lane + max(lanes, 128)].astype(f32)
        grad = grad[first - base:first - base + rows, :lanes]
        for j in range(4):
            loads[4 * i + j].wait()
        new = adam(*[bufs[4 * i + j][...] for j in range(4)], grad, rate)
        for j in range(4):
            news[4 * i + j][...] = new[j]
            copy = pltpu.make_async_copy(news[4 * i + j], view(outs[4 * group + j], row, rows), osem.at[4 * i + j])
            copy.start()
            stores.append(copy)
    for copy in stores:
        copy.wait()


def update(jobs, pieces, sets):
    states = [x for group in sets for x in group]
    bufs = [V((job[2], job[3]), f32) for job in jobs for _ in range(4)]
    return pl.pallas_call(
        functools.partial(update_kernel, jobs, len(states)),
        out_shape=[S(x.shape, f32) for x in states],
        in_specs=[VMEM] * len(pieces) + [ANY] * len(states),
        out_specs=[ANY] * len(states),
        scratch_shapes=[V((2 * pieces[0].shape[0], 1024), bf16)] + bufs + bufs
        + [pltpu.SemaphoreType.DMA((len(bufs),))] * 2,
        compiler_params=pltpu.CompilerParams(vmem_limit_bytes=63 * MIB),
        name="update",
    )(*pieces, *states)


def shards(dp, fsdp, *args):
    (
        node_feat, out_cot, node_type, node_count, edge_src, edge_dst, edge_time, edge_count,
        type_weight, type_first, type_second, type_avg,
        edge_weight, edge_first, edge_second, edge_avg,
        norm_params, norm_first, norm_second, norm_avg,
        mix_params, mix_first, mix_second, mix_avg,
    ) = args
    lines = dp // 2
    lay = Layout(fsdp)

    def swap(x, axis, mask):
        size = dp if axis == "dp" else fsdp
        return lax.ppermute(x, axis, [(i, i ^ mask) for i in range(size)])

    mine = pack_half(lay, type_weight, edge_weight, norm_params)
    near = [swap(mine, "fsdp", m) for m in range(1, fsdp)]
    kinds = node_type.reshape(1, N)
    own = pack(lay, type_weight, edge_weight, norm_params)
    idx, xg = before(edge_count, kinds, edge_src, edge_dst, edge_time, node_feat)
    own, idx, xg, near[0] = lax.optimization_barrier((own, idx, xg, near[0]))
    far = [swap(x, "dp", 1) for x in near]
    mixes = [x.reshape(1, 68) for x in (mix_params, mix_first, mix_second, mix_avg)]
    layer_out, dqkv, skp, types, keep, send = layer(
        lay, node_count, edge_count, kinds, mixes[0], idx, out_cot, node_feat,
        own, near, far, xg,
    )
    got = swap(send, "dp", 1)
    chip_a, chip_b = add_core(lay, keep, got)
    dqkv, *chip_a = lax.optimization_barrier((dqkv, *chip_a))
    part_a = [chip_a[0]] + [swap(chip_a[m], "fsdp", m) for m in range(1, fsdp)]
    part_b = [chip_b[0]] + [swap(chip_b[k], "dp", 2 * k) for k in range(1, GROUP)]
    input_grad = input_gradient(kinds, dqkv, skp, types)
    input_grad, *part_a = lax.optimization_barrier((input_grad, *part_a))
    piece_a = [summed([x[k] for x in part_a]) for k in range(GROUP)]
    piece_b = [summed([x[m] for x in part_b]) for m in range(fsdp)]
    total_a = summed([piece_a[0]] + [swap(piece_a[k], "dp", 2 * k) for k in range(1, GROUP)])
    total_b = summed([piece_b[0]] + [swap(piece_b[m], "fsdp", m) for m in range(1, fsdp)])
    total = jnp.concatenate([total_a, total_b], axis=0)
    step = GROUP
    while step < lines:
        total = summed([total, swap(total, "dp", 2 * step)])
        step *= 2
    totals = [total] + [swap(total, "dp", 2 * k) for k in range(1, GROUP)]
    totals = totals + [swap(x, "dp", 1) for x in totals]
    trows, erows = lay.trows, lay.erows
    jobs = [(0, row, erows, 1024, row, 0, rates[0]) for row in range(0, trows, erows)] + [
        (1, 0, erows, 768, trows, 0, rates[1]), (2, 0, 8, lay.wide, trows, 768, rates[2]),
        (3, 0, 1, 68, trows + 8, 768, rates[3]),
    ]
    new = update(jobs, totals, [
        [type_weight, type_first, type_second, type_avg], [edge_weight, edge_first, edge_second, edge_avg],
        [norm_params, norm_first, norm_second, norm_avg], mixes,
    ])
    return (layer_out, input_grad, *new[:12], *[x.reshape(68) for x in new[12:]])


def solution(mesh):
    whole = P(("dp", "fsdp"), None)
    flat = P(("dp", "fsdp"))
    state = [P("fsdp", None)] * 8 + [P(None, "fsdp")] * 4 + [P()] * 4
    return jax.shard_map(
        functools.partial(shards, mesh.shape["dp"], mesh.shape["fsdp"]),
        mesh=mesh,
        in_specs=tuple([whole, whole, flat, flat, whole, whole, whole, flat] + state),
        out_specs=tuple([whole, whole] + state),
        check_vma=False,
    )
```

```python
import functools

import jax
import jax.numpy as jnp
import numpy as np
from jax import lax
from jax.experimental import pallas as pl
from jax.experimental.pallas import tpu as pltpu
from jax.sharding import PartitionSpec as P

D, H, DK, TYPES, REL, TB = 256, 8, 32, 4, 8, 240
N = 1024
SLOTS = 1024
EC = 512
SUB = 128
NSUB = EC // SUB
NC = 256
NODE_STEPS = 4
EDGES = REL * SLOTS
bf16 = jnp.bfloat16
f32 = jnp.float32
norm_eps = 1e-5
STEP = 10
beta_one = 0.9
beta_two = 0.999
adam_eps = 1e-08
decay_rate = 0.01
ema_keep = 0.7
rates = (0.2, 0.2, 0.6, 0.6)
score_scale = DK ** (-0.5)

SMEM = pl.BlockSpec(memory_space=pltpu.SMEM)
VMEM = pl.BlockSpec(memory_space=pltpu.VMEM)
ANY = pl.BlockSpec(memory_space=pl.ANY)
S = jax.ShapeDtypeStruct
V = pltpu.VMEM
MIB = 1 << 20
INPUT_VMEM = 62 * MIB
SECOND = 3
SOURCE, TARGET, TIME, TYPE, BUCKET = range(5)
LAYER_VMEM = 63 * MIB
GROUP = 4
WIDE = 1024 // GROUP


def nn(a, b):
    return jnp.dot(a, b, preferred_element_type=f32)


def nt(a, b):
    return lax.dot_general(a, b, (((1,), (1,)), ((), ())), preferred_element_type=f32)


def one_hot_rows(row, count):
    wide = row.shape[1]
    base = lax.broadcasted_iota(jnp.int16, (256, wide), 0)
    one, zero = jnp.ones((), bf16), jnp.zeros((), bf16)
    return jnp.concatenate(
        [jnp.where(base == (row - 256 * g).astype(jnp.int16), one, zero) for g in range(count // 256)], axis=0
    )


def head_sum(x):
    return jnp.sum(x.reshape(H, DK, x.shape[1]), axis=1)


def head_wide(x):
    return jnp.broadcast_to(x[:, None, :], (H, DK, x.shape[1])).reshape(D, x.shape[1])


def hi_lo(x):
    high = x.astype(bf16).astype(f32)
    return jnp.concatenate([high, x - high], axis=0).astype(bf16)


def eye():
    return (
        lax.broadcasted_iota(jnp.int32, (256, 256), 0) == lax.broadcasted_iota(jnp.int32, (256, 256), 1)
    ).astype(f32).astype(bf16)


def pick(masks, wide):
    out = wide[0] * masks[0:1]
    for s in range(1, TYPES):
        out = jnp.where(masks[s:s + 1] > 0, wide[s], out)
    return out


def stack(pieces):
    return pieces[0] if len(pieces) == 1 else jnp.concatenate(pieces, axis=0)


class Layout:
    def __init__(self, blocks):
        self.blocks = blocks
        self.trows, self.erows = TYPES * D // blocks, D // blocks
        self.part = self.trows + self.erows
        self.half = self.part // 2
        self.wide = D // blocks
        self.second = self.half * SECOND // 10 // 16 * 16
        self.first = self.half - self.second

    def type_rows(self, s):
        for f in range(self.blocks):
            a, b = max(s * D, f * self.trows), min((s + 1) * D, (f + 1) * self.trows)
            if a < b:
                yield f, f * self.part + a - f * self.trows, f * self.part + b - f * self.trows, a - s * D, b - s * D

    def get_type(self, ref, s, c0, c1):
        return stack([ref[a:b, c0:c1] for _, a, b, _, _ in self.type_rows(s)])

    def get_edge(self, ref, c0, c1):
        return stack([ref[f * self.part + self.trows:(f + 1) * self.part, c0:c1] for f in range(self.blocks)])

    def get_norm(self, ref):
        rows = [f * self.part + self.trows for f in range(self.blocks)]
        return jnp.concatenate([ref[a:a + 16, 768:768 + self.wide].astype(f32) for a in rows], axis=1).astype(bf16)

    def weight_copies(self, me, core, own, near, far, wpk, sems):
        out = [pltpu.make_async_copy(own, wpk.at[pl.ds(pl.multiple_of(me * self.part, 16), self.part)], sems.at[0])]
        for m in range(1, self.blocks):
            base = jnp.bitwise_xor(me, m) * self.part
            for i, (ref, side) in enumerate(((near[m - 1], core), (far[m - 1], 1 - core))):
                at = pl.ds(pl.multiple_of(base + side * self.half, 16), self.half)
                out.append(pltpu.make_async_copy(ref, wpk.at[at], sems.at[2 * m - 1 + i]))
        return out


def position():
    return lax.axis_index("fsdp"), lax.rem(lax.axis_index("dp"), 2), lax.div(lax.axis_index("dp"), 2)


def list_blocks(cnt_ref, lst_r, lst_o, lst_c):
    def put(k, r, j, c):
        lst_r[k] = r
        lst_o[k] = j
        lst_c[k] = c - j * SUB

    def pairs(r, k):
        c = cnt_ref[r]

        def one(j, k):
            put(k, r, 2 * j, c)
            put(k + 1, r, 2 * j + 1, c)
            return k + 2
        return lax.fori_loop(0, (c + SUB - 1) // SUB // 2, one, k)

    def odd(r, k):
        c = cnt_ref[r]
        blocks = (c + SUB - 1) // SUB
        put(k, r, jnp.minimum(blocks, SLOTS // SUB) - 1, c)
        return k + lax.rem(blocks, 2)
    paired = lax.fori_loop(0, REL, pairs, 0)
    total = lax.fori_loop(0, REL, odd, paired)
    for extra in range(2 * NSUB):
        put(total + extra, 0, 0, 0)
    return paired // NSUB, (total + NSUB - 1) // NSUB, total


def rows_of(ref, lst_r, lst_o, c):
    pieces = []
    for k in range(NSUB):
        r, j = lst_r[c * NSUB + k], lst_o[c * NSUB + k]
        pair = ref[pl.ds(r, 1), pl.ds(pl.multiple_of(lax.div(j, 2) * 2 * SUB, 2 * SUB), 2 * SUB)]
        pieces.append(jnp.where(lax.rem(j, 2) == 0, pair[:, :SUB], pair[:, SUB:]))
    return jnp.concatenate(pieces, axis=1)


def place(c, span=EC):
    return pl.ds(pl.multiple_of(c * EC, EC), span)


LISTS = [pltpu.SMEM((REL * SLOTS // SUB + 2 * NSUB,), jnp.int32)] * 3


def pack_half_kernel(lay, type_ref, edge_ref, norm_hbm, mine_ref, buf, low, norm_ref, isem, osem):
    _, core, _ = position()
    norm = pltpu.make_async_copy(norm_hbm, norm_ref, isem.at[5])
    norm.start()
    rows = lay.half // 5
    for side in range(2):
        @pl.when(core == side)
        def _():
            loads = []
            for i in range(5):
                if side == 1 and i >= 3:
                    source, to = edge_ref.at[pl.ds((i - 3) * rows, rows)], buf.at[pl.ds(i * rows, rows), pl.ds(0, 768)]
                else:
                    source, to = type_ref.at[pl.ds(side * lay.half + i * rows, rows)], buf.at[pl.ds(i * rows, rows)]
                loads.append(pltpu.make_async_copy(source, to, isem.at[i]))
                loads[-1].start()
            norm.wait()
            if side == 1:
                corner = jnp.concatenate([norm_ref[...], jnp.zeros((8, 256 - lay.wide), f32)], axis=1)
                buf[3 * rows:, 768:] = jnp.concatenate([corner, jnp.zeros((lay.erows - 8, 256), f32)], axis=0)
            stores = []
            for i in range(5):
                loads[i].wait()
                at = slice(i * rows, (i + 1) * rows)
                low[at] = buf[at].astype(bf16)
                stores.append(pltpu.make_async_copy(low.at[pl.ds(i * rows, rows)], mine_ref.at[pl.ds(i * rows, rows)], osem.at[i]))
                stores[-1].start()
            for copy in stores:
                copy.wait()


def pack_half(lay, type_weight, edge_weight, norm_params):
    return pl.pallas_call(
        functools.partial(pack_half_kernel, lay),
        out_shape=S((lay.half, 1024), bf16),
        in_specs=[ANY] * 3,
        out_specs=ANY,
        scratch_shapes=[
            V((lay.half, 1024), f32), V((lay.half, 1024), bf16), V((8, lay.wide), f32),
            pltpu.SemaphoreType.DMA((6,)), pltpu.SemaphoreType.DMA((5,)),
        ],
        compiler_params=pltpu.CompilerParams(vmem_limit_bytes=63 * MIB),
        name="pack_half",
    )(type_weight, edge_weight, norm_params)


def pack_kernel(lay, type_ref, edge_ref, norm_ref, own_ref):
    own_ref[0:lay.trows, :] = type_ref[...].astype(bf16)
    own_ref[lay.trows:, 0:768] = edge_ref[...].astype(bf16)
    corner = jnp.concatenate([norm_ref[...], jnp.zeros((8, 256 - lay.wide), f32)], axis=1)
    own_ref[lay.trows:, 768:] = jnp.concatenate([corner, jnp.zeros((lay.erows - 8, 256), f32)], axis=0).astype(bf16)


def pack(lay, type_weight, edge_weight, norm_params):
    return pl.pallas_call(
        functools.partial(pack_kernel, lay),
        out_shape=S((lay.part, 1024), bf16),
        compiler_params=pltpu.CompilerParams(vmem_limit_bytes=63 * MIB),
        name="pack",
    )(type_weight, edge_weight, norm_params)


def before_kernel(cnt_ref, kinds_ref, src_ref, dst_ref, tim_ref, feat_ref, idx_ref, xg_ref, typ_ref, lst_r, lst_o, lst_c):
    _, chunks, _ = list_blocks(cnt_ref, lst_r, lst_o, lst_c)
    src = src_ref[...]
    for j in range(SLOTS // 128):
        idx = src[:, j * 128:(j + 1) * 128]
        low = jnp.bitwise_and(idx, 127)
        high = jnp.right_shift(idx, 7)
        acc = jnp.zeros((8, 128), jnp.int32)
        for k in range(N // 128):
            row = jnp.broadcast_to(kinds_ref[:, k * 128:(k + 1) * 128], (8, 128))
            acc = jnp.where(high == k, jnp.take_along_axis(row, low, axis=1), acc)
        typ_ref[:, j * 128:(j + 1) * 128] = acc
    ft = nt(eye(), feat_ref[...]).astype(bf16)

    def one(c, _):
        src, dst, tim, typ = [rows_of(ref, lst_r, lst_o, c) for ref in (src_ref, dst_ref, tim_ref, typ_ref)]
        idx_ref[pl.ds(pl.multiple_of(c * 8, 8), 8), :] = jnp.concatenate(
            [src, dst, tim, typ, typ * 256 + tim, src, src, src], axis=0
        )
        xg_ref[:, place(c)] = nn(ft, one_hot_rows(src, N)).astype(bf16)
        return 0

    def two(c, _):
        one(2 * c, 0)
        one(2 * c + 1, 0)
        return 0

    lax.fori_loop(0, (chunks + 1) // 2, two, 0)


def before(cnt, kinds, src, dst, tim, feat):
    return pl.pallas_call(
        before_kernel,
        out_shape=(S((EDGES // EC * 8, EC), jnp.int32), S((D, EDGES), bf16)),
        in_specs=[SMEM] + [VMEM] * 5,
        scratch_shapes=[V((REL, SLOTS), jnp.int32)] + LISTS,
        compiler_params=pltpu.CompilerParams(vmem_limit_bytes=63 * MIB),
        cost_estimate=pl.CostEstimate(flops=2 * D * N * EDGES, bytes_accessed=6 * MIB, transcendentals=0),
        name="before",
    )(cnt, kinds, src, dst, tim, feat)


def layer_kernel(lay, *refs):
    nb = lay.blocks - 1
    (
        live_ref, cnt_ref, kinds_hbm, mix_hbm, idx_hbm, emb_hbm, cot_hbm, feat_hbm, own_ref,
    ) = refs[:9]
    near, far, xg_hbm = refs[9:9 + nb], refs[9 + nb:9 + 2 * nb], refs[9 + 2 * nb]
    (
        out_ref, dqkv_ref, skp_ref, types_ref, keep_ref, send_ref,
        lst_r, lst_o, lst_c,
        wpk, gpack, gout, gnorm, gskip, xg, low, cot_ref, feat_ref, kinds_ref, mix_ref, idx_ref, emb_ref,
        wt, xcat, qt, rte, dn_buf, dkve_buf, mu,
        bda, bdat, bdm, bdmt, ga, gm, dmu,
        kve, qe, msg, wexp, raws,
        num, dnum, dqkv, dtkv, skp,
        wsem, xsem, osem, gsem,
    ) = refs[10 + 2 * nb:]
    me, core, zi = position()
    zi = lax.rem(zi, GROUP)
    small = [
        pltpu.make_async_copy(source, to, xsem.at[3 + i])
        for i, (source, to) in enumerate(
            ((kinds_hbm, kinds_ref), (mix_hbm, mix_ref), (feat_hbm, feat_ref), (idx_hbm, idx_ref), (emb_hbm, emb_ref))
        )
    ]
    weights = lay.weight_copies(me, core, own_ref, near, far, wpk, wsem)
    for copy in small + weights:
        copy.start()
    xg_copy = pltpu.make_async_copy(xg_hbm, xg, xsem.at[0])
    xg_copy.start()
    cot_copy = pltpu.make_async_copy(cot_hbm, cot_ref, xsem.at[2])

    ident = eye()
    whole, chunks, total = list_blocks(cnt_ref, lst_r, lst_o, lst_c)

    def row(c, k):
        return idx_ref[pl.ds(pl.multiple_of(c * 8, 8), 8), :][k:k + 1]

    for ref in (num, dqkv, dtkv, ga, gm, dmu, gnorm, gskip, gout):
        ref[...] = jnp.zeros_like(ref)
    dkve_buf[...] = jnp.zeros_like(dkve_buf)

    small[0].wait()
    small[1].wait()
    mix = jnp.broadcast_to(mix_ref[...].astype(bf16).astype(f32), (8, 68))
    lanes68 = lax.broadcasted_iota(jnp.int32, (8, 68), 1)
    line68 = lax.broadcasted_iota(jnp.int32, (8, 68), 0)

    def column(first):
        return jnp.sum(jnp.where(lanes68 == first + line68, mix, 0.0), axis=1, keepdims=True)

    for r in range(REL):
        mu[r] = jnp.broadcast_to(column(r * H) * score_scale, (H, 128))
    skip_col = column(REL * H)

    kinds = kinds_ref[...]
    masks = (lax.broadcasted_iota(jnp.int32, (8, N), 0) == kinds).astype(f32)
    small[2].wait()
    featt = nt(ident, feat_ref[...])
    for s in range(TYPES):
        xcat[s * D:(s + 1) * D, :] = (featt * masks[s:s + 1]).astype(bf16)
    for copy in weights + small[3:]:
        copy.wait()
    cot_copy.start()
    finish = [
        pltpu.make_async_copy(
            wpk.at[pl.ds(a, b - a), pl.ds(0, 3 * D)], types_ref.at[pl.ds(s * D + c, d - c)], osem.at[3 + f]
        )
        for s in range(TYPES) for f, a, b, c, d in lay.type_rows(s)
    ]
    for copy in finish:
        copy.start()

    lane = lax.broadcasted_iota(jnp.int32, (D, 128), 1)
    rowi = lax.broadcasted_iota(jnp.int32, (D, 128), 0)
    on_diag = (lane // DK) == (rowi // DK) % 4
    zeros = jnp.zeros((128, 128), f32)
    for p in range(4):
        x = lay.get_edge(wpk, p * 128, (p + 1) * 128).astype(f32)
        rolled = [x if k == 0 else pltpu.roll(x, 32 * k, 1) for k in range(4)]
        for g in range(4):
            r, m = 2 * p + g // 2, g % 2
            t = jnp.concatenate([rolled[(h % 4 - g) % 4][h * 32:(h + 1) * 32] for h in range(H)], axis=0)
            t = jnp.where(on_diag, t, 0.0)
            for ref, a, b in (
                (bdm if m else bda, t[:128], t[128:]), (bdmt if m else bdat, t[:128].T, t[128:].T)
            ):
                ref[r] = jnp.concatenate(
                    [jnp.concatenate([a, zeros], axis=1), jnp.concatenate([zeros, b], axis=1)], axis=0
                ).astype(bf16)

    for cb in range(4):
        for s in range(4):
            wt[cb * 256:(cb + 1) * 256, s * 256:(s + 1) * 256] = nt(
                ident, lay.get_type(wpk, s, cb * 256, (cb + 1) * 256)
            ).astype(bf16)
    qt[...] = nn(wt[:D, :], xcat[...]).astype(bf16)
    wet = nt(ident, lay.get_edge(wpk, 512, 768)).astype(bf16)
    rte[...] = nt(wet, emb_ref[...]).astype(bf16)

    def mu_of(c, span):
        return jnp.concatenate([mu[lst_r[c * NSUB + k]] for k in range(span // SUB)], axis=1)

    def blocks_of(c, wide, span):
        return [(lst_r[c * NSUB + k * (wide // SUB)], slice(k * wide, (k + 1) * wide)) for k in range(span // wide)]

    def lookup(c):
        rt = nn(rte[...], one_hot_rows(row(c, TIME), 256))
        return (xg[:, place(c)].astype(f32) + rt).astype(bf16)

    def lookup_q(c):
        qe[:, place(c)] = nn(qt[...], one_hot_rows(row(c, TARGET), N)).astype(bf16)

    def project(c, xe):
        cu = row(c, TYPE)
        zero = jnp.zeros((), bf16)
        xm = jnp.concatenate([jnp.where(cu == s, xe, zero) for s in range(TYPES)], axis=0)
        kve[:, place(c)] = nn(wt[D:3 * D, :], xm).astype(bf16)

    def forward(wide, more, c, _, span=EC):
        at = place(c, span)
        kv_e = kve[:, at]
        q_e = qe[:, at].astype(f32)
        ks, ms = [], []
        for r, sl in blocks_of(c, wide, span):
            ks.append(nn(bdat[r], kv_e[:D, sl]))
            ms.append(nn(bdmt[r], kv_e[D:, sl]))
        ka = jnp.concatenate(ks, axis=1)
        me_ = jnp.concatenate(ms, axis=1)
        xe = lookup(c + 1) if more else None
        xg[:, at] = ka.astype(bf16)
        msg[:, at] = me_.astype(bf16)
        raw = head_sum(ka * q_e)
        raws[:, at] = raw
        lanes = lax.broadcasted_iota(jnp.int32, (H, SUB), 1)
        w = jnp.exp(raw * mu_of(c, span))
        w = jnp.concatenate(
            [jnp.where(lanes < lst_c[c * NSUB + k], w[:, k * SUB:(k + 1) * SUB], 0.0) for k in range(span // SUB)], axis=1
        )
        wexp[:, at] = w
        wm = (head_wide(w) * me_).astype(bf16)
        if more:
            lookup_q(c + 1)
        num[...] += nt(jnp.concatenate([wm, hi_lo(w)], axis=0), one_hot_rows(row(c, TARGET)[:, :span], N))
        if more:
            project(c + 1, xe)
        return 0

    xg_copy.wait()
    project(0, lookup(0))
    lookup_q(0)
    whole, last = jnp.minimum(whole, chunks - 1), chunks - 1
    lax.fori_loop(0, whole, functools.partial(forward, 2 * SUB, True), 0)
    lax.fori_loop(whole, last, functools.partial(forward, SUB, True), 0)
    few = total - last * NSUB <= NSUB // 2

    @pl.when(few)
    def _():
        forward(SUB, False, last, 0, EC // 2)

    @pl.when(jnp.logical_not(few))
    def _():
        forward(SUB, False, last, 0)

    cot_copy.wait()
    nwt = nt(ident, lay.get_norm(wpk)).astype(bf16)
    out_rows = jnp.concatenate([lay.get_type(wpk, s, 3 * D, 4 * D) for s in range(TYPES)], axis=1)

    def nodes(c):
        at = pl.ds(pl.multiple_of(c * NC, NC), NC)
        mk = (lax.broadcasted_iota(jnp.int32, (8, NC), 0) == kinds_ref[:, at]).astype(f32)
        live = (lax.broadcasted_iota(jnp.int32, (1, NC), 1) + c * NC < live_ref[0]).astype(f32)
        den = num[D:D + H, at] + num[D + H:, at] + (1.0 - live)
        inv_den = head_wide(1.0 / den)
        agg = num[:D, at] * inv_den
        phi = 0.5 * (1.0 + lax.erf(agg * (0.5 ** 0.5)))
        act = (agg * phi).astype(bf16)
        mkl = mk.astype(bf16)
        acat = jnp.concatenate([act * mkl[s:s + 1] for s in range(TYPES)], axis=0)
        yield
        trans = nn(wt[3 * D:, :], acat)
        yield
        alpha = 1.0 / (1.0 + jnp.exp(-jnp.sum(mk * skip_col, axis=0, keepdims=True)))
        ft = nt(ident, feat_ref[at, :])
        none = jnp.zeros((4, NC), f32)
        oh16 = jnp.concatenate([mk[0:4], none, none, none], axis=0).astype(bf16)
        gain = nn(nwt, oh16)
        bias = nn(nwt, jnp.concatenate([none, mk[0:4], none, none], axis=0).astype(bf16))
        dy = live * nt(ident, cot_ref[at, :])
        res = alpha * trans + (1.0 - alpha) * ft
        mean = jnp.mean(res, axis=0, keepdims=True)
        cen = res - mean
        inv = lax.rsqrt(jnp.mean(cen * cen, axis=0, keepdims=True) + norm_eps)
        nrm = cen * inv
        cot_ref[at, :] = (live * (nrm * gain + bias)).T.astype(bf16)
        dyn = dy * nrm
        dyn_hi = dyn.astype(bf16)
        dyn_lo = (dyn - dyn_hi.astype(f32)).astype(bf16)
        gnorm[0:4, :] += (nt(oh16, dyn_hi) + nt(oh16, dyn_lo))[0:4]
        gnorm[4:8, :] += nt(oh16, dy.astype(bf16))[0:4]
        dn = dy * gain
        dres = inv * (dn - jnp.mean(dn, axis=0, keepdims=True) - nrm * jnp.mean(dn * nrm, axis=0, keepdims=True))
        dtr = (alpha * dres).astype(bf16)
        yield
        dact = nn(out_rows, jnp.concatenate([dtr * mkl[s:s + 1] for s in range(TYPES)], axis=0))
        yield
        skp[:, at] = (1.0 - alpha) * dres
        dal = jnp.sum(dres * (trans - ft), axis=0, keepdims=True) * alpha * (1.0 - alpha)
        gskip[...] += jnp.broadcast_to(jnp.sum(mk * dal, axis=1, keepdims=True), (8, 128))
        gout[...] += nt(acat, dtr)
        dagg = dact * (phi + agg * (jnp.exp(-0.5 * agg * agg) * (0.5 / np.pi) ** 0.5))
        dnum[0:D, at] = (dagg * inv_den).astype(bf16)
        dnum[D:, at] = hi_lo(-head_sum(dagg * agg) / den)
        yield

    def node_steps(c, _):
        for _ in zip(*[nodes(NODE_STEPS * c + i) for i in range(NODE_STEPS)]):
            pass
        return 0

    lax.fori_loop(0, N // NC // NODE_STEPS, node_steps, 0)
    for i, (source, to) in enumerate(((cot_ref, out_ref), (skp, skp_ref))):
        finish.append(pltpu.make_async_copy(source, to, osem.at[i]))
        finish[-1].start()

    def gather_back(c):
        dn_buf[...] = nn(dnum[...], one_hot_rows(row(c, TARGET), N))

    def scatter_nodes(c, dkve):
        dqkv[:, D:] += nt(one_hot_rows(row(c, SOURCE)[:, :dkve.shape[1]], N), dkve)

    def scatter_times(c, dkve):
        dtkv[...] += nt(one_hot_rows(row(c, BUCKET)[:, :dkve.shape[1]], 1024), dkve)

    def scatter_back(c, span=EC):
        scatter_times(c, dkve_buf[:, :span])
        scatter_nodes(c, dkve_buf[:, :span])

    def backward(wide, more, c, _, span=EC):
        at = place(c, span)
        before, dkve = jnp.maximum(c - 1, 0), dkve_buf[...]
        scatter_times(before, dkve)
        dn_e = dn_buf[:D, :span]
        w = wexp[:, at]
        dw = head_sum(dn_e * msg[:, at].astype(f32)) + dn_buf[D:D + H, :span] + dn_buf[D + H:, :span]
        ds = dw * w
        dsr = ds * raws[:, at]
        ss = head_wide(ds * mu_of(c, span))
        dka = (ss * qe[:, at].astype(f32)).astype(bf16)
        dms = (head_wide(w) * dn_e).astype(bf16)
        dqe = (ss * xg[:, at].astype(f32)).astype(bf16)
        for r, sl in blocks_of(c, wide, span):
            dkve_buf[0:D, sl] = nn(bda[r], dka[:, sl]).astype(bf16)
            dkve_buf[D:, sl] = nn(bdm[r], dms[:, sl]).astype(bf16)
        for r, sl in blocks_of(c, wide, span):
            at_k = pl.ds(pl.multiple_of(c * EC + sl.start, SUB), wide)
            gak = nt(kve[0:D, at_k], dka[:, sl])
            gmk = nt(kve[D:, at_k], dms[:, sl])
            ga[r, 0:128] += gak[0:128, 0:128]
            ga[r, 128:] += gak[128:, 128:]
            gm[r, 0:128] += gmk[0:128, 0:128]
            gm[r, 128:] += gmk[128:, 128:]
            dmu[r] += sum(dsr[:, k:k + 128] for k in range(sl.start, sl.stop, 128))
        dqkv[:, :D] += nt(one_hot_rows(row(c, TARGET)[:, :span], N), dqe)
        scatter_nodes(before, dkve)
        if more:
            gather_back(c + 1)
        return 0

    gather_back(0)
    def backward_pair(c, _):
        backward(2 * SUB, True, 2 * c, 0)
        backward(2 * SUB, True, 2 * c + 1, 0)
        return 0

    lax.fori_loop(0, whole // 2, backward_pair, 0)
    lax.fori_loop(whole // 2 * 2, whole, functools.partial(backward, 2 * SUB, True), 0)
    lax.fori_loop(whole, last, functools.partial(backward, SUB, True), 0)

    @pl.when(few)
    def _():
        backward(SUB, False, last, 0, EC // 2)
        scatter_back(last, EC // 2)

    @pl.when(jnp.logical_not(few))
    def _():
        backward(SUB, False, last, 0)
        scatter_back(last)


    low[...] = dqkv[...].astype(bf16)
    last = pltpu.make_async_copy(low, dqkv_ref, osem.at[2])
    last.start()
    finish.append(last)
    dt = dtkv[...].astype(bf16)
    drte = jnp.zeros((D, 256), f32)
    for s in range(TYPES):
        drte = drte + nt(lay.get_type(wpk, s, D, 3 * D), dt[s * 256:(s + 1) * 256, :])

    spots = [jnp.bitwise_xor(zi, j) for j in range(GROUP)]

    def put_edge(c0, value):
        lanes = slice(c0 % WIDE, c0 % WIDE + value.shape[1])
        for f in range(lay.blocks):
            gpack[spots[c0 // WIDE], f * lay.part + lay.trows:(f + 1) * lay.part, lanes] = value[
                f * lay.erows:(f + 1) * lay.erows
            ].astype(bf16)

    for p in range(4):
        acc = jnp.zeros((D, 128), f32)
        for g in range(4):
            r, m = 2 * p + g // 2, g % 2
            t = jnp.where(on_diag, (gm if m else ga)[r], 0.0)
            rolled = [t if k == 0 else pltpu.roll(t, 32 * k, 1) for k in range(4)]
            acc = acc + jnp.concatenate([rolled[(g - h % 4) % 4][h * 32:(h + 1) * 32] for h in range(H)], axis=0)
        put_edge(p * 128, acc)
    embt = nt(ident, emb_ref[...]).astype(bf16)
    put_edge(512, nt(embt, drte.astype(bf16)))

    lane8 = lax.broadcasted_iota(jnp.int32, (8, 256), 1)
    line8 = lax.broadcasted_iota(jnp.int32, (8, 256), 0)
    mixg = jnp.where(lane8 == REL * H + line8, gskip[:, 0:1], 0.0)
    for r in range(REL):
        col = jnp.sum(dmu[r], axis=1, keepdims=True) * score_scale
        mixg = mixg + jnp.where(lane8 == r * H + line8, col, 0.0)
    mixg = jnp.broadcast_to(jnp.sum(mixg, axis=0, keepdims=True), (8, 256))
    for f in range(lay.blocks):
        corner = jnp.concatenate(
            [gnorm[:, f * lay.wide:(f + 1) * lay.wide], jnp.zeros((8, 256 - lay.wide), f32)], axis=1
        )
        small = jnp.concatenate([corner, mixg, jnp.zeros((lay.erows - 16, 256), f32)], axis=0)
        gpack[spots[3], f * lay.part + lay.trows:(f + 1) * lay.part, :] = small.astype(bf16)

    done = 0
    for s in range(TYPES):
        g = nn(xcat[s * D:(s + 1) * D, :], low[...])
        g_kv = g[:, D:] + nn(rte[...], dt[s * 256:(s + 1) * 256, :])
        values = [g[:, :D], g_kv[:, :D], g_kv[:, D:], gout[s * D:(s + 1) * D, :]]
        for _, a, b, c, d in lay.type_rows(s):
            for j in range(GROUP):
                gpack[spots[j], a:b, :] = values[j][c:d].astype(bf16)
        while done < lay.blocks and (done + 1) * lay.trows <= (s + 1) * D:
            m = jnp.bitwise_xor(me, done)
            for i, (ref, side) in enumerate(((send_ref, 1 - core), (keep_ref, core))):
                at = pl.ds(pl.multiple_of(done * lay.part + side * lay.half, 16), lay.half)
                copy = pltpu.make_async_copy(gpack.at[:, at], ref.at[m], gsem.at[2 * done + i])
                copy.start()
                finish.append(copy)
            done += 1
    for copy in finish:
        copy.wait()


def emb_table():
    steps = np.arange(TB, dtype=np.float32)[:, None]
    col = np.arange(D)
    freq = np.exp(-np.log(np.float32(10000.0)) * (2 * (col // 2)).astype(np.float32) / np.float32(D)).astype(np.float32)
    angle = steps * freq[None]
    tab = np.where(col[None] % 2 == 0, np.sin(angle), np.cos(angle)).astype(np.float32)
    return np.concatenate([tab, np.zeros((256 - TB, D), np.float32)], axis=0)


def layer(lay, live, cnt, kinds, mix, idx, cot, feat, own, near, far, xg):
    sums = S((lay.blocks, GROUP, lay.half, WIDE), bf16)
    edges = lambda rows, kind: V((rows, EDGES), kind)
    return pl.pallas_call(
        functools.partial(layer_kernel, lay),
        out_shape=[S((N, D), bf16), S((N, 3 * D), bf16), S((D, N), f32), S((TYPES * D, 3 * D), bf16), sums, sums],
        in_specs=[SMEM, SMEM] + [ANY] * (2 * lay.blocks + 6),
        out_specs=[ANY] * 6,
        scratch_shapes=LISTS + [
            V((lay.blocks * lay.part, 1024), bf16), V((GROUP, lay.blocks * lay.part, WIDE), bf16), V((TYPES * D, D), f32),
            V((8, D), f32), V((8, 128), f32), edges(D, bf16), V((N, 3 * D), bf16), V((N, D), bf16), V((N, D), bf16),
            V(kinds.shape, jnp.int32), V(mix.shape, f32), V(idx.shape, jnp.int32), V((256, D), bf16),
            V((4 * D, TYPES * D), bf16), V((TYPES * D, N), bf16), V((D, N), bf16), V((D, 256), bf16),
            V((D + 16, EC), f32), V((2 * D, EC), bf16), V((REL, H, 128), f32),
            V((8, D, D), bf16), V((8, D, D), bf16), V((8, D, D), bf16), V((8, D, D), bf16),
            V((8, D, 128), f32), V((8, D, 128), f32), V((8, 8, 128), f32),
            edges(2 * D, bf16), edges(D, bf16), V((D, REL * SLOTS), bf16),
            V((H, REL * SLOTS), f32), V((H, REL * SLOTS), f32),
            V((D + 16, N), f32), V((D + 16, N), bf16), V((N, 3 * D), f32), V((TYPES * 256, 2 * D), f32), V((D, N), f32),
            pltpu.SemaphoreType.DMA((2 * lay.blocks - 1,)), pltpu.SemaphoreType.DMA((8,)),
            pltpu.SemaphoreType.DMA((3 + lay.blocks,)), pltpu.SemaphoreType.DMA((2 * lay.blocks,)),
        ],
        compiler_params=pltpu.CompilerParams(vmem_limit_bytes=LAYER_VMEM),
        cost_estimate=pl.CostEstimate(flops=60 * 10**9, bytes_accessed=16 * MIB, transcendentals=0),
        name="layer",
    )(live, cnt, kinds, mix, idx, jnp.asarray(emb_table(), bf16), cot, feat, own, *near, *far, xg)


def input_kernel(kinds_ref, dqkv_ref, skp_ref, types_ref, out_ref):
    masks = (lax.broadcasted_iota(jnp.int32, (8, N), 0) == kinds_ref[...]).astype(f32)
    for c in range(N // NC):
        at = slice(c * NC, (c + 1) * NC)
        proj = pick(masks[:, at], [nt(types_ref[s * D:(s + 1) * D, :], dqkv_ref[at, :]) for s in range(TYPES)])
        out_ref[at, :] = (proj + skp_ref[:, at]).T.astype(bf16)


def input_gradient(kinds, dqkv, skp, types):
    return pl.pallas_call(
        input_kernel,
        out_shape=S((N, D), bf16),
        compiler_params=pltpu.CompilerParams(vmem_limit_bytes=INPUT_VMEM),
        cost_estimate=pl.CostEstimate(flops=2 * N * D * D * 12, bytes_accessed=6 * MIB, transcendentals=0),
        name="input_gradient",
    )(kinds, dqkv, skp, types)


def tree(terms):
    while len(terms) > 1:
        terms = [terms[i] + terms[i + 1] for i in range(0, len(terms), 2)]
    return terms[0]


def add_core_kernel(lay, keep_ref, got_ref, *refs):
    ways = ((lay.blocks, lambda ref, m: ref.at[m, :, pl.ds(0, lay.first)]),
            (GROUP, lambda ref, m: ref.at[:, m, pl.ds(lay.first, lay.second)]))
    jobs = [(way, m) for way in range(2) for m in range(1, ways[way][0])] + [(0, 0), (1, 0)]
    outs, bufs, isem, osem = refs[:len(jobs)], refs[len(jobs):-2], *refs[-2:]
    loads = []
    for k, (way, m) in enumerate(jobs):
        pair = [
            pltpu.make_async_copy(ways[way][1](source, m), bufs[2 * way + i].at[m], isem.at[2 * k + i])
            for i, source in enumerate((keep_ref, got_ref))
        ]
        for copy in pair:
            copy.start()
        loads.append(pair)
    stores = []
    for k, (way, m) in enumerate(jobs):
        for copy in loads[k]:
            copy.wait()
        keep, got = bufs[2 * way], bufs[2 * way + 1]
        keep[m] = (keep[m].astype(f32) + got[m].astype(f32)).astype(bf16)
        stores.append(pltpu.make_async_copy(keep.at[m], outs[k], osem.at[k]))
        stores[-1].start()
    for copy in stores:
        copy.wait()


def add_core(lay, keep, got):
    shapes = [(lay.blocks, GROUP, lay.first, WIDE)] * 2 + [(GROUP, lay.blocks, lay.second, WIDE)] * 2
    out_shape = [S(shape[1:], bf16) for shape in shapes[::2] for _ in range(shape[0] - 1)] + [S(shape[1:], bf16) for shape in shapes[::2]]
    outs = pl.pallas_call(
        functools.partial(add_core_kernel, lay),
        out_shape=out_shape,
        in_specs=[ANY] * 2,
        out_specs=[ANY] * len(out_shape),
        scratch_shapes=[V(shape, bf16) for shape in shapes]
        + [pltpu.SemaphoreType.DMA((2 * len(out_shape),)), pltpu.SemaphoreType.DMA((len(out_shape),))],
        compiler_params=pltpu.CompilerParams(vmem_limit_bytes=63 * MIB),
        name="add_core",
    )(keep, got)
    return [outs[-2], *outs[:lay.blocks - 1]], [outs[-1], *outs[lay.blocks - 1:-2]]


def summed(terms):
    return tree([x.astype(f32) for x in terms]).astype(bf16)


def adam(param, first, second, avg, grad, rate):
    root = (1.0 - beta_two**STEP) ** 0.5
    first_new = beta_one * first + (1.0 - beta_one) * grad
    second_new = beta_two * second + (1.0 - beta_two) * (grad * grad)
    below = jnp.sqrt(second_new) + adam_eps * root
    guess = pl.reciprocal(below, approx=True)
    guess = guess * (2.0 - below * guess)
    param_new = (1.0 - rate * decay_rate) * param - (rate * root / (1.0 - beta_one**STEP)) * (first_new * guess)
    avg_new = ema_keep * avg + (1.0 - ema_keep) * param_new
    return (param_new, first_new, second_new, avg_new)


def update_kernel(jobs, count, *refs):
    pieces, refs = refs[:2 * GROUP], refs[2 * GROUP:]
    states, outs, refs = refs[:count], refs[count:2 * count], refs[2 * count:]
    gsum, bufs, news, isem, osem = refs[0], refs[1:1 + 4 * len(jobs)], refs[1 + 4 * len(jobs):-2], refs[-2], refs[-1]

    def view(ref, row, rows):
        return ref if rows == ref.shape[0] else ref.at[pl.ds(row, rows)]

    loads = [
        pltpu.make_async_copy(view(states[4 * job[0] + j], job[1], job[2]), bufs[4 * i + j], isem.at[4 * i + j])
        for i, job in enumerate(jobs) for j in range(4)
    ]
    for copy in loads:
        copy.start()
    _, core, zi = position()
    zi = lax.rem(zi, GROUP)
    high = gsum.shape[0] // 2
    for side in range(2):
        at = pl.ds(pl.multiple_of(jnp.bitwise_xor(core, side) * high, 16), high)
        for k in range(GROUP):
            want = jnp.bitwise_xor(zi, k)
            for j in range(GROUP):
                @pl.when(want == j)
                def _():
                    gsum[at, j * WIDE:(j + 1) * WIDE] = pieces[side * GROUP + k][...]
    stores = []
    for i, (group, row, rows, lanes, first, lane, rate) in enumerate(jobs):
        base = first // 16 * 16
        grad = gsum[base:base + max(16, rows), lane:lane + max(lanes, 128)].astype(f32)
        grad = grad[first - base:first - base + rows, :lanes]
        for j in range(4):
            loads[4 * i + j].wait()
        new = adam(*[bufs[4 * i + j][...] for j in range(4)], grad, rate)
        for j in range(4):
            news[4 * i + j][...] = new[j]
            copy = pltpu.make_async_copy(news[4 * i + j], view(outs[4 * group + j], row, rows), osem.at[4 * i + j])
            copy.start()
            stores.append(copy)
    for copy in stores:
        copy.wait()


def update(jobs, pieces, sets):
    states = [x for group in sets for x in group]
    bufs = [V((job[2], job[3]), f32) for job in jobs for _ in range(4)]
    return pl.pallas_call(
        functools.partial(update_kernel, jobs, len(states)),
        out_shape=[S(x.shape, f32) for x in states],
        in_specs=[VMEM] * len(pieces) + [ANY] * len(states),
        out_specs=[ANY] * len(states),
        scratch_shapes=[V((2 * pieces[0].shape[0], 1024), bf16)] + bufs + bufs
        + [pltpu.SemaphoreType.DMA((len(bufs),))] * 2,
        compiler_params=pltpu.CompilerParams(vmem_limit_bytes=63 * MIB),
        name="update",
    )(*pieces, *states)


def shards(dp, fsdp, *args):
    (
        node_feat, out_cot, node_type, node_count, edge_src, edge_dst, edge_time, edge_count,
        type_weight, type_first, type_second, type_avg,
        edge_weight, edge_first, edge_second, edge_avg,
        norm_params, norm_first, norm_second, norm_avg,
        mix_params, mix_first, mix_second, mix_avg,
    ) = args
    lines = dp // 2
    lay = Layout(fsdp)

    def swap(x, axis, mask):
        size = dp if axis == "dp" else fsdp
        return lax.ppermute(x, axis, [(i, i ^ mask) for i in range(size)])

    mine = pack_half(lay, type_weight, edge_weight, norm_params)
    near = [swap(mine, "fsdp", m) for m in range(1, fsdp)]
    kinds = node_type.reshape(1, N)
    own = pack(lay, type_weight, edge_weight, norm_params)
    idx, xg = before(edge_count, kinds, edge_src, edge_dst, edge_time, node_feat)
    own, idx, xg, near[0] = lax.optimization_barrier((own, idx, xg, near[0]))
    far = [swap(x, "dp", 1) for x in near]
    mixes = [x.reshape(1, 68) for x in (mix_params, mix_first, mix_second, mix_avg)]
    layer_out, dqkv, skp, types, keep, send = layer(
        lay, node_count, edge_count, kinds, mixes[0], idx, out_cot, node_feat,
        own, near, far, xg,
    )
    got = swap(send, "dp", 1)
    chip_a, chip_b = add_core(lay, keep, got)
    dqkv, *chip_a = lax.optimization_barrier((dqkv, *chip_a))
    part_a = [chip_a[0]] + [swap(chip_a[m], "fsdp", m) for m in range(1, fsdp)]
    part_b = [chip_b[0]] + [swap(chip_b[k], "dp", 2 * k) for k in range(1, GROUP)]
    input_grad = input_gradient(kinds, dqkv, skp, types)
    input_grad, *part_a = lax.optimization_barrier((input_grad, *part_a))
    piece_a = [summed([x[k] for x in part_a]) for k in range(GROUP)]
    piece_b = [summed([x[m] for x in part_b]) for m in range(fsdp)]
    total_a = summed([piece_a[0]] + [swap(piece_a[k], "dp", 2 * k) for k in range(1, GROUP)])
    total_b = summed([piece_b[0]] + [swap(piece_b[m], "fsdp", m) for m in range(1, fsdp)])
    total = jnp.concatenate([total_a, total_b], axis=0)
    step = GROUP
    while step < lines:
        total = summed([total, swap(total, "dp", 2 * step)])
        step *= 2
    totals = [total] + [swap(total, "dp", 2 * k) for k in range(1, GROUP)]
    totals = totals + [swap(x, "dp", 1) for x in totals]
    trows, erows = lay.trows, lay.erows
    jobs = [(0, row, erows, 1024, row, 0, rates[0]) for row in range(0, trows, erows)] + [
        (1, 0, erows, 768, trows, 0, rates[1]), (2, 0, 8, lay.wide, trows, 768, rates[2]),
        (3, 0, 1, 68, trows + 8, 768, rates[3]),
    ]
    new = update(jobs, totals, [
        [type_weight, type_first, type_second, type_avg], [edge_weight, edge_first, edge_second, edge_avg],
        [norm_params, norm_first, norm_second, norm_avg], mixes,
    ])
    return (layer_out, input_grad, *new[:12], *[x.reshape(68) for x in new[12:]])


def solution(mesh):
    whole = P(("dp", "fsdp"), None)
    flat = P(("dp", "fsdp"))
    state = [P("fsdp", None)] * 8 + [P(None, "fsdp")] * 4 + [P()] * 4
    return jax.shard_map(
        functools.partial(shards, mesh.shape["dp"], mesh.shape["fsdp"]),
        mesh=mesh,
        in_specs=tuple([whole, whole, flat, flat, whole, whole, whole, flat] + state),
        out_specs=tuple([whole, whole] + state),
        check_vma=False,
    )
```

```python
import functools

import jax
import jax.numpy as jnp
import numpy as np
from jax import lax
from jax.experimental import pallas as pl
from jax.experimental.pallas import tpu as pltpu
from jax.sharding import PartitionSpec as P

D, H, DK, TYPES, REL, TB = 256, 8, 32, 4, 8, 240
N = 1024
SLOTS = 1024
EC = 512
SUB = 128
NSUB = EC // SUB
NC = 256
NODE_STEPS = 4
EDGES = REL * SLOTS
bf16 = jnp.bfloat16
f32 = jnp.float32
norm_eps = 1e-5
STEP = 10
beta_one = 0.9
beta_two = 0.999
adam_eps = 1e-08
decay_rate = 0.01
ema_keep = 0.7
rates = (0.2, 0.2, 0.6, 0.6)
score_scale = DK ** (-0.5)

SMEM = pl.BlockSpec(memory_space=pltpu.SMEM)
VMEM = pl.BlockSpec(memory_space=pltpu.VMEM)
ANY = pl.BlockSpec(memory_space=pl.ANY)
S = jax.ShapeDtypeStruct
V = pltpu.VMEM
MIB = 1 << 20
INPUT_VMEM = 62 * MIB
SECOND = 3
SOURCE, TARGET, TIME, TYPE, BUCKET = range(5)
LAYER_VMEM = 63 * MIB
GROUP = 4
WIDE = 1024 // GROUP


def nn(a, b):
    return jnp.dot(a, b, preferred_element_type=f32)


def nt(a, b):
    return lax.dot_general(a, b, (((1,), (1,)), ((), ())), preferred_element_type=f32)


def one_hot_rows(row, count):
    wide = row.shape[1]
    base = lax.broadcasted_iota(jnp.int16, (256, wide), 0)
    one, zero = jnp.ones((), bf16), jnp.zeros((), bf16)
    return jnp.concatenate(
        [jnp.where(base == (row - 256 * g).astype(jnp.int16), one, zero) for g in range(count // 256)], axis=0
    )


def head_sum(x):
    return jnp.sum(x.reshape(H, DK, x.shape[1]), axis=1)


def head_wide(x):
    return jnp.broadcast_to(x[:, None, :], (H, DK, x.shape[1])).reshape(D, x.shape[1])


def hi_lo(x):
    high = x.astype(bf16).astype(f32)
    return jnp.concatenate([high, x - high], axis=0).astype(bf16)


def eye():
    return (
        lax.broadcasted_iota(jnp.int32, (256, 256), 0) == lax.broadcasted_iota(jnp.int32, (256, 256), 1)
    ).astype(f32).astype(bf16)


def pick(masks, wide):
    out = wide[0] * masks[0:1]
    for s in range(1, TYPES):
        out = jnp.where(masks[s:s + 1] > 0, wide[s], out)
    return out


def stack(pieces):
    return pieces[0] if len(pieces) == 1 else jnp.concatenate(pieces, axis=0)


class Layout:
    def __init__(self, blocks):
        self.blocks = blocks
        self.trows, self.erows = TYPES * D // blocks, D // blocks
        self.part = self.trows + self.erows
        self.half = self.part // 2
        self.wide = D // blocks
        self.second = self.half * SECOND // 10 // 16 * 16
        self.first = self.half - self.second

    def type_rows(self, s):
        for f in range(self.blocks):
            a, b = max(s * D, f * self.trows), min((s + 1) * D, (f + 1) * self.trows)
            if a < b:
                yield f, f * self.part + a - f * self.trows, f * self.part + b - f * self.trows, a - s * D, b - s * D

    def get_type(self, ref, s, c0, c1):
        return stack([ref[a:b, c0:c1] for _, a, b, _, _ in self.type_rows(s)])

    def get_edge(self, ref, c0, c1):
        return stack([ref[f * self.part + self.trows:(f + 1) * self.part, c0:c1] for f in range(self.blocks)])

    def get_norm(self, ref):
        rows = [f * self.part + self.trows for f in range(self.blocks)]
        return jnp.concatenate([ref[a:a + 16, 768:768 + self.wide].astype(f32) for a in rows], axis=1).astype(bf16)

    def weight_copies(self, me, core, own, near, far, wpk, sems):
        out = [pltpu.make_async_copy(own, wpk.at[pl.ds(pl.multiple_of(me * self.part, 16), self.part)], sems.at[0])]
        for m in range(1, self.blocks):
            base = jnp.bitwise_xor(me, m) * self.part
            for i, (ref, side) in enumerate(((near[m - 1], core), (far[m - 1], 1 - core))):
                at = pl.ds(pl.multiple_of(base + side * self.half, 16), self.half)
                out.append(pltpu.make_async_copy(ref, wpk.at[at], sems.at[2 * m - 1 + i]))
        return out


def position():
    return lax.axis_index("fsdp"), lax.rem(lax.axis_index("dp"), 2), lax.div(lax.axis_index("dp"), 2)


def list_blocks(cnt_ref, lst_r, lst_o, lst_c):
    def put(k, r, j, c):
        lst_r[k] = r
        lst_o[k] = j
        lst_c[k] = c - j * SUB

    def pairs(r, k):
        c = cnt_ref[r]

        def one(j, k):
            put(k, r, 2 * j, c)
            put(k + 1, r, 2 * j + 1, c)
            return k + 2
        return lax.fori_loop(0, (c + SUB - 1) // SUB // 2, one, k)

    def odd(r, k):
        c = cnt_ref[r]
        blocks = (c + SUB - 1) // SUB
        put(k, r, jnp.minimum(blocks, SLOTS // SUB) - 1, c)
        return k + lax.rem(blocks, 2)
    paired = lax.fori_loop(0, REL, pairs, 0)
    total = lax.fori_loop(0, REL, odd, paired)
    for extra in range(2 * NSUB):
        put(total + extra, 0, 0, 0)
    return paired // NSUB, (total + NSUB - 1) // NSUB, total


def rows_of(ref, lst_r, lst_o, c):
    pieces = []
    for k in range(NSUB):
        r, j = lst_r[c * NSUB + k], lst_o[c * NSUB + k]
        pair = ref[pl.ds(r, 1), pl.ds(pl.multiple_of(lax.div(j, 2) * 2 * SUB, 2 * SUB), 2 * SUB)]
        pieces.append(jnp.where(lax.rem(j, 2) == 0, pair[:, :SUB], pair[:, SUB:]))
    return jnp.concatenate(pieces, axis=1)


def place(c, span=EC):
    return pl.ds(pl.multiple_of(c * EC, EC), span)


LISTS = [pltpu.SMEM((REL * SLOTS // SUB + 2 * NSUB,), jnp.int32)] * 3


def pack_half_kernel(lay, type_ref, edge_ref, norm_hbm, mine_ref, buf, low, norm_ref, isem, osem):
    _, core, _ = position()
    norm = pltpu.make_async_copy(norm_hbm, norm_ref, isem.at[5])
    norm.start()
    rows = lay.half // 5
    for side in range(2):
        @pl.when(core == side)
        def _():
            loads = []
            for i in range(5):
                if side == 1 and i >= 3:
                    source, to = edge_ref.at[pl.ds((i - 3) * rows, rows)], buf.at[pl.ds(i * rows, rows), pl.ds(0, 768)]
                else:
                    source, to = type_ref.at[pl.ds(side * lay.half + i * rows, rows)], buf.at[pl.ds(i * rows, rows)]
                loads.append(pltpu.make_async_copy(source, to, isem.at[i]))
                loads[-1].start()
            norm.wait()
            if side == 1:
                corner = jnp.concatenate([norm_ref[...], jnp.zeros((8, 256 - lay.wide), f32)], axis=1)
                buf[3 * rows:, 768:] = jnp.concatenate([corner, jnp.zeros((lay.erows - 8, 256), f32)], axis=0)
            stores = []
            for i in range(5):
                loads[i].wait()
                at = slice(i * rows, (i + 1) * rows)
                low[at] = buf[at].astype(bf16)
                stores.append(pltpu.make_async_copy(low.at[pl.ds(i * rows, rows)], mine_ref.at[pl.ds(i * rows, rows)], osem.at[i]))
                stores[-1].start()
            for copy in stores:
                copy.wait()


def pack_half(lay, type_weight, edge_weight, norm_params):
    return pl.pallas_call(
        functools.partial(pack_half_kernel, lay),
        out_shape=S((lay.half, 1024), bf16),
        in_specs=[ANY] * 3,
        out_specs=ANY,
        scratch_shapes=[
            V((lay.half, 1024), f32), V((lay.half, 1024), bf16), V((8, lay.wide), f32),
            pltpu.SemaphoreType.DMA((6,)), pltpu.SemaphoreType.DMA((5,)),
        ],
        compiler_params=pltpu.CompilerParams(vmem_limit_bytes=63 * MIB),
        name="pack_half",
    )(type_weight, edge_weight, norm_params)


def pack_kernel(lay, type_ref, edge_ref, norm_ref, own_ref):
    own_ref[0:lay.trows, :] = type_ref[...].astype(bf16)
    own_ref[lay.trows:, 0:768] = edge_ref[...].astype(bf16)
    corner = jnp.concatenate([norm_ref[...], jnp.zeros((8, 256 - lay.wide), f32)], axis=1)
    own_ref[lay.trows:, 768:] = jnp.concatenate([corner, jnp.zeros((lay.erows - 8, 256), f32)], axis=0).astype(bf16)


def pack(lay, type_weight, edge_weight, norm_params):
    return pl.pallas_call(
        functools.partial(pack_kernel, lay),
        out_shape=S((lay.part, 1024), bf16),
        compiler_params=pltpu.CompilerParams(vmem_limit_bytes=63 * MIB),
        name="pack",
    )(type_weight, edge_weight, norm_params)


def before_kernel(cnt_ref, kinds_ref, src_ref, dst_ref, tim_ref, feat_ref, idx_ref, xg_ref, typ_ref, lst_r, lst_o, lst_c):
    _, chunks, _ = list_blocks(cnt_ref, lst_r, lst_o, lst_c)
    src = src_ref[...]
    for j in range(SLOTS // 128):
        idx = src[:, j * 128:(j + 1) * 128]
        low = jnp.bitwise_and(idx, 127)
        high = jnp.right_shift(idx, 7)
        acc = jnp.zeros((8, 128), jnp.int32)
        for k in range(N // 128):
            row = jnp.broadcast_to(kinds_ref[:, k * 128:(k + 1) * 128], (8, 128))
            acc = jnp.where(high == k, jnp.take_along_axis(row, low, axis=1), acc)
        typ_ref[:, j * 128:(j + 1) * 128] = acc
    ft = nt(eye(), feat_ref[...]).astype(bf16)

    def one(c, _):
        src, dst, tim, typ = [rows_of(ref, lst_r, lst_o, c) for ref in (src_ref, dst_ref, tim_ref, typ_ref)]
        idx_ref[pl.ds(pl.multiple_of(c * 8, 8), 8), :] = jnp.concatenate(
            [src, dst, tim, typ, typ * 256 + tim, src, src, src], axis=0
        )
        xg_ref[:, place(c)] = nn(ft, one_hot_rows(src, N)).astype(bf16)
        return 0

    def two(c, _):
        one(2 * c, 0)
        one(2 * c + 1, 0)
        return 0

    lax.fori_loop(0, (chunks + 1) // 2, two, 0)


def before(cnt, kinds, src, dst, tim, feat):
    return pl.pallas_call(
        before_kernel,
        out_shape=(S((EDGES // EC * 8, EC), jnp.int32), S((D, EDGES), bf16)),
        in_specs=[SMEM] + [VMEM] * 5,
        scratch_shapes=[V((REL, SLOTS), jnp.int32)] + LISTS,
        compiler_params=pltpu.CompilerParams(vmem_limit_bytes=63 * MIB),
        cost_estimate=pl.CostEstimate(flops=2 * D * N * EDGES, bytes_accessed=6 * MIB, transcendentals=0),
        name="before",
    )(cnt, kinds, src, dst, tim, feat)


def layer_kernel(lay, *refs):
    nb = lay.blocks - 1
    (
        live_ref, cnt_ref, kinds_hbm, mix_hbm, idx_hbm, emb_hbm, cot_hbm, feat_hbm, own_ref,
    ) = refs[:9]
    near, far, xg_hbm = refs[9:9 + nb], refs[9 + nb:9 + 2 * nb], refs[9 + 2 * nb]
    (
        out_ref, dqkv_ref, skp_ref, types_ref, keep_ref, send_ref,
        lst_r, lst_o, lst_c,
        wpk, gpack, gout, gnorm, gskip, xg, low, cot_ref, feat_ref, kinds_ref, mix_ref, idx_ref, emb_ref,
        wt, xcat, qt, rte, dn_buf, dkve_buf, mu,
        bda, bdat, bdm, bdmt, ga, gm, dmu,
        kve, qe, msg, wexp, raws,
        num, dnum, dqkv, dtkv, skp,
        wsem, xsem, osem, gsem,
    ) = refs[10 + 2 * nb:]
    me, core, zi = position()
    zi = lax.rem(zi, GROUP)
    small = [
        pltpu.make_async_copy(source, to, xsem.at[3 + i])
        for i, (source, to) in enumerate(
            ((kinds_hbm, kinds_ref), (mix_hbm, mix_ref), (feat_hbm, feat_ref), (idx_hbm, idx_ref), (emb_hbm, emb_ref))
        )
    ]
    weights = lay.weight_copies(me, core, own_ref, near, far, wpk, wsem)
    for copy in small + weights:
        copy.start()
    first, rest = pl.ds(0, EC), pl.ds(EC, EDGES - EC)
    xg_first = pltpu.make_async_copy(xg_hbm.at[:, first], xg.at[:, first], xsem.at[0])
    xg_rest = pltpu.make_async_copy(xg_hbm.at[:, rest], xg.at[:, rest], xsem.at[1])
    xg_first.start()
    cot_copy = pltpu.make_async_copy(cot_hbm, cot_ref, xsem.at[2])

    ident = eye()
    whole, chunks, total = list_blocks(cnt_ref, lst_r, lst_o, lst_c)

    def row(c, k):
        return idx_ref[pl.ds(pl.multiple_of(c * 8, 8), 8), :][k:k + 1]

    for ref in (num, dqkv, dtkv, ga, gm, dmu, gnorm, gskip, gout):
        ref[...] = jnp.zeros_like(ref)
    dkve_buf[...] = jnp.zeros_like(dkve_buf)

    small[0].wait()
    small[1].wait()
    mix = jnp.broadcast_to(mix_ref[...].astype(bf16).astype(f32), (8, 68))
    lanes68 = lax.broadcasted_iota(jnp.int32, (8, 68), 1)
    line68 = lax.broadcasted_iota(jnp.int32, (8, 68), 0)

    def column(first):
        return jnp.sum(jnp.where(lanes68 == first + line68, mix, 0.0), axis=1, keepdims=True)

    for r in range(REL):
        mu[r] = jnp.broadcast_to(column(r * H) * score_scale, (H, 128))
    skip_col = column(REL * H)

    kinds = kinds_ref[...]
    masks = (lax.broadcasted_iota(jnp.int32, (8, N), 0) == kinds).astype(f32)
    small[2].wait()
    featt = nt(ident, feat_ref[...])
    for s in range(TYPES):
        xcat[s * D:(s + 1) * D, :] = (featt * masks[s:s + 1]).astype(bf16)
    for copy in weights + small[3:]:
        copy.wait()
    xg_rest.start()
    cot_copy.start()
    finish = [
        pltpu.make_async_copy(
            wpk.at[pl.ds(a, b - a), pl.ds(0, 3 * D)], types_ref.at[pl.ds(s * D + c, d - c)], osem.at[3 + f]
        )
        for s in range(TYPES) for f, a, b, c, d in lay.type_rows(s)
    ]
    for copy in finish:
        copy.start()

    lane = lax.broadcasted_iota(jnp.int32, (D, 128), 1)
    rowi = lax.broadcasted_iota(jnp.int32, (D, 128), 0)
    on_diag = (lane // DK) == (rowi // DK) % 4
    zeros = jnp.zeros((128, 128), f32)
    for p in range(4):
        x = lay.get_edge(wpk, p * 128, (p + 1) * 128).astype(f32)
        rolled = [x if k == 0 else pltpu.roll(x, 32 * k, 1) for k in range(4)]
        for g in range(4):
            r, m = 2 * p + g // 2, g % 2
            t = jnp.concatenate([rolled[(h % 4 - g) % 4][h * 32:(h + 1) * 32] for h in range(H)], axis=0)
            t = jnp.where(on_diag, t, 0.0)
            for ref, a, b in (
                (bdm if m else bda, t[:128], t[128:]), (bdmt if m else bdat, t[:128].T, t[128:].T)
            ):
                ref[r] = jnp.concatenate(
                    [jnp.concatenate([a, zeros], axis=1), jnp.concatenate([zeros, b], axis=1)], axis=0
                ).astype(bf16)

    for cb in range(4):
        for s in range(4):
            wt[cb * 256:(cb + 1) * 256, s * 256:(s + 1) * 256] = nt(
                ident, lay.get_type(wpk, s, cb * 256, (cb + 1) * 256)
            ).astype(bf16)
    qt[...] = nn(wt[:D, :], xcat[...]).astype(bf16)
    wet = nt(ident, lay.get_edge(wpk, 512, 768)).astype(bf16)
    rte[...] = nt(wet, emb_ref[...]).astype(bf16)

    def mu_of(c, span):
        return jnp.concatenate([mu[lst_r[c * NSUB + k]] for k in range(span // SUB)], axis=1)

    def blocks_of(c, wide, span):
        return [(lst_r[c * NSUB + k * (wide // SUB)], slice(k * wide, (k + 1) * wide)) for k in range(span // wide)]

    def lookup(c):
        rt = nn(rte[...], one_hot_rows(row(c, TIME), 256))
        return (xg[:, place(c)].astype(f32) + rt).astype(bf16)

    def lookup_q(c):
        qe[:, place(c)] = nn(qt[...], one_hot_rows(row(c, TARGET), N)).astype(bf16)

    def project(c, xe):
        cu = row(c, TYPE)
        zero = jnp.zeros((), bf16)
        xm = jnp.concatenate([jnp.where(cu == s, xe, zero) for s in range(TYPES)], axis=0)
        kve[:, place(c)] = nn(wt[D:3 * D, :], xm).astype(bf16)

    def forward(wide, more, c, _, span=EC):
        at = place(c, span)
        kv_e = kve[:, at]
        q_e = qe[:, at].astype(f32)
        ks, ms = [], []
        for r, sl in blocks_of(c, wide, span):
            ks.append(nn(bdat[r], kv_e[:D, sl]))
            ms.append(nn(bdmt[r], kv_e[D:, sl]))
        ka = jnp.concatenate(ks, axis=1)
        me_ = jnp.concatenate(ms, axis=1)
        xe = lookup(c + 1) if more else None
        xg[:, at] = ka.astype(bf16)
        msg[:, at] = me_.astype(bf16)
        raw = head_sum(ka * q_e)
        raws[:, at] = raw
        lanes = lax.broadcasted_iota(jnp.int32, (H, SUB), 1)
        w = jnp.exp(raw * mu_of(c, span))
        w = jnp.concatenate(
            [jnp.where(lanes < lst_c[c * NSUB + k], w[:, k * SUB:(k + 1) * SUB], 0.0) for k in range(span // SUB)], axis=1
        )
        wexp[:, at] = w
        wm = (head_wide(w) * me_).astype(bf16)
        if more:
            lookup_q(c + 1)
        num[...] += nt(jnp.concatenate([wm, hi_lo(w)], axis=0), one_hot_rows(row(c, TARGET)[:, :span], N))
        if more:
            project(c + 1, xe)
        return 0

    xg_first.wait()
    project(0, lookup(0))
    lookup_q(0)
    xg_rest.wait()
    whole, last = jnp.minimum(whole, chunks - 1), chunks - 1
    lax.fori_loop(0, whole, functools.partial(forward, 2 * SUB, True), 0)
    lax.fori_loop(whole, last, functools.partial(forward, SUB, True), 0)
    few = total - last * NSUB <= NSUB // 2

    @pl.when(few)
    def _():
        forward(SUB, False, last, 0, EC // 2)

    @pl.when(jnp.logical_not(few))
    def _():
        forward(SUB, False, last, 0)

    cot_copy.wait()
    nwt = nt(ident, lay.get_norm(wpk)).astype(bf16)
    out_rows = jnp.concatenate([lay.get_type(wpk, s, 3 * D, 4 * D) for s in range(TYPES)], axis=1)

    def nodes(c):
        at = pl.ds(pl.multiple_of(c * NC, NC), NC)
        mk = (lax.broadcasted_iota(jnp.int32, (8, NC), 0) == kinds_ref[:, at]).astype(f32)
        live = (lax.broadcasted_iota(jnp.int32, (1, NC), 1) + c * NC < live_ref[0]).astype(f32)
        den = num[D:D + H, at] + num[D + H:, at] + (1.0 - live)
        inv_den = head_wide(1.0 / den)
        agg = num[:D, at] * inv_den
        phi = 0.5 * (1.0 + lax.erf(agg * (0.5 ** 0.5)))
        act = (agg * phi).astype(bf16)
        mkl = mk.astype(bf16)
        acat = jnp.concatenate([act * mkl[s:s + 1] for s in range(TYPES)], axis=0)
        yield
        trans = nn(wt[3 * D:, :], acat)
        yield
        alpha = 1.0 / (1.0 + jnp.exp(-jnp.sum(mk * skip_col, axis=0, keepdims=True)))
        ft = nt(ident, feat_ref[at, :])
        none = jnp.zeros((4, NC), f32)
        oh16 = jnp.concatenate([mk[0:4], none, none, none], axis=0).astype(bf16)
        gain = nn(nwt, oh16)
        bias = nn(nwt, jnp.concatenate([none, mk[0:4], none, none], axis=0).astype(bf16))
        dy = live * nt(ident, cot_ref[at, :])
        res = alpha * trans + (1.0 - alpha) * ft
        mean = jnp.mean(res, axis=0, keepdims=True)
        cen = res - mean
        inv = lax.rsqrt(jnp.mean(cen * cen, axis=0, keepdims=True) + norm_eps)
        nrm = cen * inv
        cot_ref[at, :] = (live * (nrm * gain + bias)).T.astype(bf16)
        dyn = dy * nrm
        dyn_hi = dyn.astype(bf16)
        dyn_lo = (dyn - dyn_hi.astype(f32)).astype(bf16)
        gnorm[0:4, :] += (nt(oh16, dyn_hi) + nt(oh16, dyn_lo))[0:4]
        gnorm[4:8, :] += nt(oh16, dy.astype(bf16))[0:4]
        dn = dy * gain
        dres = inv * (dn - jnp.mean(dn, axis=0, keepdims=True) - nrm * jnp.mean(dn * nrm, axis=0, keepdims=True))
        dtr = (alpha * dres).astype(bf16)
        yield
        dact = nn(out_rows, jnp.concatenate([dtr * mkl[s:s + 1] for s in range(TYPES)], axis=0))
        yield
        skp[:, at] = (1.0 - alpha) * dres
        dal = jnp.sum(dres * (trans - ft), axis=0, keepdims=True) * alpha * (1.0 - alpha)
        gskip[...] += jnp.broadcast_to(jnp.sum(mk * dal, axis=1, keepdims=True), (8, 128))
        gout[...] += nt(acat, dtr)
        dagg = dact * (phi + agg * (jnp.exp(-0.5 * agg * agg) * (0.5 / np.pi) ** 0.5))
        dnum[0:D, at] = (dagg * inv_den).astype(bf16)
        dnum[D:, at] = hi_lo(-head_sum(dagg * agg) / den)
        yield

    def node_steps(c, _):
        for _ in zip(*[nodes(NODE_STEPS * c + i) for i in range(NODE_STEPS)]):
            pass
        return 0

    lax.fori_loop(0, N // NC // NODE_STEPS, node_steps, 0)
    for i, (source, to) in enumerate(((cot_ref, out_ref), (skp, skp_ref))):
        finish.append(pltpu.make_async_copy(source, to, osem.at[i]))
        finish[-1].start()

    def gather_back(c):
        dn_buf[...] = nn(dnum[...], one_hot_rows(row(c, TARGET), N))

    def scatter_nodes(c, dkve):
        dqkv[:, D:] += nt(one_hot_rows(row(c, SOURCE)[:, :dkve.shape[1]], N), dkve)

    def scatter_times(c, dkve):
        dtkv[...] += nt(one_hot_rows(row(c, BUCKET)[:, :dkve.shape[1]], 1024), dkve)

    def scatter_back(c, span=EC):
        scatter_times(c, dkve_buf[:, :span])
        scatter_nodes(c, dkve_buf[:, :span])

    def backward(wide, more, c, _, span=EC):
        at = place(c, span)
        before, dkve = jnp.maximum(c - 1, 0), dkve_buf[...]
        scatter_times(before, dkve)
        dn_e = dn_buf[:D, :span]
        w = wexp[:, at]
        dw = head_sum(dn_e * msg[:, at].astype(f32)) + dn_buf[D:D + H, :span] + dn_buf[D + H:, :span]
        ds = dw * w
        dsr = ds * raws[:, at]
        ss = head_wide(ds * mu_of(c, span))
        dka = (ss * qe[:, at].astype(f32)).astype(bf16)
        dms = (head_wide(w) * dn_e).astype(bf16)
        dqe = (ss * xg[:, at].astype(f32)).astype(bf16)
        for r, sl in blocks_of(c, wide, span):
            dkve_buf[0:D, sl] = nn(bda[r], dka[:, sl]).astype(bf16)
            dkve_buf[D:, sl] = nn(bdm[r], dms[:, sl]).astype(bf16)
        for r, sl in blocks_of(c, wide, span):
            at_k = pl.ds(pl.multiple_of(c * EC + sl.start, SUB), wide)
            gak = nt(kve[0:D, at_k], dka[:, sl])
            gmk = nt(kve[D:, at_k], dms[:, sl])
            ga[r, 0:128] += gak[0:128, 0:128]
            ga[r, 128:] += gak[128:, 128:]
            gm[r, 0:128] += gmk[0:128, 0:128]
            gm[r, 128:] += gmk[128:, 128:]
            dmu[r] += sum(dsr[:, k:k + 128] for k in range(sl.start, sl.stop, 128))
        dqkv[:, :D] += nt(one_hot_rows(row(c, TARGET)[:, :span], N), dqe)
        scatter_nodes(before, dkve)
        if more:
            gather_back(c + 1)
        return 0

    gather_back(0)
    def backward_pair(c, _):
        backward(2 * SUB, True, 2 * c, 0)
        backward(2 * SUB, True, 2 * c + 1, 0)
        return 0

    lax.fori_loop(0, whole // 2, backward_pair, 0)
    lax.fori_loop(whole // 2 * 2, whole, functools.partial(backward, 2 * SUB, True), 0)
    lax.fori_loop(whole, last, functools.partial(backward, SUB, True), 0)

    @pl.when(few)
    def _():
        backward(SUB, False, last, 0, EC // 2)
        scatter_back(last, EC // 2)

    @pl.when(jnp.logical_not(few))
    def _():
        backward(SUB, False, last, 0)
        scatter_back(last)


    low[...] = dqkv[...].astype(bf16)
    last = pltpu.make_async_copy(low, dqkv_ref, osem.at[2])
    last.start()
    finish.append(last)
    dt = dtkv[...].astype(bf16)
    drte = jnp.zeros((D, 256), f32)
    for s in range(TYPES):
        drte = drte + nt(lay.get_type(wpk, s, D, 3 * D), dt[s * 256:(s + 1) * 256, :])

    spots = [jnp.bitwise_xor(zi, j) for j in range(GROUP)]

    def put_edge(c0, value):
        lanes = slice(c0 % WIDE, c0 % WIDE + value.shape[1])
        for f in range(lay.blocks):
            gpack[spots[c0 // WIDE], f * lay.part + lay.trows:(f + 1) * lay.part, lanes] = value[
                f * lay.erows:(f + 1) * lay.erows
            ].astype(bf16)

    for p in range(4):
        acc = jnp.zeros((D, 128), f32)
        for g in range(4):
            r, m = 2 * p + g // 2, g % 2
            t = jnp.where(on_diag, (gm if m else ga)[r], 0.0)
            rolled = [t if k == 0 else pltpu.roll(t, 32 * k, 1) for k in range(4)]
            acc = acc + jnp.concatenate([rolled[(g - h % 4) % 4][h * 32:(h + 1) * 32] for h in range(H)], axis=0)
        put_edge(p * 128, acc)
    embt = nt(ident, emb_ref[...]).astype(bf16)
    put_edge(512, nt(embt, drte.astype(bf16)))

    lane8 = lax.broadcasted_iota(jnp.int32, (8, 256), 1)
    line8 = lax.broadcasted_iota(jnp.int32, (8, 256), 0)
    mixg = jnp.where(lane8 == REL * H + line8, gskip[:, 0:1], 0.0)
    for r in range(REL):
        col = jnp.sum(dmu[r], axis=1, keepdims=True) * score_scale
        mixg = mixg + jnp.where(lane8 == r * H + line8, col, 0.0)
    mixg = jnp.broadcast_to(jnp.sum(mixg, axis=0, keepdims=True), (8, 256))
    for f in range(lay.blocks):
        corner = jnp.concatenate(
            [gnorm[:, f * lay.wide:(f + 1) * lay.wide], jnp.zeros((8, 256 - lay.wide), f32)], axis=1
        )
        small = jnp.concatenate([corner, mixg, jnp.zeros((lay.erows - 16, 256), f32)], axis=0)
        gpack[spots[3], f * lay.part + lay.trows:(f + 1) * lay.part, :] = small.astype(bf16)

    done = 0
    for s in range(TYPES):
        g = nn(xcat[s * D:(s + 1) * D, :], low[...])
        g_kv = g[:, D:] + nn(rte[...], dt[s * 256:(s + 1) * 256, :])
        values = [g[:, :D], g_kv[:, :D], g_kv[:, D:], gout[s * D:(s + 1) * D, :]]
        for _, a, b, c, d in lay.type_rows(s):
            for j in range(GROUP):
                gpack[spots[j], a:b, :] = values[j][c:d].astype(bf16)
        while done < lay.blocks and (done + 1) * lay.trows <= (s + 1) * D:
            m = jnp.bitwise_xor(me, done)
            for i, (ref, side) in enumerate(((send_ref, 1 - core), (keep_ref, core))):
                at = pl.ds(pl.multiple_of(done * lay.part + side * lay.half, 16), lay.half)
                copy = pltpu.make_async_copy(gpack.at[:, at], ref.at[m], gsem.at[2 * done + i])
                copy.start()
                finish.append(copy)
            done += 1
    for copy in finish:
        copy.wait()


def emb_table():
    steps = np.arange(TB, dtype=np.float32)[:, None]
    col = np.arange(D)
    freq = np.exp(-np.log(np.float32(10000.0)) * (2 * (col // 2)).astype(np.float32) / np.float32(D)).astype(np.float32)
    angle = steps * freq[None]
    tab = np.where(col[None] % 2 == 0, np.sin(angle), np.cos(angle)).astype(np.float32)
    return np.concatenate([tab, np.zeros((256 - TB, D), np.float32)], axis=0)


def layer(lay, live, cnt, kinds, mix, idx, cot, feat, own, near, far, xg):
    sums = S((lay.blocks, GROUP, lay.half, WIDE), bf16)
    edges = lambda rows, kind: V((rows, EDGES), kind)
    return pl.pallas_call(
        functools.partial(layer_kernel, lay),
        out_shape=[S((N, D), bf16), S((N, 3 * D), bf16), S((D, N), f32), S((TYPES * D, 3 * D), bf16), sums, sums],
        in_specs=[SMEM, SMEM] + [ANY] * (2 * lay.blocks + 6),
        out_specs=[ANY] * 6,
        scratch_shapes=LISTS + [
            V((lay.blocks * lay.part, 1024), bf16), V((GROUP, lay.blocks * lay.part, WIDE), bf16), V((TYPES * D, D), f32),
            V((8, D), f32), V((8, 128), f32), edges(D, bf16), V((N, 3 * D), bf16), V((N, D), bf16), V((N, D), bf16),
            V(kinds.shape, jnp.int32), V(mix.shape, f32), V(idx.shape, jnp.int32), V((256, D), bf16),
            V((4 * D, TYPES * D), bf16), V((TYPES * D, N), bf16), V((D, N), bf16), V((D, 256), bf16),
            V((D + 16, EC), f32), V((2 * D, EC), bf16), V((REL, H, 128), f32),
            V((8, D, D), bf16), V((8, D, D), bf16), V((8, D, D), bf16), V((8, D, D), bf16),
            V((8, D, 128), f32), V((8, D, 128), f32), V((8, 8, 128), f32),
            edges(2 * D, bf16), edges(D, bf16), V((D, REL * SLOTS), bf16),
            V((H, REL * SLOTS), f32), V((H, REL * SLOTS), f32),
            V((D + 16, N), f32), V((D + 16, N), bf16), V((N, 3 * D), f32), V((TYPES * 256, 2 * D), f32), V((D, N), f32),
            pltpu.SemaphoreType.DMA((2 * lay.blocks - 1,)), pltpu.SemaphoreType.DMA((8,)),
            pltpu.SemaphoreType.DMA((3 + lay.blocks,)), pltpu.SemaphoreType.DMA((2 * lay.blocks,)),
        ],
        compiler_params=pltpu.CompilerParams(vmem_limit_bytes=LAYER_VMEM),
        cost_estimate=pl.CostEstimate(flops=60 * 10**9, bytes_accessed=16 * MIB, transcendentals=0),
        name="layer",
    )(live, cnt, kinds, mix, idx, jnp.asarray(emb_table(), bf16), cot, feat, own, *near, *far, xg)


def input_kernel(kinds_ref, dqkv_ref, skp_ref, types_ref, out_ref):
    masks = (lax.broadcasted_iota(jnp.int32, (8, N), 0) == kinds_ref[...]).astype(f32)
    for c in range(N // NC):
        at = slice(c * NC, (c + 1) * NC)
        proj = pick(masks[:, at], [nt(types_ref[s * D:(s + 1) * D, :], dqkv_ref[at, :]) for s in range(TYPES)])
        out_ref[at, :] = (proj + skp_ref[:, at]).T.astype(bf16)


def input_gradient(kinds, dqkv, skp, types):
    return pl.pallas_call(
        input_kernel,
        out_shape=S((N, D), bf16),
        compiler_params=pltpu.CompilerParams(vmem_limit_bytes=INPUT_VMEM),
        cost_estimate=pl.CostEstimate(flops=2 * N * D * D * 12, bytes_accessed=6 * MIB, transcendentals=0),
        name="input_gradient",
    )(kinds, dqkv, skp, types)


def tree(terms):
    while len(terms) > 1:
        terms = [terms[i] + terms[i + 1] for i in range(0, len(terms), 2)]
    return terms[0]


def add_core_kernel(lay, keep_ref, got_ref, *refs):
    ways = ((lay.blocks, lambda ref, m: ref.at[m, :, pl.ds(0, lay.first)]),
            (GROUP, lambda ref, m: ref.at[:, m, pl.ds(lay.first, lay.second)]))
    jobs = [(way, m) for way in range(2) for m in range(1, ways[way][0])] + [(0, 0), (1, 0)]
    outs, bufs, isem, osem = refs[:len(jobs)], refs[len(jobs):-2], *refs[-2:]
    loads = []
    for k, (way, m) in enumerate(jobs):
        pair = [
            pltpu.make_async_copy(ways[way][1](source, m), bufs[2 * way + i].at[m], isem.at[2 * k + i])
            for i, source in enumerate((keep_ref, got_ref))
        ]
        for copy in pair:
            copy.start()
        loads.append(pair)
    stores = []
    for k, (way, m) in enumerate(jobs):
        for copy in loads[k]:
            copy.wait()
        keep, got = bufs[2 * way], bufs[2 * way + 1]
        keep[m] = (keep[m].astype(f32) + got[m].astype(f32)).astype(bf16)
        stores.append(pltpu.make_async_copy(keep.at[m], outs[k], osem.at[k]))
        stores[-1].start()
    for copy in stores:
        copy.wait()


def add_core(lay, keep, got):
    shapes = [(lay.blocks, GROUP, lay.first, WIDE)] * 2 + [(GROUP, lay.blocks, lay.second, WIDE)] * 2
    out_shape = [S(shape[1:], bf16) for shape in shapes[::2] for _ in range(shape[0] - 1)] + [S(shape[1:], bf16) for shape in shapes[::2]]
    outs = pl.pallas_call(
        functools.partial(add_core_kernel, lay),
        out_shape=out_shape,
        in_specs=[ANY] * 2,
        out_specs=[ANY] * len(out_shape),
        scratch_shapes=[V(shape, bf16) for shape in shapes]
        + [pltpu.SemaphoreType.DMA((2 * len(out_shape),)), pltpu.SemaphoreType.DMA((len(out_shape),))],
        compiler_params=pltpu.CompilerParams(vmem_limit_bytes=63 * MIB),
        name="add_core",
    )(keep, got)
    return [outs[-2], *outs[:lay.blocks - 1]], [outs[-1], *outs[lay.blocks - 1:-2]]


def summed(terms):
    return tree([x.astype(f32) for x in terms]).astype(bf16)


def adam(param, first, second, avg, grad, rate):
    root = (1.0 - beta_two**STEP) ** 0.5
    first_new = beta_one * first + (1.0 - beta_one) * grad
    second_new = beta_two * second + (1.0 - beta_two) * (grad * grad)
    below = jnp.sqrt(second_new) + adam_eps * root
    guess = pl.reciprocal(below, approx=True)
    guess = guess * (2.0 - below * guess)
    param_new = (1.0 - rate * decay_rate) * param - (rate * root / (1.0 - beta_one**STEP)) * (first_new * guess)
    avg_new = ema_keep * avg + (1.0 - ema_keep) * param_new
    return (param_new, first_new, second_new, avg_new)


def update_kernel(jobs, count, *refs):
    pieces, refs = refs[:2 * GROUP], refs[2 * GROUP:]
    states, outs, refs = refs[:count], refs[count:2 * count], refs[2 * count:]
    gsum, bufs, news, isem, osem = refs[0], refs[1:1 + 4 * len(jobs)], refs[1 + 4 * len(jobs):-2], refs[-2], refs[-1]

    def view(ref, row, rows):
        return ref if rows == ref.shape[0] else ref.at[pl.ds(row, rows)]

    loads = [
        pltpu.make_async_copy(view(states[4 * job[0] + j], job[1], job[2]), bufs[4 * i + j], isem.at[4 * i + j])
        for i, job in enumerate(jobs) for j in range(4)
    ]
    for copy in loads:
        copy.start()
    _, core, zi = position()
    zi = lax.rem(zi, GROUP)
    high = gsum.shape[0] // 2
    for side in range(2):
        at = pl.ds(pl.multiple_of(jnp.bitwise_xor(core, side) * high, 16), high)
        for k in range(GROUP):
            want = jnp.bitwise_xor(zi, k)
            for j in range(GROUP):
                @pl.when(want == j)
                def _():
                    gsum[at, j * WIDE:(j + 1) * WIDE] = pieces[side * GROUP + k][...]
    stores = []
    for i, (group, row, rows, lanes, first, lane, rate) in enumerate(jobs):
        base = first // 16 * 16
        grad = gsum[base:base + max(16, rows), lane:lane + max(lanes, 128)].astype(f32)
        grad = grad[first - base:first - base + rows, :lanes]
        for j in range(4):
            loads[4 * i + j].wait()
        new = adam(*[bufs[4 * i + j][...] for j in range(4)], grad, rate)
        for j in range(4):
            news[4 * i + j][...] = new[j]
            copy = pltpu.make_async_copy(news[4 * i + j], view(outs[4 * group + j], row, rows), osem.at[4 * i + j])
            copy.start()
            stores.append(copy)
    for copy in stores:
        copy.wait()


def update(jobs, pieces, sets):
    states = [x for group in sets for x in group]
    bufs = [V((job[2], job[3]), f32) for job in jobs for _ in range(4)]
    return pl.pallas_call(
        functools.partial(update_kernel, jobs, len(states)),
        out_shape=[S(x.shape, f32) for x in states],
        in_specs=[VMEM] * len(pieces) + [ANY] * len(states),
        out_specs=[ANY] * len(states),
        scratch_shapes=[V((2 * pieces[0].shape[0], 1024), bf16)] + bufs + bufs
        + [pltpu.SemaphoreType.DMA((len(bufs),))] * 2,
        compiler_params=pltpu.CompilerParams(vmem_limit_bytes=63 * MIB),
        name="update",
    )(*pieces, *states)


def shards(dp, fsdp, *args):
    (
        node_feat, out_cot, node_type, node_count, edge_src, edge_dst, edge_time, edge_count,
        type_weight, type_first, type_second, type_avg,
        edge_weight, edge_first, edge_second, edge_avg,
        norm_params, norm_first, norm_second, norm_avg,
        mix_params, mix_first, mix_second, mix_avg,
    ) = args
    lines = dp // 2
    lay = Layout(fsdp)

    def swap(x, axis, mask):
        size = dp if axis == "dp" else fsdp
        return lax.ppermute(x, axis, [(i, i ^ mask) for i in range(size)])

    mine = pack_half(lay, type_weight, edge_weight, norm_params)
    near = [swap(mine, "fsdp", m) for m in range(1, fsdp)]
    kinds = node_type.reshape(1, N)
    own = pack(lay, type_weight, edge_weight, norm_params)
    idx, xg = before(edge_count, kinds, edge_src, edge_dst, edge_time, node_feat)
    own, idx, xg, near[0] = lax.optimization_barrier((own, idx, xg, near[0]))
    far = [swap(x, "dp", 1) for x in near]
    mixes = [x.reshape(1, 68) for x in (mix_params, mix_first, mix_second, mix_avg)]
    layer_out, dqkv, skp, types, keep, send = layer(
        lay, node_count, edge_count, kinds, mixes[0], idx, out_cot, node_feat,
        own, near, far, xg,
    )
    got = swap(send, "dp", 1)
    chip_a, chip_b = add_core(lay, keep, got)
    dqkv, *chip_a = lax.optimization_barrier((dqkv, *chip_a))
    part_a = [chip_a[0]] + [swap(chip_a[m], "fsdp", m) for m in range(1, fsdp)]
    part_b = [chip_b[0]] + [swap(chip_b[k], "dp", 2 * k) for k in range(1, GROUP)]
    input_grad = input_gradient(kinds, dqkv, skp, types)
    input_grad, *part_a = lax.optimization_barrier((input_grad, *part_a))
    piece_a = [summed([x[k] for x in part_a]) for k in range(GROUP)]
    piece_b = [summed([x[m] for x in part_b]) for m in range(fsdp)]
    total_a = summed([piece_a[0]] + [swap(piece_a[k], "dp", 2 * k) for k in range(1, GROUP)])
    total_b = summed([piece_b[0]] + [swap(piece_b[m], "fsdp", m) for m in range(1, fsdp)])
    total = jnp.concatenate([total_a, total_b], axis=0)
    step = GROUP
    while step < lines:
        total = summed([total, swap(total, "dp", 2 * step)])
        step *= 2
    totals = [total] + [swap(total, "dp", 2 * k) for k in range(1, GROUP)]
    totals = totals + [swap(x, "dp", 1) for x in totals]
    trows, erows = lay.trows, lay.erows
    jobs = [(0, row, erows, 1024, row, 0, rates[0]) for row in range(0, trows, erows)] + [
        (1, 0, erows, 768, trows, 0, rates[1]), (2, 0, 8, lay.wide, trows, 768, rates[2]),
        (3, 0, 1, 68, trows + 8, 768, rates[3]),
    ]
    new = update(jobs, totals, [
        [type_weight, type_first, type_second, type_avg], [edge_weight, edge_first, edge_second, edge_avg],
        [norm_params, norm_first, norm_second, norm_avg], mixes,
    ])
    return (layer_out, input_grad, *new[:12], *[x.reshape(68) for x in new[12:]])


def solution(mesh):
    whole = P(("dp", "fsdp"), None)
    flat = P(("dp", "fsdp"))
    state = [P("fsdp", None)] * 8 + [P(None, "fsdp")] * 4 + [P()] * 4
    return jax.shard_map(
        functools.partial(shards, mesh.shape["dp"], mesh.shape["fsdp"]),
        mesh=mesh,
        in_specs=tuple([whole, whole, flat, flat, whole, whole, whole, flat] + state),
        out_specs=tuple([whole, whole] + state),
        check_vma=False,
    )
```
